512 devices in a mesh: ctx: 32 (over y_hi, z), tp: 16 (over x, y_lo, core).
Axes of the slice: x: 4, y: 4 (y_hi: 2, y_lo: 2; y = y_hi * 2 + y_lo), z: 16, core: 2. Of those that a mesh axis runs over, the one named last changes fastest.
Arguments:
- queries: bfloat16 [16384, 2048], P('ctx', 'tp'), may hold values from -6 to 6
- keys: bfloat16 [16384, 2048], P('ctx', 'tp'), may hold values from -6 to 6
- values: bfloat16 [16384, 2048], P('ctx', 'tp'), may hold values from -6 to 6
- residual: bfloat16 [16384, 2048], P('ctx', 'tp'), may hold values from -3 to 3
- out_proj: bfloat16 [2048, 2048], P('tp'), may hold values from -0.5 to 0.5
- norm_gain: float32 [2048], replicated, may hold values from 0.1 to 1.9
- in_proj: bfloat16 [2048, 3, 2048], P(None, None, 'tp'), may hold values from -0.125 to 0.125
- feat_taps: float32 [3, 3, 2048], P(None, None, 'tp'), may hold values from -3 to 3
- long_filter: float32 [7, 128], P(None, 'tp'), may hold values from -2 to 2
Outputs:
- hidden: bfloat16 [16384, 2048], P('ctx', 'tp')
- gated: bfloat16 [16384, 2048], P('ctx', 'tp')
The draws below stay inside these ranges and needn't reach their ends.
All inputs are finite; a program needn't handle non-finite values.
Results may differ from the reference program's by a relative error of at most 0.04.
Values may be sent and summed in bfloat16 or wider, within the bound.
A program may use at most 64 MiB of HBM per device.

```python
import jax
import jax.numpy as jnp
from jax import lax

HEADS = 16
HEAD_DIM = 128
WIDTH = 2048
GROUP = 16
FEAT_TAPS = 3
FILTER_TAPS = 7
TOK_DEV = 512
TOKENS = 16384
N_CTX = 32
N_TP = 16


def draw_queries(key, part):
    key = jax.random.fold_in(key, 11)
    return jnp.clip(jax.random.normal(key, (TOKENS, HEADS * HEAD_DIM), jnp.float32), -6.0, 6.0).astype(jnp.bfloat16)


def draw_keys(key, part):
    key = jax.random.fold_in(key, 23)
    return jnp.clip(2.5 * jax.random.normal(key, (TOKENS, HEADS * HEAD_DIM), jnp.float32), -6.0, 6.0).astype(jnp.bfloat16)


def level_of(key, extent, shards, smallest, top_value):
    loudness = 1.0
    for axis_at, blocks in shards:
        heights = jax.random.uniform(jax.random.fold_in(jax.random.fold_in(key, 6), axis_at), (blocks,), jnp.float32, smallest / len(shards), top_value / len(shards))
        loudness = loudness * jnp.repeat(jnp.exp(heights), extent[axis_at] // blocks).reshape((-1,) + (1,) * (len(extent) - 1 - axis_at))
    return loudness


def normal_values(key, shape, deviation, limit, split=(), kind=jnp.bfloat16):
    gain = level_of(key, shape, split, -0.22, 0.18) if split else 1.0
    array = jax.random.normal(key, shape, jnp.float32) * deviation * gain
    return jnp.minimum(jnp.maximum(array, -limit), limit).astype(kind)


def setup_inputs(seed: int = 0) -> dict:
    splits = jax.random.split(jax.random.key(seed), 10)
    return {
        "queries": draw_queries(jax.random.fold_in(splits[9], 71), 0),
        "keys": draw_keys(jax.random.fold_in(splits[9], 71), 0),
        "values": normal_values(splits[2], (TOKENS, HEADS * HEAD_DIM), 1.0, 6.0, ((0, 32), (1, 16))),
        "residual": normal_values(splits[3], (TOKENS, WIDTH), 0.5, 3.0, ((0, 32), (1, 16))),
        "out_proj": normal_values(splits[4], (HEADS * HEAD_DIM, WIDTH), HEAD_DIM ** -0.5, 0.5, ((0, 16),)),
        "norm_gain": jnp.clip(1.0 + 0.18 * jax.random.normal(splits[5], (WIDTH,), jnp.float32), 0.1, 1.9),
        "in_proj": normal_values(splits[6], (WIDTH, 3, WIDTH), WIDTH ** -0.5, 0.125, ((2, 16),)),
        "feat_taps": normal_values(splits[7], (FEAT_TAPS, 3, WIDTH), 0.6, 3.0, ((2, 16),), jnp.float32),
        "long_filter": normal_values(splits[8], (FILTER_TAPS, WIDTH // GROUP), 0.4, 2.0, ((1, 16),), jnp.float32),
    }


def mirror_place(rows_total):
    half_rows = TOK_DEV // 2
    rows_index = jnp.arange(rows_total, dtype=jnp.int32)
    device = rows_index // TOK_DEV
    within = rows_index % TOK_DEV
    block_idx = jnp.where(within < half_rows, device, 2 * N_CTX - 1 - device)
    return block_idx * half_rows + within % half_rows

def reference(queries, keys, values, residual, out_proj, norm_gain, in_proj, feat_taps, long_filter):
    places = mirror_place(TOKENS)
    natural = jnp.zeros((TOKENS,), jnp.int32).at[places].set(jnp.arange(TOKENS, dtype=jnp.int32))
    query_nat = queries[natural].astype(jnp.float32).reshape(TOKENS, HEADS, HEAD_DIM)
    key_nat = keys[natural].astype(jnp.float32).reshape(TOKENS, HEADS, HEAD_DIM)
    value_nat = values[natural].astype(jnp.float32).reshape(TOKENS, HEADS, HEAD_DIM)
    scale_factor = HEAD_DIM ** (-0.5)
    pieces_out = []
    for block_idx in range(TOKENS // TOK_DEV):
        lower = block_idx * TOK_DEV
        upper = lower + TOK_DEV
        scores = jnp.einsum('qhd,khd->hqk', query_nat[lower:upper], key_nat[:upper]) * scale_factor
        visible = (jnp.arange(upper, dtype=jnp.int32)[None, :] <= (lower + jnp.arange(TOK_DEV, dtype=jnp.int32))[:, None])[None]
        scores = jnp.where(visible, scores, -1e+30)
        largest = lax.optimization_barrier(jnp.max(scores, axis=-1, keepdims=True))
        weights = jnp.where(visible, jnp.exp(scores - largest), 0.0)
        totals = lax.optimization_barrier(jnp.sum(weights, axis=-1, keepdims=True))
        rounded = lax.optimization_barrier(weights.astype(jnp.bfloat16)).astype(jnp.float32)
        mixed_out = jnp.einsum('hqk,khd->hqd', rounded, value_nat[:upper]) / totals
        pieces_out.append(jnp.transpose(mixed_out, (1, 0, 2)).reshape(TOK_DEV, HEADS * HEAD_DIM))
    attended = jnp.concatenate(pieces_out, 0).astype(jnp.bfloat16)
    group_cols = HEADS // N_TP * HEAD_DIM

    def add_group(running, group_idx):
        start_col = group_idx * group_cols
        part_sum = jnp.dot(lax.dynamic_slice_in_dim(attended, start_col, group_cols, 1), lax.dynamic_slice_in_dim(out_proj, start_col, group_cols, 0), preferred_element_type=jnp.float32)
        return (running + lax.optimization_barrier(part_sum.astype(jnp.bfloat16)).astype(jnp.float32), None)
    summed, _ = lax.scan(add_group, jnp.zeros((TOKENS, WIDTH), jnp.float32), jnp.arange(N_TP, dtype=jnp.int32))
    hidden = (residual[natural].astype(jnp.float32) + summed).astype(jnp.bfloat16)
    widened = hidden.astype(jnp.float32)
    mean_square = lax.optimization_barrier(jnp.mean(widened * widened, axis=-1, keepdims=True))
    normed = (widened * lax.rsqrt(mean_square + 1e-06) * norm_gain.astype(jnp.float32)).astype(jnp.bfloat16)
    streams = jnp.dot(normed, in_proj.reshape(WIDTH, 3 * WIDTH), preferred_element_type=jnp.float32).astype(jnp.bfloat16)
    padded = jnp.pad(streams.astype(jnp.float32).reshape(TOKENS, 3, WIDTH), ((FEAT_TAPS - 1, 0), (0, 0), (0, 0)))
    featured = jnp.zeros((TOKENS, 3, WIDTH), jnp.float32)
    for tap_index in range(FEAT_TAPS):
        offset = FEAT_TAPS - 1 - tap_index
        featured = featured + feat_taps[tap_index].astype(jnp.float32)[None] * padded[offset:offset + TOKENS]
    mixture = featured[:, 0] * featured[:, 2]
    mixture_pad = jnp.pad(mixture, ((FILTER_TAPS - 1, 0), (0, 0)))
    filter_rows = jnp.repeat(long_filter.astype(jnp.float32), GROUP, axis=1)
    response = jnp.zeros((TOKENS, WIDTH), jnp.float32)
    for tap_index in range(FILTER_TAPS):
        offset = FILTER_TAPS - 1 - tap_index
        response = response + filter_rows[tap_index][None] * mixture_pad[offset:offset + TOKENS]
    gated_out = (featured[:, 1] * response).astype(jnp.bfloat16)
    return (hidden[places], gated_out[places])
```

```python
import functools

import jax
import jax.numpy as jnp
from jax import lax
from jax.experimental import pallas as pl
from jax.experimental.pallas import tpu as pltpu
from jax.sharding import PartitionSpec as P

MESH = pl.DeviceIdType.MESH
LANES = 128
GROUP = 16
FEAT_TAPS = 3
FILTER_TAPS = 7
RIM = 8
LOW = -1e30
LOG2E = 1.4426950408889634
F32 = jnp.float32
BF16 = jnp.bfloat16


def kernel(
    ring,
    q_ref,
    k_ref,
    v_ref,
    res_ref,
    outp_ref,
    gain_ref,
    inp_ref,
    taps_ref,
    filt_ref,
    hid_ref,
    gated_ref,
    kbuf,
    vbuf,
    qpar,
    acc_own,
    acc_par,
    max_own,
    max_par,
    o_send,
    o_recv,
    st_send,
    st_recv,
    wout,
    win,
    att_all,
    hid_all,
    hid_acc,
    str_acc,
    sq_acc,
    str_ref,
    halo,
    ext,
    mix,
    in_sem,
    ks_sem,
    kr_sem,
    vs_sem,
    vr_sem,
    x_send,
    x_recv,
    w_send,
    w_recv,
    g_send,
    g_recv,
):
    rows, width = q_ref.shape
    half = rows // 2
    top = ring // 2
    n_ctx = 2 * ring
    n_tp = wout.shape[0]
    n_x = n_tp // 4
    dev = lax.axis_index("ctx")
    y_hi = dev // ring
    z = lax.rem(dev, ring)
    tp = lax.axis_index("tp")
    x = tp // 4
    y_lo = lax.rem(tp, 4) // 2
    core = lax.rem(tp, 2)
    scale = LOG2E * width**-0.5

    def ctx_id(y_at, z_at):
        return {"ctx": y_at * ring + z_at}

    right = ctx_id(y_hi, lax.rem(z + 1, ring))
    left = ctx_id(y_hi, lax.rem(z + ring - 1, ring))
    across = ctx_id(1 - y_hi, z)
    after = {"ctx": lax.rem(dev + 1, n_ctx)}
    before = {"ctx": lax.rem(dev + n_ctx - 1, n_ctx)}

    def tp_at(dx, dy, dc):
        return (
            lax.rem(x + dx + n_x, n_x) * 4
            + (1 - y_lo if dy else y_lo) * 2
            + (1 - core if dc else core)
        )

    barrier = pltpu.get_barrier_semaphore()
    for other in (right, left, across, after, before):
        pl.semaphore_signal(barrier, inc=1, device_id=other, device_id_type=MESH)

    def greet(step, carry):
        peer = lax.rem(tp + step, n_tp)
        pl.semaphore_signal(barrier, inc=1, device_id={"tp": peer}, device_id_type=MESH)
        return carry

    lax.fori_loop(1, n_tp, greet, 0)

    loads = [
        pltpu.make_async_copy(
            inp_ref.at[s], win.at[:, s * LANES : (s + 1) * LANES], in_sem.at[s]
        )
        for s in range(3)
    ]
    for load in loads:
        load.start()
    pl.semaphore_wait(barrier, n_tp - 1 + 5)

    def remote(src, dst, send, recv, to):
        return pltpu.make_async_remote_copy(
            src_ref=src, dst_ref=dst, send_sem=send, recv_sem=recv, device_id=to, device_id_type=MESH
        )

    def key_copy(src, slot, to):
        return remote(src, kbuf.at[slot], ks_sem.at[slot], kr_sem.at[slot], to)

    def value_copy(src, slot, to):
        return remote(src, vbuf.at[slot], vs_sem.at[slot], vr_sem.at[slot], to)

    key_copy(k_ref, 1, right).start()
    key_copy(k_ref, ring - 1, left).start()
    q_copy = remote(q_ref, qpar, x_send.at[0], x_recv.at[0], across)
    q_copy.start()
    value_copy(v_ref, 1, right).start()
    value_copy(v_ref, ring - 1, left).start()

    def out_copy(step):
        peer = lax.rem(tp + step, n_tp)
        cols = pl.ds(pl.multiple_of(peer * LANES, LANES), LANES)
        return remote(
            outp_ref.at[:, cols], wout.at[tp], w_send.at[step], w_recv.at[step], {"tp": peer}
        )

    def out_start(step, carry):
        out_copy(step).start()
        return carry

    lax.fori_loop(1, n_tp, out_start, 0)
    wout[tp] = outp_ref[:, pl.ds(pl.multiple_of(tp * LANES, LANES), LANES)]

    for acc, top_ref in ((acc_own, max_own), (acc_par, max_par)):
        acc[...] = jnp.zeros_like(acc)
        top_ref[...] = jnp.full(top_ref.shape, LOW, F32)

    ones = jnp.ones((half, LANES), BF16)
    tri = lax.broadcasted_iota(jnp.int32, (half, half), 0) >= lax.broadcasted_iota(
        jnp.int32, (half, half), 1
    )

    def unit(queries, acc, top_ref, offset, keys, values, masked=False):
        at = pl.ds(offset, half)
        scores = lax.dot_general(
            queries[at, :], keys, (((1,), (1,)), ((), ())), preferred_element_type=F32
        )
        if masked:
            scores = jnp.where(tri, scores, LOW)
        old = top_ref[at, :]
        new = jnp.maximum(old, jnp.max(scores, axis=1, keepdims=True))
        top_ref[at, :] = new
        wide = jnp.concatenate([new] * (half // LANES), axis=1)
        weights = jnp.exp2((scores - wide) * scale).astype(BF16)
        factor = jnp.exp2((old - new) * scale)
        acc[at, :] = acc[at, :] * jnp.concatenate([factor, factor], axis=1) + jnp.dot(
            weights, jnp.concatenate([values, ones], axis=1), preferred_element_type=F32
        )

    row_c = pl.multiple_of(y_hi * half, half)

    def partner_units(keys, values):
        unit(qpar, acc_par, max_par, half, keys[:half, :], values[:half, :])
        at = pl.ds(row_c, half)
        unit(qpar, acc_par, max_par, row_c, keys[at, :], values[at, :])

    def own_units(keys, values, slot):
        unit(q_ref, acc_own, max_own, half, keys[:half, :], values[:half, :])
        row_d = pl.multiple_of(jnp.where(slot <= z, 0, half), half)
        at = pl.ds(row_d, half)
        unit(q_ref, acc_own, max_own, row_d, keys[at, :], values[at, :])

    unit(q_ref, acc_own, max_own, 0, k_ref[:half, :], v_ref[:half, :], True)
    unit(q_ref, acc_own, max_own, half, k_ref[half:, :], v_ref[half:, :], True)
    unit(q_ref, acc_own, max_own, half, k_ref[:half, :], v_ref[:half, :])
    q_copy.wait_recv()
    partner_units(k_ref, v_ref)

    def turn(step, carry):
        back = ring - step
        key_copy(k_ref, step, right).wait_recv()
        key_copy(kbuf.at[step], step + 1, right).start()
        key_copy(k_ref, back, left).wait_recv()

        @pl.when(step < top - 1)
        def _():
            key_copy(kbuf.at[back], back - 1, left).start()

        value_copy(v_ref, step, right).wait_recv()

        @pl.when(step < top - 1)
        def _():
            value_copy(vbuf.at[step], step + 1, right).start()

        value_copy(v_ref, back, left).wait_recv()
        value_copy(vbuf.at[back], back - 1, left).start()
        for slot in (step, back):
            partner_units(kbuf.at[slot], vbuf.at[slot])
            own_units(kbuf.at[slot], vbuf.at[slot], slot)
        return carry

    lax.fori_loop(1, top, turn, 0)
    key_copy(k_ref, top, right).wait_recv()
    value_copy(v_ref, top, left).wait_recv()
    partner_units(kbuf.at[top], vbuf.at[top])

    def settle(acc, top_ref):
        total = acc[:, LANES:]
        seen = total > 0.0
        inverse = 1.0 / jnp.where(seen, total, 1.0)
        level = jnp.where(seen, top_ref[...] * scale + jnp.log2(jnp.where(seen, total, 1.0)), LOW)
        return acc[:, :LANES] * inverse, level

    diagonal = lax.broadcasted_iota(jnp.int32, (LANES, LANES), 0) == lax.broadcasted_iota(
        jnp.int32, (LANES, LANES), 1
    )
    mean_par, level_par = settle(acc_par, max_par)
    o_send[...] = mean_par.astype(BF16)
    st_send[...] = jnp.zeros_like(st_send)
    for g in range(rows // LANES):
        block = level_par[g * LANES : (g + 1) * LANES, :]
        st_send[g : g + 1, :] = jnp.sum(jnp.where(diagonal, block, 0.0), axis=0, keepdims=True)
    o_copy = remote(o_send, o_recv, x_send.at[1], x_recv.at[1], across)
    st_copy = remote(st_send, st_recv, x_send.at[2], x_recv.at[2], across)
    st_copy.start()
    o_copy.start()
    own_units(kbuf.at[top], vbuf.at[top], top)
    mean_own, level_own = settle(acc_own, max_own)
    for load in loads:
        load.wait()
    st_copy.wait_recv()
    o_copy.wait_recv()
    for g in range(rows // LANES):
        at = slice(g * LANES, (g + 1) * LANES)
        line = jnp.broadcast_to(st_recv[g : g + 1, :], (LANES, LANES))
        level_other = jnp.sum(jnp.where(diagonal, line, 0.0), axis=1, keepdims=True)
        here = level_own[at, :]
        most = jnp.maximum(here, level_other)
        w_own = jnp.exp2(here - most)
        w_other = jnp.exp2(level_other - most)
        joined = (w_own * mean_own[at, :] + w_other * o_recv[at, :].astype(F32)) / (w_own + w_other)
        att_all[tp, at, :] = joined.astype(BF16)

    mid = rows // 2
    whole, head, tail = pl.ds(0, rows), pl.ds(0, mid), pl.ds(mid, mid)
    MOVES = [
        ((0, 0), whole, "y"),
        ((0, 0), whole, "xp"),
        ((0, 0), whole, "xm"),
        ((0, 0), whole, "c"),
        ((0, 1), whole, "xp"),
        ((0, 1), whole, "xm"),
        ((0, 1), whole, "c"),
        ((-1, 0), head, "xp"),
        ((-1, 0), whole, "c"),
        ((1, 0), tail, "xm"),
        ((1, 0), whole, "c"),
        ((-1, 1), head, "xp"),
        ((-1, 1), whole, "c"),
        ((1, 1), tail, "xm"),
        ((1, 1), whole, "c"),
        ((2, 0), whole, "c"),
        ((2, 1), whole, "c"),
    ]
    targets = {
        "y": {"tp": tp_at(0, 1, 0)},
        "xp": {"tp": tp_at(1, 0, 0)},
        "xm": {"tp": tp_at(-1, 0, 0)},
        "c": {"tp": tp_at(0, 0, 1)},
    }

    def gather(which, buf, consume):
        def move(n):
            (dx, dy), part, to = MOVES[n]
            chunk = tp_at(dx, dy, 0)
            ref = buf.at[chunk, part, :]
            return remote(ref, ref, g_send.at[which, n], g_recv.at[which, n], targets[to])

        def arrive(n):
            (dx, dy), part, to = MOVES[n]
            sx = dx + {"xp": -1, "xm": 1}.get(to, 0)
            sy = 1 - dy if to == "y" else dy
            chunk = tp_at(sx, sy, 1 if to == "c" else 0)
            ref = buf.at[chunk, part, :]
            remote(ref, ref, g_send.at[which, n], g_recv.at[which, n], targets[to]).wait_recv()

        def go(*moves):
            for n in moves:
                move(n).start()

        def pair(dx, dy):
            consume(tp_at(dx, dy, 0) // 2)

        go(0, 1, 2, 3)
        arrive(3)
        pair(0, 0)
        arrive(0)
        go(4, 5, 6)
        arrive(1)
        go(7, 8)
        arrive(2)
        go(9, 10)
        arrive(6)
        pair(0, 1)
        arrive(4)
        go(11, 12)
        arrive(5)
        go(13, 14)
        arrive(8)
        pair(-1, 0)
        arrive(10)
        pair(1, 0)
        arrive(7)
        arrive(9)
        go(15)
        arrive(12)
        pair(-1, 1)
        arrive(14)
        pair(1, 1)
        arrive(11)
        arrive(13)
        go(16)
        arrive(15)
        pair(2, 0)
        arrive(16)
        pair(2, 1)
        return [move(n) for n in range(len(MOVES))]

    def out_arrive(step, carry):
        out_copy(step).wait_recv()
        return carry

    lax.fori_loop(1, n_tp, out_arrive, 0)
    hid_acc[...] = res_ref[...].astype(F32)

    def project_out(chip):
        left_side = jnp.concatenate([att_all[2 * chip], att_all[2 * chip + 1]], axis=1)
        weight = jnp.concatenate([wout[2 * chip], wout[2 * chip + 1]], axis=0)
        hid_acc[...] += jnp.dot(left_side, weight, preferred_element_type=F32)

    moves = gather(0, att_all, project_out)
    hidden = hid_acc[...].astype(BF16)
    hid_all[tp] = hidden
    hid_ref[...] = hidden
    str_acc[...] = jnp.zeros_like(str_acc)
    sq_acc[...] = jnp.zeros_like(sq_acc)

    def project_in(chip):
        sides = []
        for c in range(2):
            wide = hid_all[2 * chip + c].astype(F32)
            sq_acc[...] += wide * wide
            sides.append((wide * gain_ref[pl.ds(2 * chip + c, 1), :]).astype(BF16))
        at = pl.ds(pl.multiple_of(chip * 2 * LANES, 2 * LANES), 2 * LANES)
        str_acc[...] += jnp.dot(
            jnp.concatenate(sides, axis=1), win[at, :], preferred_element_type=F32
        )

    moves += gather(1, hid_all, project_in)
    mean_square = jnp.sum(sq_acc[...], axis=1, keepdims=True) / (n_tp * LANES)
    streams = (str_acc[...] * lax.rsqrt(mean_square + 1e-6)).astype(BF16)
    str_ref[...] = streams
    edge = 2 * RIM
    rim_copies = [
        remote(str_ref.at[half - edge : half, :], halo.at[0], x_send.at[3], x_recv.at[3], after),
        remote(str_ref.at[rows - edge : rows, :], halo.at[1], x_send.at[4], x_recv.at[4], before),
    ]
    for copy in rim_copies:
        copy.start()
    spread = streams.astype(F32)
    ext[0, RIM:, :] = spread[:half]
    ext[1, RIM:, :] = spread[half:]
    lane_group = lax.broadcasted_iota(jnp.int32, (FILTER_TAPS, LANES), 1) // GROUP
    filt = jnp.zeros((FILTER_TAPS, LANES), F32)
    for g in range(LANES // GROUP):
        filt = jnp.where(lane_group == g, filt_ref[:, g : g + 1], filt)
    for copy in rim_copies:
        copy.wait_recv()
    first_tail = str_ref[half - edge : half, :].astype(F32)[RIM:]
    ext[0, :RIM, :] = jnp.where(dev == 0, 0.0, halo[0].astype(F32)[RIM:])
    ext[1, :RIM, :] = jnp.where(dev == n_ctx - 1, first_tail, halo[1].astype(F32)[RIM:])
    span = half + FILTER_TAPS - 1
    for side in range(2):

        def featured(stream, start, count, side=side):
            cols = slice(stream * LANES, (stream + 1) * LANES)
            total = None
            for j in range(FEAT_TAPS):
                low = start + FEAT_TAPS - 1 - j
                term = taps_ref[j, stream : stream + 1, :] * ext[side, low : low + count, cols]
                total = term if total is None else total + term
            return total

        mix[0:span, :] = featured(0, 0, span) * featured(2, 0, span)
        response = None
        for j in range(FILTER_TAPS):
            low = FILTER_TAPS - 1 - j
            term = filt[j : j + 1, :] * mix[low : low + half, :]
            response = term if response is None else response + term
        out = featured(1, FILTER_TAPS - 1, half) * response
        gated_ref[side * half : (side + 1) * half, :] = out.astype(BF16)

    def drain(slot, carry):
        key_copy(k_ref, slot, right).wait_send()
        value_copy(v_ref, slot, right).wait_send()
        return carry

    lax.fori_loop(1, ring, drain, 0)

    def out_drain(step, carry):
        out_copy(step).wait_send()
        return carry

    lax.fori_loop(1, n_tp, out_drain, 0)
    for copy in [q_copy, st_copy, o_copy] + rim_copies + moves:
        copy.wait_send()


def local(queries, keys, values, residual, out_proj, norm_gain, in_proj, feat_taps, long_filter):
    rows, width = queries.shape
    half = rows // 2
    n_tp = lax.axis_size("tp")
    ring = lax.axis_size("ctx") // 2
    vmem = pl.BlockSpec(memory_space=pltpu.VMEM)
    anywhere = pl.BlockSpec(memory_space=pl.ANY)
    dma = pltpu.SemaphoreType.DMA
    shape = jax.ShapeDtypeStruct((rows, width), BF16)
    return pl.pallas_call(
        functools.partial(kernel, ring),
        out_shape=(shape, shape),
        in_specs=[vmem] * 6 + [anywhere] + [vmem] * 2,
        out_specs=(vmem, vmem),
        scratch_shapes=[
            pltpu.VMEM((ring, rows, width), BF16),
            pltpu.VMEM((ring, rows, width), BF16),
            pltpu.VMEM((rows, width), BF16),
            pltpu.VMEM((rows, 2 * width), F32),
            pltpu.VMEM((rows, 2 * width), F32),
            pltpu.VMEM((rows, width), F32),
            pltpu.VMEM((rows, width), F32),
            pltpu.VMEM((rows, width), BF16),
            pltpu.VMEM((rows, width), BF16),
            pltpu.VMEM((8, LANES), F32),
            pltpu.VMEM((8, LANES), F32),
            pltpu.VMEM((n_tp, LANES, LANES), BF16),
            pltpu.VMEM((n_tp * LANES, 3 * LANES), BF16),
            pltpu.VMEM((n_tp, rows, width), BF16),
            pltpu.VMEM((n_tp, rows, width), BF16),
            pltpu.VMEM((rows, LANES), F32),
            pltpu.VMEM((rows, 3 * LANES), F32),
            pltpu.VMEM((rows, LANES), F32),
            pltpu.VMEM((rows, 3 * LANES), BF16),
            pltpu.VMEM((2, 2 * RIM, 3 * LANES), BF16),
            pltpu.VMEM((2, RIM + half, 3 * LANES), F32),
            pltpu.VMEM((RIM + half, LANES), F32),
            dma((3,)),
            dma((ring,)),
            dma((ring,)),
            dma((ring,)),
            dma((ring,)),
            dma((5,)),
            dma((5,)),
            dma((n_tp,)),
            dma((n_tp,)),
            dma((2, 17)),
            dma((2, 17)),
        ],
        compiler_params=pltpu.CompilerParams(
            collective_id=0, has_side_effects=True, vmem_limit_bytes=48 * 1024 * 1024
        ),
        cost_estimate=pl.CostEstimate(
            flops=4 * 10**9, bytes_accessed=4 * 10**6, transcendentals=5 * 10**6
        ),
    )(
        queries,
        keys,
        values,
        residual,
        out_proj,
        norm_gain.reshape(n_tp, LANES),
        jnp.transpose(in_proj, (1, 0, 2)),
        feat_taps,
        long_filter,
    )


def solution(mesh):
    return jax.shard_map(
        local,
        mesh=mesh,
        in_specs=(
            P("ctx", "tp"),
            P("ctx", "tp"),
            P("ctx", "tp"),
            P("ctx", "tp"),
            P("tp", None),
            P(),
            P(None, None, "tp"),
            P(None, None, "tp"),
            P(None, "tp"),
        ),
        out_specs=(P("ctx", "tp"), P("ctx", "tp")),
        check_vma=False,
    )
```

```python
import functools

import jax
import jax.numpy as jnp
from jax import lax
from jax.experimental import pallas as pl
from jax.experimental.pallas import tpu as pltpu
from jax.sharding import PartitionSpec as P

MESH = pl.DeviceIdType.MESH
LANES = 128
GROUP = 16
FEAT_TAPS = 3
FILTER_TAPS = 7
RIM = 8
LOW = -1e30
LOG2E = 1.4426950408889634
F32 = jnp.float32
BF16 = jnp.bfloat16


def kernel(
    ring,
    q_hbm,
    k_hbm,
    v_hbm,
    res_hbm,
    outp_hbm,
    gain_hbm,
    inp_hbm,
    taps_hbm,
    filt_hbm,
    hid_ref,
    gated_ref,
    q_ref,
    k_ref,
    v_ref,
    res_ref,
    gain_ref,
    taps_ref,
    filt_ref,
    kbuf,
    vbuf,
    qpar,
    acc_own,
    acc_par,
    max_own,
    max_par,
    o_send,
    o_recv,
    st_send,
    st_recv,
    wout,
    win,
    att_all,
    hid_all,
    hid_acc,
    str_acc,
    sq_acc,
    str_ref,
    halo,
    ext,
    mix,
    in_sem,
    ks_sem,
    kr_sem,
    vs_sem,
    vr_sem,
    x_send,
    x_recv,
    w_send,
    w_recv,
    g_send,
    g_recv,
):
    rows, width = q_ref.shape
    half = rows // 2
    quarter = half // 2
    top = ring // 2
    n_ctx = 2 * ring
    n_tp = wout.shape[0]
    n_x = n_tp // 4
    dev = lax.axis_index("ctx")
    y_hi = dev // ring
    z = lax.rem(dev, ring)
    tp = lax.axis_index("tp")
    x = tp // 4
    y_lo = lax.rem(tp, 4) // 2
    core = lax.rem(tp, 2)
    scale = LOG2E * width**-0.5

    def ctx_id(y_at, z_at):
        return {"ctx": y_at * ring + z_at}

    right = ctx_id(y_hi, lax.rem(z + 1, ring))
    left = ctx_id(y_hi, lax.rem(z + ring - 1, ring))
    across = ctx_id(1 - y_hi, z)
    after = {"ctx": lax.rem(dev + 1, n_ctx)}
    before = {"ctx": lax.rem(dev + n_ctx - 1, n_ctx)}

    def tp_at(dx, dy, dc):
        return (
            lax.rem(x + dx + n_x, n_x) * 4
            + (1 - y_lo if dy else y_lo) * 2
            + (1 - core if dc else core)
        )

    barrier = pltpu.get_barrier_semaphore()
    for other in (right, left, across, after, before):
        pl.semaphore_signal(barrier, inc=1, device_id=other, device_id_type=MESH)

    def greet(step, carry):
        peer = lax.rem(tp + step, n_tp)
        pl.semaphore_signal(barrier, inc=1, device_id={"tp": peer}, device_id_type=MESH)
        return carry

    lax.fori_loop(1, n_tp, greet, 0)

    own_cols = pl.ds(pl.multiple_of(tp * LANES, LANES), LANES)
    loads = []
    for src, dst in [
        (q_hbm, q_ref),
        (k_hbm, k_ref),
        (v_hbm, v_ref),
        (res_hbm, res_ref),
        (gain_hbm, gain_ref),
        (taps_hbm, taps_ref),
        (filt_hbm, filt_ref),
        (outp_hbm.at[:, own_cols], wout.at[tp]),
    ] + [(inp_hbm.at[s], win.at[:, s * LANES : (s + 1) * LANES]) for s in range(3)]:
        load = pltpu.make_async_copy(src, dst, in_sem.at[len(loads)])
        load.start()
        loads.append(load)

    for acc, top_ref in ((acc_own, max_own), (acc_par, max_par)):
        acc[...] = jnp.zeros_like(acc)
        top_ref[...] = jnp.full(top_ref.shape, LOW, F32)
    pl.semaphore_wait(barrier, n_tp - 1 + 5)

    def remote(src, dst, send, recv, to):
        return pltpu.make_async_remote_copy(
            src_ref=src, dst_ref=dst, send_sem=send, recv_sem=recv, device_id=to, device_id_type=MESH
        )

    def key_copy(src, slot, to):
        return remote(src, kbuf.at[slot], ks_sem.at[slot], kr_sem.at[slot], to)

    def value_copy(src, slot, to):
        return remote(src, vbuf.at[slot], vs_sem.at[slot], vr_sem.at[slot], to)

    key_copy(k_hbm, 1, right).start()
    key_copy(k_hbm, ring - 1, left).start()
    q_copy = remote(q_hbm, qpar, x_send.at[0], x_recv.at[0], across)
    q_copy.start()
    value_copy(v_hbm, 1, right).start()
    value_copy(v_hbm, ring - 1, left).start()

    def out_copy(step):
        peer = lax.rem(tp + step, n_tp)
        cols = pl.ds(pl.multiple_of(peer * LANES, LANES), LANES)
        return remote(
            outp_hbm.at[:, cols], wout.at[tp], w_send.at[step], w_recv.at[step], {"tp": peer}
        )

    def out_start(step, carry):
        out_copy(step).start()
        return carry

    ones = jnp.ones((half, LANES), BF16)
    tri = lax.broadcasted_iota(jnp.int32, (half, half), 0) >= lax.broadcasted_iota(
        jnp.int32, (half, half), 1
    )

    def unit(queries, acc, top_ref, offset, blocks, masked=False):
        at = pl.ds(offset, half)
        rows_q = queries[at, :]
        scores = [
            lax.dot_general(rows_q, keys, (((1,), (1,)), ((), ())), preferred_element_type=F32)
            for keys, _ in blocks
        ]
        if masked:
            scores = [jnp.where(tri, block, LOW) for block in scores]
        old = top_ref[at, :]
        best = functools.reduce(jnp.maximum, scores)
        new = jnp.maximum(old, jnp.max(best, axis=1, keepdims=True))
        top_ref[at, :] = new
        wide = jnp.concatenate([new] * (half // LANES), axis=1)
        factor = jnp.exp2((old - new) * scale)
        total = acc[at, :] * jnp.concatenate([factor, factor], axis=1)
        for block, (_, values) in zip(scores, blocks):
            weights = jnp.exp2((block - wide) * scale).astype(BF16)
            total = total + jnp.dot(
                weights, jnp.concatenate([values, ones], axis=1), preferred_element_type=F32
            )
        acc[at, :] = total

    row_c = pl.multiple_of(y_hi * half, half)

    def first_units(pairs):
        blocks = [(keys[:half, :], values[:half, :]) for keys, values in pairs]
        unit(qpar, acc_par, max_par, half, blocks)
        return blocks

    def third_unit(pairs):
        at = pl.ds(row_c, half)
        unit(qpar, acc_par, max_par, row_c, [(keys[at, :], values[at, :]) for keys, values in pairs])

    def last_unit(keys, values, slot):
        row_d = pl.multiple_of(jnp.where(slot <= z, 0, half), half)
        at = pl.ds(row_d, half)
        unit(q_ref, acc_own, max_own, row_d, [(keys[at, :], values[at, :])])

    def early(slots):
        pairs = [(kbuf.at[slot], vbuf.at[slot]) for slot in slots]
        blocks = first_units(pairs)
        unit(q_ref, acc_own, max_own, half, blocks)

    def late(slots):
        third_unit([(kbuf.at[slot], vbuf.at[slot]) for slot in slots])
        for slot in slots:
            last_unit(kbuf.at[slot], vbuf.at[slot], slot)

    for load in loads[:3]:
        load.wait()
    unit(q_ref, acc_own, max_own, 0, [(k_ref[:half, :], v_ref[:half, :])], True)
    unit(q_ref, acc_own, max_own, half, [(k_ref[half:, :], v_ref[half:, :])], True)
    unit(q_ref, acc_own, max_own, half, [(k_ref[:half, :], v_ref[:half, :])])

    def turn(step, carry):
        back = ring - step
        key_copy(k_ref, step, right).wait_recv()
        key_copy(kbuf.at[step], step + 1, right).start()
        key_copy(k_ref, back, left).wait_recv()

        @pl.when(step < top - 1)
        def _():
            key_copy(kbuf.at[back], back - 1, left).start()

        @pl.when(step > 1)
        def _():
            late((step - 1, back + 1))

        @pl.when(step == 1)
        def _():
            q_copy.wait_recv()
            lax.fori_loop(1, n_tp, out_start, 0)
            first_units([(k_ref, v_ref)])
            third_unit([(k_ref, v_ref)])

        value_copy(v_ref, step, right).wait_recv()

        @pl.when(step < top - 1)
        def _():
            value_copy(vbuf.at[step], step + 1, right).start()

        value_copy(v_ref, back, left).wait_recv()
        value_copy(vbuf.at[back], back - 1, left).start()
        early((step, back))
        return carry

    lax.fori_loop(1, top, turn, 0)
    late((top - 1, top + 1))
    key_copy(k_ref, top, right).wait_recv()
    value_copy(v_ref, top, left).wait_recv()
    far = [(kbuf.at[top], vbuf.at[top])]
    blocks = first_units(far)
    third_unit(far)

    def settle(acc, top_ref):
        total = acc[:, LANES:]
        seen = total > 0.0
        inverse = 1.0 / jnp.where(seen, total, 1.0)
        level = jnp.where(seen, top_ref[...] * scale + jnp.log2(jnp.where(seen, total, 1.0)), LOW)
        return acc[:, :LANES] * inverse, level

    diagonal = lax.broadcasted_iota(jnp.int32, (LANES, LANES), 0) == lax.broadcasted_iota(
        jnp.int32, (LANES, LANES), 1
    )
    mean_par, level_par = settle(acc_par, max_par)
    o_send[...] = mean_par.astype(BF16)
    st_send[...] = jnp.zeros_like(st_send)
    for g in range(rows // LANES):
        block = level_par[g * LANES : (g + 1) * LANES, :]
        st_send[g : g + 1, :] = jnp.sum(jnp.where(diagonal, block, 0.0), axis=0, keepdims=True)
    sides = (pl.ds(0, half), pl.ds(half, half))
    st_copy = remote(st_send, st_recv, x_send.at[1], x_recv.at[1], across)
    st_copy.start()
    o_copies = [
        remote(o_send.at[at, :], o_recv.at[at, :], x_send.at[2 + n], x_recv.at[2 + n], across)
        for n, at in enumerate(sides)
    ]
    for copy in o_copies:
        copy.start()
    unit(q_ref, acc_own, max_own, half, blocks)
    last_unit(kbuf.at[top], vbuf.at[top], top)
    mean_own, level_own = settle(acc_own, max_own)
    for load in loads[3:]:
        load.wait()

    def out_arrive(step, carry):
        out_copy(step).wait_recv()
        return carry

    lax.fori_loop(1, n_tp, out_arrive, 0)
    hid_acc[...] = res_ref[...].astype(F32)
    str_acc[...] = jnp.zeros_like(str_acc)
    sq_acc[...] = jnp.zeros_like(sq_acc)
    st_copy.wait_recv()

    def join(side):
        o_copies[side].wait_recv()
        for g in range(side * half // LANES, (side + 1) * half // LANES):
            at = slice(g * LANES, (g + 1) * LANES)
            line = jnp.broadcast_to(st_recv[g : g + 1, :], (LANES, LANES))
            level_other = jnp.sum(jnp.where(diagonal, line, 0.0), axis=1, keepdims=True)
            here = level_own[at, :]
            most = jnp.maximum(here, level_other)
            w_own = jnp.exp2(here - most)
            w_other = jnp.exp2(level_other - most)
            joined = (w_own * mean_own[at, :] + w_other * o_recv[at, :].astype(F32)) / (
                w_own + w_other
            )
            att_all[tp, at, :] = joined.astype(BF16)

    targets = {
        "y": {"tp": tp_at(0, 1, 0)},
        "xp": {"tp": tp_at(1, 0, 0)},
        "xm": {"tp": tp_at(-1, 0, 0)},
        "c": {"tp": tp_at(0, 0, 1)},
    }
    moves = []

    def gather(which, side, buf, consume):
        whole = sides[side]
        head = pl.ds(side * half, quarter)
        tail = pl.ds(side * half + quarter, quarter)
        known = {}

        def copy_of(dx, dy, dc, part, number, to):
            ref = buf.at[tp_at(dx, dy, dc), part, :]
            return remote(
                ref, ref, g_send.at[which, side, number], g_recv.at[which, side, number], targets[to]
            )

        def go(dx, dy, to, part=whole):
            number = len(known)
            known[dx, dy, to] = (number, part)
            copy = copy_of(dx, dy, 0, part, number, to)
            copy.start()
            moves.append(copy)

        def come(dx, dy, to):
            number, part = known[dx, dy, to]
            sx = dx + {"xp": -1, "xm": 1}.get(to, 0)
            sy = 1 - dy if to == "y" else dy
            copy_of(sx, sy, 1 if to == "c" else 0, part, number, to).wait_recv()

        def pair(dx, dy):
            come(dx, dy, "c")
            consume(tp_at(dx, dy, 0) // 2, whole)

        def relay(dx, dy):
            go(dx, dy, "xp" if dx < 0 else "xm", head if dx < 0 else tail)

        def y_first():
            for to in ("y", "xp", "xm", "c"):
                go(0, 0, to)
            yield
            come(0, 0, "y")
            for to in ("xp", "xm", "c"):
                go(0, 1, to)
            pair(0, 0)
            yield
            for dx, to in ((-1, "xp"), (1, "xm")):
                come(0, 0, to)
                relay(dx, 0)
                go(dx, 0, "c")
            yield
            pair(0, 1)
            for dx, to in ((-1, "xp"), (1, "xm")):
                come(0, 1, to)
                relay(dx, 1)
                go(dx, 1, "c")
            yield
            pair(-1, 0)
            pair(1, 0)
            yield
            come(-1, 0, "xp")
            come(1, 0, "xm")
            go(2, 0, "c")
            pair(-1, 1)
            pair(1, 1)
            yield
            come(-1, 1, "xp")
            come(1, 1, "xm")
            go(2, 1, "c")
            pair(2, 0)
            yield
            pair(2, 1)
            yield

        def x_first():
            for to in ("xp", "xm", "y", "c"):
                go(0, 0, to)
            yield
            pair(0, 0)
            for dx, to in ((-1, "xp"), (1, "xm")):
                come(0, 0, to)
                relay(dx, 0)
                go(dx, 0, "y")
                go(dx, 0, "c")
            yield
            come(0, 0, "y")
            go(0, 1, "c")
            pair(-1, 0)
            pair(1, 0)
            yield
            come(-1, 0, "xp")
            come(1, 0, "xm")
            go(2, 0, "y")
            go(2, 0, "c")
            come(-1, 0, "y")
            go(-1, 1, "c")
            come(1, 0, "y")
            go(1, 1, "c")
            yield
            pair(0, 1)
            pair(2, 0)
            yield
            come(2, 0, "y")
            go(2, 1, "c")
            pair(-1, 1)
            pair(1, 1)
            yield
            pair(2, 1)
            yield

        return x_first() if side else y_first()

    def project_out(chip, at):
        left_side = jnp.concatenate([att_all[2 * chip, at, :], att_all[2 * chip + 1, at, :]], axis=1)
        weight = jnp.concatenate([wout[2 * chip], wout[2 * chip + 1]], axis=0)
        hid_acc[at, :] += jnp.dot(left_side, weight, preferred_element_type=F32)

    def project_in(chip, at):
        parts = []
        for c in range(2):
            wide = hid_all[2 * chip + c, at, :].astype(F32)
            sq_acc[at, :] += wide * wide
            parts.append((wide * gain_ref[pl.ds(2 * chip + c, 1), :]).astype(BF16))
        deep = pl.ds(pl.multiple_of(chip * 2 * LANES, 2 * LANES), 2 * LANES)
        str_acc[at, :] += jnp.dot(
            jnp.concatenate(parts, axis=1), win[deep, :], preferred_element_type=F32
        )

    def finish_hidden(side):
        at = sides[side]
        hidden = hid_acc[at, :].astype(BF16)
        hid_all[tp, at, :] = hidden
        hid_ref[at, :] = hidden

    edge = 2 * RIM
    rim_copies = [
        remote(
            str_ref.at[(side + 1) * half - edge : (side + 1) * half, :],
            halo.at[side],
            x_send.at[4 + side],
            x_recv.at[4 + side],
            to,
        )
        for side, to in enumerate((after, before))
    ]

    def finish_streams(side):
        at = sides[side]
        mean_square = jnp.sum(sq_acc[at, :], axis=1, keepdims=True) / (n_tp * LANES)
        streams = (str_acc[at, :] * lax.rsqrt(mean_square + 1e-6)).astype(BF16)
        str_ref[at, :] = streams
        rim_copies[side].start()
        ext[side, RIM:, :] = streams.astype(F32)

    out_a, out_b = gather(0, 0, att_all, project_out), gather(0, 1, att_all, project_out)
    in_a, in_b = gather(1, 0, hid_all, project_in), gather(1, 1, hid_all, project_in)
    join(0)
    next(out_a)
    join(1)
    next(out_b)
    order = ["a", "a", "b", "b", "a", "a", "a", "b", "a", "b", "a"]
    for name in order:
        next(out_a if name == "a" else out_b)
    finish_hidden(0)
    next(in_a)
    next(out_b)
    next(out_b)
    finish_hidden(1)
    next(in_b)
    for name in order:
        next(in_a if name == "a" else in_b)
    finish_streams(0)
    next(in_b)
    next(in_b)
    finish_streams(1)

    lane_group = lax.broadcasted_iota(jnp.int32, (FILTER_TAPS, LANES), 1) // GROUP
    filt = jnp.zeros((FILTER_TAPS, LANES), F32)
    for g in range(LANES // GROUP):
        filt = jnp.where(lane_group == g, filt_ref[:, g : g + 1], filt)

    def convolve(side, low, high):
        count = high - low
        span = count + FILTER_TAPS - 1

        def featured(stream, first, number):
            cols = slice(stream * LANES, (stream + 1) * LANES)
            total = None
            for j in range(FEAT_TAPS):
                row = first + RIM - j
                term = taps_ref[j, stream : stream + 1, :] * ext[side, row : row + number, cols]
                total = term if total is None else total + term
            return total

        first = low - (FILTER_TAPS - 1)
        mix[0:span, :] = featured(0, first, span) * featured(2, first, span)
        response = None
        for j in range(FILTER_TAPS):
            row = FILTER_TAPS - 1 - j
            term = filt[j : j + 1, :] * mix[row : row + count, :]
            response = term if response is None else response + term
        out = featured(1, low, count) * response
        gated_ref[side * half + low : side * half + high, :] = out.astype(BF16)

    convolve(0, edge, half)
    convolve(1, edge, half)
    rim_copies[0].wait_recv()
    ext[0, :RIM, :] = jnp.where(dev == 0, 0.0, halo[0].astype(F32)[RIM:])
    convolve(0, 0, edge)
    rim_copies[1].wait_recv()
    first_tail = str_ref[half - edge : half, :].astype(F32)[RIM:]
    ext[1, :RIM, :] = jnp.where(dev == n_ctx - 1, first_tail, halo[1].astype(F32)[RIM:])
    convolve(1, 0, edge)

    def drain(slot, carry):
        key_copy(k_ref, slot, right).wait_send()
        value_copy(v_ref, slot, right).wait_send()
        return carry

    lax.fori_loop(1, ring, drain, 0)

    def out_drain(step, carry):
        out_copy(step).wait_send()
        return carry

    lax.fori_loop(1, n_tp, out_drain, 0)
    for copy in [q_copy, st_copy] + o_copies + rim_copies + moves:
        copy.wait_send()


def local(queries, keys, values, residual, out_proj, norm_gain, in_proj, feat_taps, long_filter):
    rows, width = queries.shape
    half = rows // 2
    n_tp = lax.axis_size("tp")
    ring = lax.axis_size("ctx") // 2
    vmem = pl.BlockSpec(memory_space=pltpu.VMEM)
    hbm = pl.BlockSpec(memory_space=pltpu.HBM)
    dma = pltpu.SemaphoreType.DMA
    shape = jax.ShapeDtypeStruct((rows, width), BF16)
    return pl.pallas_call(
        functools.partial(kernel, ring),
        out_shape=(shape, shape),
        in_specs=[hbm] * 9,
        out_specs=(vmem, vmem),
        scratch_shapes=[
            pltpu.VMEM((rows, width), BF16),
            pltpu.VMEM((rows, width), BF16),
            pltpu.VMEM((rows, width), BF16),
            pltpu.VMEM((rows, width), BF16),
            pltpu.VMEM((n_tp, LANES), F32),
            pltpu.VMEM((FEAT_TAPS, 3, LANES), F32),
            pltpu.VMEM((FILTER_TAPS, LANES // GROUP), F32),
            pltpu.VMEM((ring, rows, width), BF16),
            pltpu.VMEM((ring, rows, width), BF16),
            pltpu.VMEM((rows, width), BF16),
            pltpu.VMEM((rows, 2 * width), F32),
            pltpu.VMEM((rows, 2 * width), F32),
            pltpu.VMEM((rows, width), F32),
            pltpu.VMEM((rows, width), F32),
            pltpu.VMEM((rows, width), BF16),
            pltpu.VMEM((rows, width), BF16),
            pltpu.VMEM((8, LANES), F32),
            pltpu.VMEM((8, LANES), F32),
            pltpu.VMEM((n_tp, LANES, LANES), BF16),
            pltpu.VMEM((n_tp * LANES, 3 * LANES), BF16),
            pltpu.VMEM((n_tp, rows, width), BF16),
            pltpu.VMEM((n_tp, rows, width), BF16),
            pltpu.VMEM((rows, LANES), F32),
            pltpu.VMEM((rows, 3 * LANES), F32),
            pltpu.VMEM((rows, LANES), F32),
            pltpu.VMEM((rows, 3 * LANES), BF16),
            pltpu.VMEM((2, 2 * RIM, 3 * LANES), BF16),
            pltpu.VMEM((2, RIM + half, 3 * LANES), F32),
            pltpu.VMEM((RIM + half, LANES), F32),
            dma((11,)),
            dma((ring,)),
            dma((ring,)),
            dma((ring,)),
            dma((ring,)),
            dma((6,)),
            dma((6,)),
            dma((n_tp,)),
            dma((n_tp,)),
            dma((2, 2, 17)),
            dma((2, 2, 17)),
        ],
        compiler_params=pltpu.CompilerParams(
            collective_id=0, has_side_effects=True, vmem_limit_bytes=60 * 1024 * 1024
        ),
        cost_estimate=pl.CostEstimate(
            flops=4 * 10**9, bytes_accessed=4 * 10**6, transcendentals=5 * 10**6
        ),
    )(
        queries,
        keys,
        values,
        residual,
        out_proj,
        norm_gain.reshape(n_tp, LANES),
        jnp.transpose(in_proj, (1, 0, 2)),
        feat_taps,
        long_filter,
    )


def solution(mesh):
    return jax.shard_map(
        local,
        mesh=mesh,
        in_specs=(
            P("ctx", "tp"),
            P("ctx", "tp"),
            P("ctx", "tp"),
            P("ctx", "tp"),
            P("tp", None),
            P(),
            P(None, None, "tp"),
            P(None, None, "tp"),
            P(None, "tp"),
        ),
        out_specs=(P("ctx", "tp"), P("ctx", "tp")),
        check_vma=False,
    )
```

```python
import functools

import jax
import jax.numpy as jnp
from jax import lax
from jax.experimental import pallas as pl
from jax.experimental.pallas import tpu as pltpu
from jax.sharding import PartitionSpec as P

MESH = pl.DeviceIdType.MESH
LANES = 128
GROUP = 16
FEAT_TAPS = 3
FILTER_TAPS = 7
RIM = 8
LOW = -1e30
LOG2E = 1.4426950408889634
F32 = jnp.float32
BF16 = jnp.bfloat16


def kernel(
    ring,
    q_hbm,
    k_hbm,
    v_hbm,
    res_hbm,
    outp_hbm,
    gain_hbm,
    inp_hbm,
    taps_hbm,
    filt_hbm,
    hid_ref,
    gated_ref,
    q_ref,
    k_ref,
    v_ref,
    gain_ref,
    taps_ref,
    filt_ref,
    kbuf,
    vbuf,
    qpar,
    acc_own,
    acc_par,
    max_own,
    max_par,
    o_send,
    o_recv,
    st_send,
    st_recv,
    wo_all,
    win,
    joint,
    att_all,
    res_all,
    hid_acc,
    str_acc,
    sq_all,
    str_ref,
    halo,
    ext,
    mix,
    in_sem,
    ks_sem,
    kr_sem,
    vs_sem,
    vr_sem,
    x_send,
    x_recv,
    w_send,
    w_recv,
    g_send,
    g_recv,
):
    rows, width = q_ref.shape
    half = rows // 2
    quarter = half // 2
    top = ring // 2
    n_ctx = 2 * ring
    n_tp = att_all.shape[0]
    n_x = n_tp // 4
    dev = lax.axis_index("ctx")
    y_hi = dev // ring
    z = lax.rem(dev, ring)
    tp = lax.axis_index("tp")
    x = tp // 4
    y_lo = lax.rem(tp, 4) // 2
    core = lax.rem(tp, 2)
    scale = LOG2E * width**-0.5

    def ctx_id(y_at, z_at):
        return {"ctx": y_at * ring + z_at}

    right = ctx_id(y_hi, lax.rem(z + 1, ring))
    left = ctx_id(y_hi, lax.rem(z + ring - 1, ring))
    across = ctx_id(1 - y_hi, z)
    after = {"ctx": lax.rem(dev + 1, n_ctx)}
    before = {"ctx": lax.rem(dev + n_ctx - 1, n_ctx)}

    def tp_at(dx, dy, dc):
        return (
            lax.rem(x + dx + n_x, n_x) * 4
            + (1 - y_lo if dy else y_lo) * 2
            + (1 - core if dc else core)
        )

    barrier = pltpu.get_barrier_semaphore()
    for other in (right, left, across, after, before):
        pl.semaphore_signal(barrier, inc=1, device_id=other, device_id_type=MESH)

    def greet(step, carry):
        peer = lax.rem(tp + step, n_tp)
        pl.semaphore_signal(barrier, inc=1, device_id={"tp": peer}, device_id_type=MESH)
        return carry

    lax.fori_loop(1, n_tp, greet, 0)

    own_cols = pl.ds(pl.multiple_of(tp * LANES, LANES), LANES)

    def head_rows(head, first=0, count=LANES):
        return pl.ds(pl.multiple_of(head * LANES + first, count), count)

    loads = []
    for src, dst in [
        (q_hbm, q_ref),
        (k_hbm, k_ref),
        (v_hbm, v_ref),
        (res_hbm, res_all.at[tp]),
        (outp_hbm, wo_all.at[head_rows(tp), :]),
        (gain_hbm, gain_ref),
        (taps_hbm, taps_ref),
        (filt_hbm, filt_ref),
    ] + [(inp_hbm.at[s], win.at[:, s * LANES : (s + 1) * LANES]) for s in range(3)]:
        load = pltpu.make_async_copy(src, dst, in_sem.at[len(loads)])
        load.start()
        loads.append(load)

    for acc, top_ref in ((acc_own, max_own), (acc_par, max_par)):
        acc[...] = jnp.zeros_like(acc)
        top_ref[...] = jnp.full(top_ref.shape, LOW, F32)
    pl.semaphore_wait(barrier, n_tp - 1 + 5)

    def remote(src, dst, send, recv, to):
        return pltpu.make_async_remote_copy(
            src_ref=src, dst_ref=dst, send_sem=send, recv_sem=recv, device_id=to, device_id_type=MESH
        )

    def key_copy(src, slot, to):
        return remote(src, kbuf.at[slot], ks_sem.at[slot], kr_sem.at[slot], to)

    def value_copy(src, slot, to):
        return remote(src, vbuf.at[slot], vs_sem.at[slot], vr_sem.at[slot], to)

    key_copy(k_hbm, 1, right).start()
    key_copy(k_hbm, ring - 1, left).start()
    q_copy = remote(q_hbm, qpar, x_send.at[0], x_recv.at[0], across)
    q_copy.start()
    value_copy(v_hbm, 1, right).start()
    value_copy(v_hbm, ring - 1, left).start()

    targets = {
        "y": {"tp": tp_at(0, 1, 0)},
        "xp": {"tp": tp_at(1, 0, 0)},
        "xm": {"tp": tp_at(-1, 0, 0)},
        "c": {"tp": tp_at(0, 0, 1)},
    }
    moves = []

    def gather(which, side, place, span, consume):
        whole = (side * span, span)
        head = (side * span, span // 2)
        tail = (side * span + span // 2, span // 2)
        known = {}

        def copy_of(dx, dy, dc, part, number, to):
            ref = place(tp_at(dx, dy, dc), *part)
            return remote(
                ref, ref, g_send.at[which, side, number], g_recv.at[which, side, number], targets[to]
            )

        def go(dx, dy, to, part=whole):
            number = len(known)
            known[dx, dy, to] = (number, part)
            copy_of(dx, dy, 0, part, number, to).start()
            moves.append(lambda: copy_of(dx, dy, 0, part, number, to))

        def come(dx, dy, to):
            number, part = known[dx, dy, to]
            sx = dx + {"xp": -1, "xm": 1}.get(to, 0)
            sy = 1 - dy if to == "y" else dy
            copy_of(sx, sy, 1 if to == "c" else 0, part, number, to).wait_recv()

        def pair(dx, dy):
            come(dx, dy, "c")
            consume(tp_at(dx, dy, 0) // 2)

        def relay(dx, dy):
            go(dx, dy, "xp" if dx < 0 else "xm", head if dx < 0 else tail)

        def y_first():
            for to in ("y", "xp", "xm", "c"):
                go(0, 0, to)
            yield
            come(0, 0, "y")
            for to in ("xp", "xm", "c"):
                go(0, 1, to)
            pair(0, 0)
            yield
            for dx, to in ((-1, "xp"), (1, "xm")):
                come(0, 0, to)
                relay(dx, 0)
                go(dx, 0, "c")
            yield
            pair(0, 1)
            for dx, to in ((-1, "xp"), (1, "xm")):
                come(0, 1, to)
                relay(dx, 1)
                go(dx, 1, "c")
            yield
            pair(-1, 0)
            pair(1, 0)
            yield
            come(-1, 0, "xp")
            come(1, 0, "xm")
            go(2, 0, "c")
            pair(-1, 1)
            pair(1, 1)
            yield
            come(-1, 1, "xp")
            come(1, 1, "xm")
            go(2, 1, "c")
            pair(2, 0)
            yield
            pair(2, 1)
            yield

        def x_first():
            for to in ("xp", "xm", "y", "c"):
                go(0, 0, to)
            yield
            pair(0, 0)
            for dx, to in ((-1, "xp"), (1, "xm")):
                come(0, 0, to)
                relay(dx, 0)
                go(dx, 0, "y")
                go(dx, 0, "c")
            yield
            come(0, 0, "y")
            go(0, 1, "c")
            pair(-1, 0)
            pair(1, 0)
            yield
            come(-1, 0, "xp")
            come(1, 0, "xm")
            go(2, 0, "y")
            go(2, 0, "c")
            come(-1, 0, "y")
            go(-1, 1, "c")
            come(1, 0, "y")
            go(1, 1, "c")
            yield
            pair(0, 1)
            pair(2, 0)
            yield
            come(2, 0, "y")
            go(2, 1, "c")
            pair(-1, 1)
            pair(1, 1)
            yield
            pair(2, 1)
            yield

        return x_first() if side else y_first()

    ones = jnp.ones((half, LANES), BF16)
    tri = lax.broadcasted_iota(jnp.int32, (half, half), 0) >= lax.broadcasted_iota(
        jnp.int32, (half, half), 1
    )

    def unit(queries, acc, top_ref, offset, blocks, masked=False):
        at = pl.ds(offset, half)
        rows_q = queries[at, :]
        scores = [
            lax.dot_general(rows_q, keys, (((1,), (1,)), ((), ())), preferred_element_type=F32)
            for keys, _ in blocks
        ]
        if masked:
            scores = [jnp.where(tri, block, LOW) for block in scores]
        old = top_ref[at, :]
        best = functools.reduce(jnp.maximum, scores)
        new = jnp.maximum(old, jnp.max(best, axis=1, keepdims=True))
        top_ref[at, :] = new
        wide = jnp.concatenate([new] * (half // LANES), axis=1)
        factor = jnp.exp2((old - new) * scale)
        total = acc[at, :] * jnp.concatenate([factor, factor], axis=1)
        for block, (_, values) in zip(scores, blocks):
            weights = jnp.exp2((block - wide) * scale).astype(BF16)
            total = total + jnp.dot(
                weights, jnp.concatenate([values, ones], axis=1), preferred_element_type=F32
            )
        acc[at, :] = total

    row_c = pl.multiple_of(y_hi * half, half)

    def first_units(pairs):
        blocks = [(keys[:half, :], values[:half, :]) for keys, values in pairs]
        unit(qpar, acc_par, max_par, half, blocks)
        return blocks

    def third_unit(pairs):
        at = pl.ds(row_c, half)
        unit(qpar, acc_par, max_par, row_c, [(keys[at, :], values[at, :]) for keys, values in pairs])

    def last_unit(keys, values, slot):
        row_d = pl.multiple_of(jnp.where(slot <= z, 0, half), half)
        at = pl.ds(row_d, half)
        unit(q_ref, acc_own, max_own, row_d, [(keys[at, :], values[at, :])])

    def early(slots):
        pairs = [(kbuf.at[slot], vbuf.at[slot]) for slot in slots]
        blocks = first_units(pairs)
        unit(q_ref, acc_own, max_own, half, blocks)

    def late(slots):
        third_unit([(kbuf.at[slot], vbuf.at[slot]) for slot in slots])
        for slot in slots:
            last_unit(kbuf.at[slot], vbuf.at[slot], slot)

    for load in loads[:5]:
        load.wait()

    def res_place(chunk, first, count):
        return res_all.at[chunk, pl.ds(first, count), :]

    def wo_place(chunk, first, count):
        return wo_all.at[head_rows(chunk, first, count), :]

    def att_place(chunk, first, count):
        return att_all.at[chunk, pl.ds(first, count), :]

    def nothing(chip):
        pass

    res_a = gather(1, 0, res_place, half, nothing)
    res_b = gather(1, 1, res_place, half, nothing)
    wo_a = gather(2, 0, wo_place, LANES // 2, nothing)
    wo_b = gather(2, 1, wo_place, LANES // 2, nothing)
    for stages in (res_a, res_b, wo_a, wo_b):
        next(stages)
    for load in loads[5:]:
        load.wait()
    str_acc[...] = jnp.zeros_like(str_acc)
    diagonal = lax.broadcasted_iota(jnp.int32, (LANES, LANES), 0) == lax.broadcasted_iota(
        jnp.int32, (LANES, LANES), 1
    )

    def to_column(line):
        return jnp.sum(jnp.where(diagonal, line, 0.0), axis=1, keepdims=True)

    def to_line(column):
        return jnp.sum(jnp.where(diagonal, column, 0.0), axis=0, keepdims=True)

    def scale_win():
        def block(head, carry):
            at = head_rows(head)
            column = to_column(gain_ref[pl.ds(head, 1), :])
            win[at, :] = (win[at, :].astype(F32) * column).astype(BF16)
            return carry

        lax.fori_loop(0, n_tp, block, 0)

    def chip_rows(chip):
        return pl.ds(pl.multiple_of(chip * 2 * LANES, 2 * LANES), 2 * LANES)

    def prepare(*offsets):
        for dx, dy in offsets:
            chip = tp_at(dx, dy, 0) // 2
            deep = chip_rows(chip)
            joint[deep, :] = jnp.dot(
                wo_all[deep, :], win[...], preferred_element_type=F32
            ).astype(BF16)
            left_side = jnp.concatenate([res_all[2 * chip], res_all[2 * chip + 1]], axis=1)
            str_acc[...] += jnp.dot(left_side, win[deep, :], preferred_element_type=F32)

    def steps(*names):
        for stages in names:
            next(stages)

    plan = {
        1: ((res_a, res_a, res_b), ()),
        2: ((wo_a, wo_a, wo_b, res_a, res_a, res_b), ()),
        3: ((res_a, res_b), ()),
        4: ((wo_b, wo_a, wo_a, res_a, res_b), ()),
        5: ((wo_a, wo_b, res_a, res_b), ()),
        6: ((wo_a, wo_b, res_b), ((0, 0), (0, 1))),
        7: ((wo_a, wo_b), ((-1, 0), (1, 0))),
    }

    def extra(number):
        names, offsets = plan[number]
        steps(*names)
        prepare(*offsets)
        if number == 3:
            scale_win()
    unit(q_ref, acc_own, max_own, 0, [(k_ref[:half, :], v_ref[:half, :])], True)
    unit(q_ref, acc_own, max_own, half, [(k_ref[half:, :], v_ref[half:, :])], True)
    unit(q_ref, acc_own, max_own, half, [(k_ref[:half, :], v_ref[:half, :])])

    def turn(step, carry):
        back = ring - step
        key_copy(k_ref, step, right).wait_recv()
        key_copy(kbuf.at[step], step + 1, right).start()
        key_copy(k_ref, back, left).wait_recv()

        @pl.when(step < top - 1)
        def _():
            key_copy(kbuf.at[back], back - 1, left).start()

        @pl.when(step > 1)
        def _():
            late((step - 1, back + 1))

        @pl.when(step == 1)
        def _():
            q_copy.wait_recv()
            first_units([(k_ref, v_ref)])
            third_unit([(k_ref, v_ref)])

        value_copy(v_ref, step, right).wait_recv()

        @pl.when(step < top - 1)
        def _():
            value_copy(vbuf.at[step], step + 1, right).start()

        value_copy(v_ref, back, left).wait_recv()
        value_copy(vbuf.at[back], back - 1, left).start()
        early((step, back))
        for number in range(1, top):
            pl.when(step == number)(functools.partial(extra, number))
        return carry

    lax.fori_loop(1, top, turn, 0)
    for number in range(top, 8):
        extra(number)
    late((top - 1, top + 1))
    key_copy(k_ref, top, right).wait_recv()
    value_copy(v_ref, top, left).wait_recv()
    far = [(kbuf.at[top], vbuf.at[top])]
    blocks = first_units(far)
    third_unit(far)

    def settle(acc, top_ref):
        total = acc[:, LANES:]
        seen = total > 0.0
        inverse = 1.0 / jnp.where(seen, total, 1.0)
        level = jnp.where(seen, top_ref[...] * scale + jnp.log2(jnp.where(seen, total, 1.0)), LOW)
        return acc[:, :LANES] * inverse, level

    mean_par, level_par = settle(acc_par, max_par)
    o_send[...] = mean_par.astype(BF16)
    st_send[...] = jnp.zeros_like(st_send)
    for g in range(rows // LANES):
        block = level_par[g * LANES : (g + 1) * LANES, :]
        st_send[g : g + 1, :] = to_line(block)
    sides = (pl.ds(0, half), pl.ds(half, half))
    st_copy = remote(st_send, st_recv, x_send.at[1], x_recv.at[1], across)
    st_copy.start()
    o_copies = [
        remote(o_send.at[at, :], o_recv.at[at, :], x_send.at[2 + n], x_recv.at[2 + n], across)
        for n, at in enumerate(sides)
    ]
    for copy in o_copies:
        copy.start()
    unit(q_ref, acc_own, max_own, half, blocks)
    last_unit(kbuf.at[top], vbuf.at[top], top)
    mean_own, level_own = settle(acc_own, max_own)
    steps(wo_b)
    prepare((-1, 1), (1, 1), (2, 0), (2, 1))
    hid_acc[...] = res_all[tp].astype(F32)
    st_copy.wait_recv()

    def join(side):
        o_copies[side].wait_recv()
        for g in range(side * half // LANES, (side + 1) * half // LANES):
            at = slice(g * LANES, (g + 1) * LANES)
            level_other = to_column(st_recv[g : g + 1, :])
            here = level_own[at, :]
            most = jnp.maximum(here, level_other)
            w_own = jnp.exp2(here - most)
            w_other = jnp.exp2(level_other - most)
            joined = (w_own * mean_own[at, :] + w_other * o_recv[at, :].astype(F32)) / (
                w_own + w_other
            )
            att_all[tp, at, :] = joined.astype(BF16)

    def project(side):
        at = sides[side]

        def apply(chip):
            left_side = jnp.concatenate(
                [att_all[2 * chip, at, :], att_all[2 * chip + 1, at, :]], axis=1
            )
            deep = chip_rows(chip)
            weight = jnp.concatenate([wo_all[deep, own_cols], joint[deep, :]], axis=1)
            product = jnp.dot(left_side, weight, preferred_element_type=F32)
            hid_acc[at, :] += product[:, :LANES]
            str_acc[at, :] += product[:, LANES:]

        return apply

    def square_copy(side, step):
        peer = lax.rem(tp + step, n_tp)
        ref = sq_all.at[tp, side]
        return remote(ref, ref, w_send.at[side, step], w_recv.at[side, step], {"tp": peer})

    def square_each(side, act):
        def one(step, carry):
            act(square_copy(side, step))
            return carry

        lax.fori_loop(1, n_tp, one, 0)

    def finish_hidden(side):
        at = sides[side]
        hidden = hid_acc[at, :].astype(BF16)
        hid_ref[at, :] = hidden
        wide = hidden.astype(F32)
        column = jnp.sum(wide * wide, axis=1, keepdims=True)
        sq_all[tp, side] = jnp.zeros((8, LANES), F32)
        for g in range(half // LANES):
            sq_all[tp, side, g : g + 1, :] = to_line(column[g * LANES : (g + 1) * LANES])
        square_each(side, lambda copy: copy.start())

    edge = 2 * RIM
    rim_copies = [
        remote(
            str_ref.at[(side + 1) * half - edge : (side + 1) * half, :],
            halo.at[side],
            x_send.at[4 + side],
            x_recv.at[4 + side],
            to,
        )
        for side, to in enumerate((after, before))
    ]

    def finish_streams(side):
        square_each(side, lambda copy: copy.wait_recv())
        lines = jnp.sum(sq_all[:, side], axis=0)
        for g in range(half // LANES):
            at = slice(side * half + g * LANES, side * half + (g + 1) * LANES)
            mean_square = to_column(lines[g : g + 1, :]) / (n_tp * LANES)
            streams = (str_acc[at, :] * lax.rsqrt(mean_square + 1e-6)).astype(BF16)
            str_ref[at, :] = streams
            ext[side, RIM + g * LANES : RIM + (g + 1) * LANES, :] = streams.astype(F32)
        rim_copies[side].start()

    out_a = gather(0, 0, att_place, half, project(0))
    out_b = gather(0, 1, att_place, half, project(1))
    join(0)
    next(out_a)
    join(1)
    next(out_b)
    steps(out_a, out_a, out_b, out_b, out_a, out_a, out_a, out_b, out_a, out_b, out_a)
    finish_hidden(0)
    steps(out_b, out_b)
    finish_hidden(1)
    finish_streams(0)
    finish_streams(1)

    lane_group = lax.broadcasted_iota(jnp.int32, (FILTER_TAPS, LANES), 1) // GROUP
    filt = jnp.zeros((FILTER_TAPS, LANES), F32)
    for g in range(LANES // GROUP):
        filt = jnp.where(lane_group == g, filt_ref[:, g : g + 1], filt)

    def convolve(side, low, high):
        count = high - low
        span = count + FILTER_TAPS - 1

        def featured(stream, first, number):
            cols = slice(stream * LANES, (stream + 1) * LANES)
            total = None
            for j in range(FEAT_TAPS):
                row = first + RIM - j
                term = taps_ref[j, stream : stream + 1, :] * ext[side, row : row + number, cols]
                total = term if total is None else total + term
            return total

        first = low - (FILTER_TAPS - 1)
        mix[0:span, :] = featured(0, first, span) * featured(2, first, span)
        response = None
        for j in range(FILTER_TAPS):
            row = FILTER_TAPS - 1 - j
            term = filt[j : j + 1, :] * mix[row : row + count, :]
            response = term if response is None else response + term
        out = featured(1, low, count) * response
        gated_ref[side * half + low : side * half + high, :] = out.astype(BF16)

    convolve(0, edge, half)
    convolve(1, edge, half)
    rim_copies[0].wait_recv()
    ext[0, :RIM, :] = jnp.where(dev == 0, 0.0, halo[0].astype(F32)[RIM:])
    convolve(0, 0, edge)
    rim_copies[1].wait_recv()
    first_tail = str_ref[half - edge : half, :].astype(F32)[RIM:]
    ext[1, :RIM, :] = jnp.where(dev == n_ctx - 1, first_tail, halo[1].astype(F32)[RIM:])
    convolve(1, 0, edge)

    def drain(slot, carry):
        key_copy(k_ref, slot, right).wait_send()
        value_copy(v_ref, slot, right).wait_send()
        return carry

    lax.fori_loop(1, ring, drain, 0)

    for side in range(2):
        square_each(side, lambda copy: copy.wait_send())
    for copy in [q_copy, st_copy] + o_copies + rim_copies:
        copy.wait_send()
    for move in moves:
        move().wait_send()


def local(queries, keys, values, residual, out_proj, norm_gain, in_proj, feat_taps, long_filter):
    rows, width = queries.shape
    half = rows // 2
    n_tp = lax.axis_size("tp")
    ring = lax.axis_size("ctx") // 2
    vmem = pl.BlockSpec(memory_space=pltpu.VMEM)
    hbm = pl.BlockSpec(memory_space=pltpu.HBM)
    dma = pltpu.SemaphoreType.DMA
    shape = jax.ShapeDtypeStruct((rows, width), BF16)
    return pl.pallas_call(
        functools.partial(kernel, ring),
        out_shape=(shape, shape),
        in_specs=[hbm] * 9,
        out_specs=(vmem, vmem),
        scratch_shapes=[
            pltpu.VMEM((rows, width), BF16),
            pltpu.VMEM((rows, width), BF16),
            pltpu.VMEM((rows, width), BF16),
            pltpu.VMEM((n_tp, LANES), F32),
            pltpu.VMEM((FEAT_TAPS, 3, LANES), F32),
            pltpu.VMEM((FILTER_TAPS, LANES // GROUP), F32),
            pltpu.VMEM((ring, rows, width), BF16),
            pltpu.VMEM((ring, rows, width), BF16),
            pltpu.VMEM((rows, width), BF16),
            pltpu.VMEM((rows, 2 * width), F32),
            pltpu.VMEM((rows, 2 * width), F32),
            pltpu.VMEM((rows, width), F32),
            pltpu.VMEM((rows, width), F32),
            pltpu.VMEM((rows, width), BF16),
            pltpu.VMEM((rows, width), BF16),
            pltpu.VMEM((8, LANES), F32),
            pltpu.VMEM((8, LANES), F32),
            pltpu.VMEM((n_tp * LANES, n_tp * LANES), BF16),
            pltpu.VMEM((n_tp * LANES, 3 * LANES), BF16),
            pltpu.VMEM((n_tp * LANES, 3 * LANES), BF16),
            pltpu.VMEM((n_tp, rows, width), BF16),
            pltpu.VMEM((n_tp, rows, width), BF16),
            pltpu.VMEM((rows, LANES), F32),
            pltpu.VMEM((rows, 3 * LANES), F32),
            pltpu.VMEM((n_tp, 2, 8, LANES), F32),
            pltpu.VMEM((rows, 3 * LANES), BF16),
            pltpu.VMEM((2, 2 * RIM, 3 * LANES), BF16),
            pltpu.VMEM((2, RIM + half, 3 * LANES), F32),
            pltpu.VMEM((RIM + half, LANES), F32),
            dma((11,)),
            dma((ring,)),
            dma((ring,)),
            dma((ring,)),
            dma((ring,)),
            dma((6,)),
            dma((6,)),
            dma((2, n_tp)),
            dma((2, n_tp)),
            dma((3, 2, 17)),
            dma((3, 2, 17)),
        ],
        compiler_params=pltpu.CompilerParams(
            collective_id=0, has_side_effects=True, vmem_limit_bytes=40 * 1024 * 1024
        ),
        cost_estimate=pl.CostEstimate(
            flops=4 * 10**9, bytes_accessed=4 * 10**6, transcendentals=5 * 10**6
        ),
    )(
        *(
            pltpu.with_memory_space_constraint(operand, pltpu.HBM)
            for operand in (
                queries,
                keys,
                values,
                residual,
                out_proj,
                norm_gain.reshape(n_tp, LANES),
                jnp.transpose(in_proj, (1, 0, 2)),
                feat_taps,
                long_filter,
            )
        )
    )


def solution(mesh):
    return jax.shard_map(
        local,
        mesh=mesh,
        in_specs=(
            P("ctx", "tp"),
            P("ctx", "tp"),
            P("ctx", "tp"),
            P("ctx", "tp"),
            P("tp", None),
            P(),
            P(None, None, "tp"),
            P(None, None, "tp"),
            P(None, "tp"),
        ),
        out_specs=(P("ctx", "tp"), P("ctx", "tp")),
        check_vma=False,
    )
```

```python
import functools

import jax
import jax.numpy as jnp
from jax import lax
from jax.experimental import pallas as pl
from jax.experimental.pallas import tpu as pltpu
from jax.sharding import PartitionSpec as P

MESH = pl.DeviceIdType.MESH
LANES = 128
GROUP = 16
FEAT_TAPS = 3
FILTER_TAPS = 7
RIM = 8
LOW = -1e30
LOG2E = 1.4426950408889634
F32 = jnp.float32
BF16 = jnp.bfloat16


def kernel(
    ring,
    q_hbm,
    k_hbm,
    v_hbm,
    res_hbm,
    outp_hbm,
    gain_hbm,
    inp_hbm,
    taps_hbm,
    filt_hbm,
    hid_ref,
    gated_ref,
    q_ref,
    k_ref,
    v_ref,
    gain_ref,
    taps_ref,
    filt_ref,
    kbuf,
    vbuf,
    qpar,
    acc_own,
    acc_par,
    max_own,
    max_par,
    o_send,
    o_recv,
    st_send,
    st_recv,
    wo_all,
    win,
    joint,
    att_all,
    res_all,
    hid_acc,
    str_acc,
    sq_all,
    ext,
    mix,
    in_sem,
    ks_sem,
    kr_sem,
    vs_sem,
    vr_sem,
    x_send,
    x_recv,
    w_send,
    w_recv,
    h_send,
    h_recv,
    g_send,
    g_recv,
):
    rows, width = q_ref.shape
    half = rows // 2
    edge = 2 * RIM
    rim = pl.ds(rows, 2 * edge)
    top = ring // 2
    n_ctx = 2 * ring
    n_tp = att_all.shape[0]
    n_x = n_tp // 4
    dev = lax.axis_index("ctx")
    y_hi = dev // ring
    z = lax.rem(dev, ring)
    tp = lax.axis_index("tp")
    x = tp // 4
    y_lo = lax.rem(tp, 4) // 2
    core = lax.rem(tp, 2)
    scale = LOG2E * width**-0.5

    def ctx_id(y_at, z_at):
        return {"ctx": y_at * ring + z_at}

    right = ctx_id(y_hi, lax.rem(z + 1, ring))
    left = ctx_id(y_hi, lax.rem(z + ring - 1, ring))
    across = ctx_id(1 - y_hi, z)
    after = {"ctx": lax.rem(dev + 1, n_ctx)}
    before = {"ctx": lax.rem(dev + n_ctx - 1, n_ctx)}

    def tp_at(dx, dy, dc):
        return (
            lax.rem(x + dx + n_x, n_x) * 4
            + (1 - y_lo if dy else y_lo) * 2
            + (1 - core if dc else core)
        )

    barrier = pltpu.get_barrier_semaphore()
    for other in (right, left, across, after, before):
        pl.semaphore_signal(barrier, inc=1, device_id=other, device_id_type=MESH)

    def greet(step, carry):
        peer = lax.rem(tp + step, n_tp)
        pl.semaphore_signal(barrier, inc=1, device_id={"tp": peer}, device_id_type=MESH)
        return carry

    lax.fori_loop(1, n_tp, greet, 0)

    own_cols = pl.ds(pl.multiple_of(tp * LANES, LANES), LANES)

    def head_rows(head, first=0, count=LANES):
        return pl.ds(pl.multiple_of(head * LANES + first, count), count)

    loads = []
    for src, dst in [
        (q_hbm, q_ref),
        (k_hbm, k_ref),
        (v_hbm, v_ref),
        (res_hbm, res_all.at[tp, pl.ds(0, rows), :]),
        (outp_hbm, wo_all.at[head_rows(tp), :]),
        (gain_hbm, gain_ref),
        (taps_hbm, taps_ref),
        (filt_hbm, filt_ref),
    ] + [(inp_hbm.at[s], win.at[:, s * LANES : (s + 1) * LANES]) for s in range(3)]:
        load = pltpu.make_async_copy(src, dst, in_sem.at[len(loads)])
        load.start()
        loads.append(load)

    for acc, top_ref in ((acc_own, max_own), (acc_par, max_par)):
        acc[...] = jnp.zeros_like(acc)
        top_ref[...] = jnp.full(top_ref.shape, LOW, F32)
    pl.semaphore_wait(barrier, n_tp - 1 + 5)

    def remote(src, dst, send, recv, to):
        return pltpu.make_async_remote_copy(
            src_ref=src, dst_ref=dst, send_sem=send, recv_sem=recv, device_id=to, device_id_type=MESH
        )

    def part_of(ref, side):
        return ref.at[pl.ds(side * half, half), :]

    def key_copy(src, slot, side, to):
        dst = part_of(kbuf.at[slot], side)
        return remote(src, dst, ks_sem.at[slot, side], kr_sem.at[slot, side], to)

    def value_copy(src, slot, side, to):
        dst = part_of(vbuf.at[slot], side)
        return remote(src, dst, vs_sem.at[slot, side], vr_sem.at[slot, side], to)

    q_copy = remote(q_hbm, qpar, x_send.at[0], x_recv.at[0], across)
    for side in range(2):
        for to, slot in ((right, 1), (left, ring - 1)):
            key_copy(part_of(k_hbm, side), slot, side, to).start()
        for to, slot in ((right, 1), (left, ring - 1)):
            value_copy(part_of(v_hbm, side), slot, side, to).start()
        if side == 0:
            q_copy.start()

    def tail_copies(src, dst, first_sem):
        return [
            remote(
                src.at[pl.ds((side + 1) * half - edge, edge), :],
                dst.at[tp, pl.ds(rows + side * edge, edge), :],
                x_send.at[first_sem + side],
                x_recv.at[first_sem + side],
                to,
            )
            for side, to in enumerate((after, before))
        ]

    res_tails = tail_copies(res_hbm, res_all, 5)
    for copy in res_tails:
        copy.start()

    def spread_each(which, buf, act):
        def one(step, carry):
            ref = buf.at[tp, rim, :]
            peer = lax.rem(tp + step, n_tp)
            act(remote(ref, ref, h_send.at[which, step], h_recv.at[which, step], {"tp": peer}))
            return carry

        lax.fori_loop(1, n_tp, one, 0)

    targets = {
        "y": {"tp": tp_at(0, 1, 0)},
        "xp": {"tp": tp_at(1, 0, 0)},
        "xm": {"tp": tp_at(-1, 0, 0)},
        "c": {"tp": tp_at(0, 0, 1)},
    }
    moves = []

    def gather(which, side, place, span, consume):
        whole = (side * span, span)
        head = (side * span, span // 2)
        tail = (side * span + span // 2, span // 2)
        known = {}

        def copy_of(dx, dy, dc, part, number, to):
            ref = place(tp_at(dx, dy, dc), *part)
            return remote(
                ref, ref, g_send.at[which, side, number], g_recv.at[which, side, number], targets[to]
            )

        def go(dx, dy, to, part=whole):
            number = len(known)
            known[dx, dy, to] = (number, part)
            copy_of(dx, dy, 0, part, number, to).start()
            moves.append(lambda: copy_of(dx, dy, 0, part, number, to))

        def come(dx, dy, to):
            number, part = known[dx, dy, to]
            sx = dx + {"xp": -1, "xm": 1}.get(to, 0)
            sy = 1 - dy if to == "y" else dy
            copy_of(sx, sy, 1 if to == "c" else 0, part, number, to).wait_recv()

        def pair(dx, dy):
            come(dx, dy, "c")
            consume(tp_at(dx, dy, 0) // 2)

        def relay(dx, dy):
            go(dx, dy, "xp" if dx < 0 else "xm", head if dx < 0 else tail)

        def y_first():
            for to in ("y", "xp", "xm", "c"):
                go(0, 0, to)
            yield
            come(0, 0, "y")
            for to in ("xp", "xm", "c"):
                go(0, 1, to)
            pair(0, 0)
            yield
            for dx, to in ((-1, "xp"), (1, "xm")):
                come(0, 0, to)
                relay(dx, 0)
                go(dx, 0, "c")
            yield
            pair(0, 1)
            for dx, to in ((-1, "xp"), (1, "xm")):
                come(0, 1, to)
                relay(dx, 1)
                go(dx, 1, "c")
            yield
            pair(-1, 0)
            pair(1, 0)
            yield
            come(-1, 0, "xp")
            come(1, 0, "xm")
            go(2, 0, "c")
            pair(-1, 1)
            pair(1, 1)
            yield
            come(-1, 1, "xp")
            come(1, 1, "xm")
            go(2, 1, "c")
            pair(2, 0)
            yield
            pair(2, 1)
            yield

        def x_first():
            for to in ("xp", "xm", "y", "c"):
                go(0, 0, to)
            yield
            pair(0, 0)
            for dx, to in ((-1, "xp"), (1, "xm")):
                come(0, 0, to)
                relay(dx, 0)
                go(dx, 0, "y")
                go(dx, 0, "c")
            yield
            come(0, 0, "y")
            go(0, 1, "c")
            pair(-1, 0)
            pair(1, 0)
            yield
            come(-1, 0, "xp")
            come(1, 0, "xm")
            go(2, 0, "y")
            go(2, 0, "c")
            come(-1, 0, "y")
            go(-1, 1, "c")
            come(1, 0, "y")
            go(1, 1, "c")
            yield
            pair(0, 1)
            pair(2, 0)
            yield
            come(2, 0, "y")
            go(2, 1, "c")
            pair(-1, 1)
            pair(1, 1)
            yield
            pair(2, 1)
            yield

        return x_first() if side else y_first()

    ones = jnp.ones((half, LANES), BF16)
    tri = lax.broadcasted_iota(jnp.int32, (half, half), 0) >= lax.broadcasted_iota(
        jnp.int32, (half, half), 1
    )

    def unit(queries, acc, top_ref, offset, blocks, masked=False):
        at = pl.ds(offset, half)
        rows_q = queries[at, :]
        scores = [
            lax.dot_general(rows_q, keys, (((1,), (1,)), ((), ())), preferred_element_type=F32)
            for keys, _ in blocks
        ]
        if masked:
            scores = [jnp.where(tri, block, LOW) for block in scores]
        old = top_ref[at, :]
        best = functools.reduce(jnp.maximum, scores)
        new = jnp.maximum(old, jnp.max(best, axis=1, keepdims=True))
        top_ref[at, :] = new
        wide = jnp.concatenate([new] * (half // LANES), axis=1)
        factor = jnp.exp2((old - new) * scale)
        total = acc[at, :] * jnp.concatenate([factor, factor], axis=1)
        for block, (_, values) in zip(scores, blocks):
            weights = jnp.exp2((block - wide) * scale).astype(BF16)
            total = total + jnp.dot(
                weights, jnp.concatenate([values, ones], axis=1), preferred_element_type=F32
            )
        acc[at, :] = total

    row_c = pl.multiple_of(y_hi * half, half)

    def first_units(pairs):
        blocks = [(keys[:half, :], values[:half, :]) for keys, values in pairs]
        unit(qpar, acc_par, max_par, half, blocks)
        return blocks

    def third_unit(pairs):
        at = pl.ds(row_c, half)
        unit(qpar, acc_par, max_par, row_c, [(keys[at, :], values[at, :]) for keys, values in pairs])

    def last_unit(keys, values, slot):
        row_d = pl.multiple_of(jnp.where(slot <= z, 0, half), half)
        at = pl.ds(row_d, half)
        unit(q_ref, acc_own, max_own, row_d, [(keys[at, :], values[at, :])])

    def early(slots):
        pairs = [(kbuf.at[slot], vbuf.at[slot]) for slot in slots]
        blocks = first_units(pairs)
        unit(q_ref, acc_own, max_own, half, blocks)

    def late(slots):
        third_unit([(kbuf.at[slot], vbuf.at[slot]) for slot in slots])
        for slot in slots:
            last_unit(kbuf.at[slot], vbuf.at[slot], slot)

    for load in loads[:5]:
        load.wait()

    def res_place(chunk, first, count):
        return res_all.at[chunk, pl.ds(first, count), :]

    def wo_place(chunk, first, count):
        return wo_all.at[head_rows(chunk, first, count), :]

    def att_place(chunk, first, count):
        return att_all.at[chunk, pl.ds(first, count), :]

    def nothing(chip):
        pass

    res_a = gather(1, 0, res_place, half, nothing)
    res_b = gather(1, 1, res_place, half, nothing)
    wo_a = gather(2, 0, wo_place, LANES // 2, nothing)
    wo_b = gather(2, 1, wo_place, LANES // 2, nothing)
    for stages in (res_a, res_b, wo_a, wo_b):
        next(stages)
    for load in loads[5:]:
        load.wait()
    str_acc[...] = jnp.zeros_like(str_acc)
    diagonal = lax.broadcasted_iota(jnp.int32, (LANES, LANES), 0) == lax.broadcasted_iota(
        jnp.int32, (LANES, LANES), 1
    )

    def to_column(line, count=LANES):
        return jnp.sum(jnp.where(diagonal[:count], line, 0.0), axis=1, keepdims=True)

    def to_line(column):
        picked = jnp.where(diagonal[: column.shape[0]], column, 0.0)
        return jnp.sum(picked, axis=0, keepdims=True)

    def scale_win():
        def block(head, carry):
            at = head_rows(head)
            column = to_column(gain_ref[pl.ds(head, 1), :])
            win[at, :] = (win[at, :].astype(F32) * column).astype(BF16)
            return carry

        lax.fori_loop(0, n_tp, block, 0)

    def chip_rows(chip):
        return pl.ds(pl.multiple_of(chip * 2 * LANES, 2 * LANES), 2 * LANES)

    def prepare(*offsets):
        for dx, dy in offsets:
            chip = tp_at(dx, dy, 0) // 2
            deep = chip_rows(chip)
            joint[deep, :] = jnp.dot(
                wo_all[deep, :], win[...], preferred_element_type=F32
            ).astype(BF16)
            left_side = jnp.concatenate([res_all[2 * chip], res_all[2 * chip + 1]], axis=1)
            str_acc[...] += jnp.dot(left_side, win[deep, :], preferred_element_type=F32)

    def steps(*names):
        for stages in names:
            next(stages)

    plan = {
        1: ((res_a, res_a, res_b), ()),
        2: ((wo_a, wo_a, wo_b, res_a, res_a, res_b), ()),
        3: ((res_a, res_b), ()),
        4: ((wo_b, wo_a, wo_a, res_a, res_b), ()),
        5: ((wo_a, wo_b, res_a, res_b), ()),
        6: ((wo_a, wo_b, res_b), ((0, 0), (0, 1))),
        7: ((wo_a, wo_b), ((-1, 0), (1, 0))),
    }

    def share_residual_rim():
        for copy in res_tails:
            copy.wait_recv()
        spread_each(0, res_all, lambda copy: copy.start())

    def extra(number):
        names, offsets = plan[number]
        steps(*names)
        prepare(*offsets)
        if number == 2:
            share_residual_rim()
        if number == 3:
            scale_win()
        if number == 5:
            spread_each(0, res_all, lambda copy: copy.wait_recv())
    unit(q_ref, acc_own, max_own, 0, [(k_ref[:half, :], v_ref[:half, :])], True)
    unit(q_ref, acc_own, max_own, half, [(k_ref[half:, :], v_ref[half:, :])], True)
    unit(q_ref, acc_own, max_own, half, [(k_ref[:half, :], v_ref[:half, :])])

    def key_wait(slot, side):
        key_copy(part_of(k_hbm, side), slot, side, right).wait_recv()

    def value_wait(slot, side):
        value_copy(part_of(v_hbm, side), slot, side, right).wait_recv()

    def when(condition, act):
        if isinstance(condition, bool):
            if condition:
                act()
        else:
            pl.when(condition)(act)

    def pass_keys(step, side):
        back = ring - step
        key_wait(step, side)
        key_copy(part_of(kbuf.at[step], side), step + 1, side, right).start()
        key_wait(back, side)
        when(
            step < top - 1,
            lambda: key_copy(part_of(kbuf.at[back], side), back - 1, side, left).start(),
        )

    def pass_values(step, side):
        back = ring - step
        value_wait(step, side)
        when(
            step < top - 1,
            lambda: value_copy(part_of(vbuf.at[step], side), step + 1, side, right).start(),
        )
        value_wait(back, side)
        value_copy(part_of(vbuf.at[back], side), back - 1, side, left).start()

    def meet_partner():
        q_copy.wait_recv()
        first_units([(k_ref, v_ref)])
        third_unit([(k_ref, v_ref)])

    def turn(step, carry):
        back = ring - step
        pass_keys(step, 0)
        pl.when(step > 1)(lambda: pass_keys(step - 1, 1))
        pl.when(step > 2)(lambda: late((step - 2, back + 2)))
        pl.when(step == 1)(meet_partner)
        pass_values(step, 0)
        pl.when(step > 1)(lambda: pass_values(step - 1, 1))
        early((step, back))
        for number in range(1, top):
            pl.when(step == number)(functools.partial(extra, number))
        return carry

    lax.fori_loop(1, top, turn, 0)
    for number in range(top, 8):
        extra(number)
    key_wait(top, 0)
    pass_keys(top - 1, 1)
    if top > 2:
        late((top - 2, top + 2))
    value_wait(top, 0)
    pass_values(top - 1, 1)
    far = [(kbuf.at[slot], vbuf.at[slot]) for slot in (top - 1, top + 1, top)]
    blocks = first_units(far[2:])
    pl.when(y_hi == 0)(lambda: third_unit(far))

    def settle(acc, top_ref, side):
        at = pl.ds(side * half, half)
        total = acc[at, LANES:]
        seen = total > 0.0
        inverse = 1.0 / jnp.where(seen, total, 1.0)
        level = jnp.where(
            seen, top_ref[at, :] * scale + jnp.log2(jnp.where(seen, total, 1.0)), LOW
        )
        return acc[at, :LANES] * inverse, level

    st_copies = [
        remote(st_send.at[n], st_recv.at[n], x_send.at[1 + n], x_recv.at[1 + n], across)
        for n in range(2)
    ]
    o_copies = [
        remote(part_of(o_send, n), part_of(o_recv, n), x_send.at[3 + n], x_recv.at[3 + n], across)
        for n in range(2)
    ]

    def send_partial(side):
        mean, level = settle(acc_par, max_par, side)
        o_send[side * half : (side + 1) * half, :] = mean.astype(BF16)
        o_copies[side].start()
        st_send[side] = jnp.zeros((8, LANES), F32)
        for g in range(half // LANES):
            st_send[side, g : g + 1, :] = to_line(level[g * LANES : (g + 1) * LANES])
        st_copies[side].start()

    send_partial(0)
    for slot in (top - 1, top + 1):
        last_unit(kbuf.at[slot], vbuf.at[slot], slot)
    prepare((-1, 1), (1, 1))
    key_wait(top, 1)
    value_wait(top, 1)
    pl.when(y_hi == 1)(lambda: third_unit(far))
    send_partial(1)
    unit(q_ref, acc_own, max_own, half, blocks)
    last_unit(kbuf.at[top], vbuf.at[top], top)
    steps(wo_b)
    prepare((2, 0), (2, 1))
    hid_acc[...] = res_all[tp].astype(F32)
    sides = (pl.ds(0, half), pl.ds(half, half))
    att_tails = tail_copies(att_all.at[tp], att_all, 7)

    def join(side):
        mean_own, level_own = settle(acc_own, max_own, side)
        st_copies[side].wait_recv()
        o_copies[side].wait_recv()
        for g in range(half // LANES):
            inner = slice(g * LANES, (g + 1) * LANES)
            at = slice(side * half + g * LANES, side * half + (g + 1) * LANES)
            level_other = to_column(st_recv[side, g : g + 1, :])
            here = level_own[inner, :]
            most = jnp.maximum(here, level_other)
            w_own = jnp.exp2(here - most)
            w_other = jnp.exp2(level_other - most)
            joined = (w_own * mean_own[inner, :] + w_other * o_recv[at, :].astype(F32)) / (
                w_own + w_other
            )
            att_all[tp, at, :] = joined.astype(BF16)

    def project(at):

        def apply(chip):
            left_side = jnp.concatenate(
                [att_all[2 * chip, at, :], att_all[2 * chip + 1, at, :]], axis=1
            )
            deep = chip_rows(chip)
            weight = jnp.concatenate([wo_all[deep, own_cols], joint[deep, :]], axis=1)
            product = jnp.dot(left_side, weight, preferred_element_type=F32)
            hid_acc[at, :] += product[:, :LANES]
            str_acc[at, :] += product[:, LANES:]

        return apply

    def square_copy(side, step):
        peer = lax.rem(tp + step, n_tp)
        ref = sq_all.at[tp, side]
        return remote(ref, ref, w_send.at[side, step], w_recv.at[side, step], {"tp": peer})

    def square_each(side, act):
        def one(step, carry):
            act(square_copy(side, step))
            return carry

        lax.fori_loop(1, n_tp, one, 0)

    lines_used = half // LANES

    def finish_hidden(side):
        sq_all[tp, side] = jnp.zeros((8, LANES), F32)

        def squares(first, count, line):
            hidden = hid_acc[first : first + count, :].astype(BF16)
            if first < rows:
                hid_ref[first : first + count, :] = hidden
            wide = hidden.astype(F32)
            sq_all[tp, side, line : line + 1, :] = to_line(
                jnp.sum(wide * wide, axis=1, keepdims=True)
            )

        for g in range(lines_used):
            squares(side * half + g * LANES, LANES, g)
        if side:
            squares(rows, 2 * edge, lines_used)
        square_each(side, lambda copy: copy.start())

    def finish_streams(side):
        square_each(side, lambda copy: copy.wait_recv())
        lines = jnp.sum(sq_all[:, side], axis=0)

        def streams(first, count, line):
            mean_square = to_column(lines[line : line + 1, :], count) / (n_tp * LANES)
            scaled = str_acc[first : first + count, :] * lax.rsqrt(mean_square + 1e-6)
            return scaled.astype(BF16).astype(F32)

        for g in range(lines_used):
            at = slice(RIM + g * LANES, RIM + (g + 1) * LANES)
            ext[side, at, :] = streams(side * half + g * LANES, LANES, g)
        if side:
            outside = streams(rows, 2 * edge, lines_used)
            ext[0, :RIM, :] = jnp.where(dev == 0, 0.0, outside[RIM:edge])
            ext[1, :RIM, :] = jnp.where(
                dev == n_ctx - 1, ext[0, half : half + RIM, :], outside[edge + RIM :]
            )

    out_a = gather(0, 0, att_place, half, project(sides[0]))
    out_b = gather(0, 1, att_place, half, project(sides[1]))
    join(0)
    next(out_a)
    att_tails[0].start()
    join(1)
    next(out_b)
    att_tails[1].start()
    steps(out_a, out_a, out_b)
    for copy in att_tails:
        copy.wait_recv()
    spread_each(1, att_all, lambda copy: copy.start())
    steps(out_b, out_a, out_a, out_a, out_b, out_a, out_b, out_a)
    finish_hidden(0)
    spread_each(1, att_all, lambda copy: copy.wait_recv())
    project_rim = project(rim)
    for chip in range(n_tp // 2):
        project_rim(chip)
    steps(out_b, out_b)
    finish_hidden(1)

    lane_group = lax.broadcasted_iota(jnp.int32, (FILTER_TAPS, LANES), 1) // GROUP
    filt = jnp.zeros((FILTER_TAPS, LANES), F32)
    for g in range(LANES // GROUP):
        filt = jnp.where(lane_group == g, filt_ref[:, g : g + 1], filt)

    def convolve(side, low, high):
        count = high - low
        span = count + FILTER_TAPS - 1

        def featured(stream, first, number):
            cols = slice(stream * LANES, (stream + 1) * LANES)
            total = None
            for j in range(FEAT_TAPS):
                row = first + RIM - j
                term = taps_ref[j, stream : stream + 1, :] * ext[side, row : row + number, cols]
                total = term if total is None else total + term
            return total

        first = low - (FILTER_TAPS - 1)
        mix[0:span, :] = featured(0, first, span) * featured(2, first, span)
        response = None
        for j in range(FILTER_TAPS):
            row = FILTER_TAPS - 1 - j
            term = filt[j : j + 1, :] * mix[row : row + count, :]
            response = term if response is None else response + term
        out = featured(1, low, count) * response
        gated_ref[side * half + low : side * half + high, :] = out.astype(BF16)

    finish_streams(0)
    convolve(0, edge, half)
    finish_streams(1)
    convolve(0, 0, edge)
    convolve(1, 0, half)
    def drain(slot, carry):
        for side in range(2):
            key_copy(part_of(k_hbm, side), slot, side, right).wait_send()
            value_copy(part_of(v_hbm, side), slot, side, right).wait_send()
        return carry

    lax.fori_loop(1, ring, drain, 0)

    for side in range(2):
        square_each(side, lambda copy: copy.wait_send())
    spread_each(0, res_all, lambda copy: copy.wait_send())
    spread_each(1, att_all, lambda copy: copy.wait_send())
    for copy in [q_copy] + st_copies + o_copies + res_tails + att_tails:
        copy.wait_send()
    for move in moves:
        move().wait_send()


def local(queries, keys, values, residual, out_proj, norm_gain, in_proj, feat_taps, long_filter):
    rows, width = queries.shape
    half = rows // 2
    n_tp = lax.axis_size("tp")
    ring = lax.axis_size("ctx") // 2
    vmem = pl.BlockSpec(memory_space=pltpu.VMEM)
    hbm = pl.BlockSpec(memory_space=pltpu.HBM)
    dma = pltpu.SemaphoreType.DMA
    shape = jax.ShapeDtypeStruct((rows, width), BF16)
    return pl.pallas_call(
        functools.partial(kernel, ring),
        out_shape=(shape, shape),
        in_specs=[hbm] * 9,
        out_specs=(vmem, vmem),
        scratch_shapes=[
            pltpu.VMEM((rows, width), BF16),
            pltpu.VMEM((rows, width), BF16),
            pltpu.VMEM((rows, width), BF16),
            pltpu.VMEM((n_tp, LANES), F32),
            pltpu.VMEM((FEAT_TAPS, 3, LANES), F32),
            pltpu.VMEM((FILTER_TAPS, LANES // GROUP), F32),
            pltpu.VMEM((ring, rows, width), BF16),
            pltpu.VMEM((ring, rows, width), BF16),
            pltpu.VMEM((rows, width), BF16),
            pltpu.VMEM((rows, 2 * width), F32),
            pltpu.VMEM((rows, 2 * width), F32),
            pltpu.VMEM((rows, width), F32),
            pltpu.VMEM((rows, width), F32),
            pltpu.VMEM((rows, width), BF16),
            pltpu.VMEM((rows, width), BF16),
            pltpu.VMEM((2, 8, LANES), F32),
            pltpu.VMEM((2, 8, LANES), F32),
            pltpu.VMEM((n_tp * LANES, n_tp * LANES), BF16),
            pltpu.VMEM((n_tp * LANES, 3 * LANES), BF16),
            pltpu.VMEM((n_tp * LANES, 3 * LANES), BF16),
            pltpu.VMEM((n_tp, rows + 4 * RIM, width), BF16),
            pltpu.VMEM((n_tp, rows + 4 * RIM, width), BF16),
            pltpu.VMEM((rows + 4 * RIM, LANES), F32),
            pltpu.VMEM((rows + 4 * RIM, 3 * LANES), F32),
            pltpu.VMEM((n_tp, 2, 8, LANES), F32),
            pltpu.VMEM((2, RIM + half, 3 * LANES), F32),
            pltpu.VMEM((RIM + half, LANES), F32),
            dma((11,)),
            dma((ring, 2)),
            dma((ring, 2)),
            dma((ring, 2)),
            dma((ring, 2)),
            dma((9,)),
            dma((9,)),
            dma((2, n_tp)),
            dma((2, n_tp)),
            dma((2, n_tp)),
            dma((2, n_tp)),
            dma((3, 2, 17)),
            dma((3, 2, 17)),
        ],
        compiler_params=pltpu.CompilerParams(
            collective_id=0, has_side_effects=True, vmem_limit_bytes=40 * 1024 * 1024
        ),
        cost_estimate=pl.CostEstimate(
            flops=4 * 10**9, bytes_accessed=4 * 10**6, transcendentals=5 * 10**6
        ),
    )(
        *(
            pltpu.with_memory_space_constraint(operand, pltpu.HBM)
            for operand in (
                queries,
                keys,
                values,
                residual,
                out_proj,
                norm_gain.reshape(n_tp, LANES),
                jnp.transpose(in_proj, (1, 0, 2)),
                feat_taps,
                long_filter,
            )
        )
    )


def solution(mesh):
    return jax.shard_map(
        local,
        mesh=mesh,
        in_specs=(
            P("ctx", "tp"),
            P("ctx", "tp"),
            P("ctx", "tp"),
            P("ctx", "tp"),
            P("tp", None),
            P(),
            P(None, None, "tp"),
            P(None, None, "tp"),
            P(None, "tp"),
        ),
        out_specs=(P("ctx", "tp"), P("ctx", "tp")),
        check_vma=False,
    )
```

```python
import functools

import jax
import jax.numpy as jnp
from jax import lax
from jax.experimental import pallas as pl
from jax.experimental.pallas import tpu as pltpu
from jax.sharding import PartitionSpec as P

MESH = pl.DeviceIdType.MESH
LANES = 128
GROUP = 16
FEAT_TAPS = 3
FILTER_TAPS = 7
RIM = 8
LOW = -1e30
LOG2E = 1.4426950408889634
F32 = jnp.float32
BF16 = jnp.bfloat16


def kernel(
    ring,
    q_hbm,
    k_hbm,
    v_hbm,
    res_hbm,
    outp_hbm,
    gain_hbm,
    inp_hbm,
    taps_hbm,
    filt_hbm,
    hid_ref,
    gated_ref,
    q_ref,
    k_ref,
    v_ref,
    gain_ref,
    taps_ref,
    filt_ref,
    kbuf,
    vbuf,
    vt_own,
    qt_own,
    qt_par,
    qpar,
    acc_own,
    acc_par,
    max_own,
    max_par,
    o_send,
    o_recv,
    st_send,
    st_recv,
    wo_all,
    win,
    joint,
    att_all,
    res_all,
    hid_acc,
    str_acc,
    sq_all,
    ext,
    mix,
    in_sem,
    ks_sem,
    kr_sem,
    vs_sem,
    vr_sem,
    x_send,
    x_recv,
    w_send,
    w_recv,
    h_send,
    h_recv,
    g_send,
    g_recv,
):
    rows, width = q_ref.shape
    half = rows // 2
    edge = 2 * RIM
    rim = pl.ds(rows, 2 * edge)
    top = ring // 2
    n_ctx = 2 * ring
    n_tp = att_all.shape[0]
    n_x = n_tp // 4
    dev = lax.axis_index("ctx")
    y_hi = dev // ring
    z = lax.rem(dev, ring)
    tp = lax.axis_index("tp")
    x = tp // 4
    y_lo = lax.rem(tp, 4) // 2
    core = lax.rem(tp, 2)
    scale = LOG2E * width**-0.5

    def ctx_id(y_at, z_at):
        return {"ctx": y_at * ring + z_at}

    right = ctx_id(y_hi, lax.rem(z + 1, ring))
    left = ctx_id(y_hi, lax.rem(z + ring - 1, ring))
    across = ctx_id(1 - y_hi, z)
    after = {"ctx": lax.rem(dev + 1, n_ctx)}
    before = {"ctx": lax.rem(dev + n_ctx - 1, n_ctx)}

    def tp_at(dx, dy, dc):
        return (
            lax.rem(x + dx + n_x, n_x) * 4
            + (1 - y_lo if dy else y_lo) * 2
            + (1 - core if dc else core)
        )

    barrier = pltpu.get_barrier_semaphore()
    for other in (right, left, across, after, before):
        pl.semaphore_signal(barrier, inc=1, device_id=other, device_id_type=MESH)

    def greet(step, carry):
        peer = lax.rem(tp + step, n_tp)
        pl.semaphore_signal(barrier, inc=1, device_id={"tp": peer}, device_id_type=MESH)
        return carry

    lax.fori_loop(1, n_tp, greet, 0)

    own_cols = pl.ds(pl.multiple_of(tp * LANES, LANES), LANES)

    def head_rows(head, first=0, count=LANES):
        return pl.ds(pl.multiple_of(head * LANES + first, count), count)

    loads = []
    for src, dst in [
        (q_hbm, q_ref),
        (k_hbm, k_ref),
        (v_hbm, v_ref),
        (res_hbm, res_all.at[tp, pl.ds(0, rows), :]),
        (outp_hbm, wo_all.at[head_rows(tp), :]),
        (gain_hbm, gain_ref),
        (taps_hbm, taps_ref),
        (filt_hbm, filt_ref),
    ] + [(inp_hbm.at[s], win.at[:, s * LANES : (s + 1) * LANES]) for s in range(3)]:
        load = pltpu.make_async_copy(src, dst, in_sem.at[len(loads)])
        load.start()
        loads.append(load)

    for acc, top_ref in ((acc_own, max_own), (acc_par, max_par)):
        acc[...] = jnp.zeros_like(acc)
        top_ref[...] = jnp.full(top_ref.shape, LOW, F32)
    pl.semaphore_wait(barrier, n_tp - 1 + 5)

    def remote(src, dst, send, recv, to):
        return pltpu.make_async_remote_copy(
            src_ref=src, dst_ref=dst, send_sem=send, recv_sem=recv, device_id=to, device_id_type=MESH
        )

    def part_of(ref, side):
        return ref.at[pl.ds(side * half, half), :]

    def key_copy(src, slot, side, to):
        dst = part_of(kbuf.at[slot], side)
        return remote(src, dst, ks_sem.at[slot, side], kr_sem.at[slot, side], to)

    def value_copy(src, slot, side, to):
        return remote(
            src, vbuf.at[slot, side], vs_sem.at[slot, side], vr_sem.at[slot, side], to
        )

    def turned(ref, side):
        return ref[side * half : (side + 1) * half, :].astype(F32).T.astype(BF16)

    q_copy = remote(q_hbm, qpar, x_send.at[0], x_recv.at[0], across)
    for side in range(2):
        for to, slot in ((right, 1), (left, ring - 1)):
            key_copy(part_of(k_hbm, side), slot, side, to).start()
        if side == 0:
            q_copy.start()
            loads[2].wait()
        vt_own[side] = turned(v_ref, side)
        for to, slot in ((right, 1), (left, ring - 1)):
            value_copy(vt_own.at[side], slot, side, to).start()

    def tail_copies(src, dst, first_sem):
        return [
            remote(
                src.at[pl.ds((side + 1) * half - edge, edge), :],
                dst.at[tp, pl.ds(rows + side * edge, edge), :],
                x_send.at[first_sem + side],
                x_recv.at[first_sem + side],
                to,
            )
            for side, to in enumerate((after, before))
        ]

    res_tails = tail_copies(res_hbm, res_all, 5)
    for copy in res_tails:
        copy.start()

    def spread_each(which, buf, act):
        def one(step, carry):
            ref = buf.at[tp, rim, :]
            peer = lax.rem(tp + step, n_tp)
            act(remote(ref, ref, h_send.at[which, step], h_recv.at[which, step], {"tp": peer}))
            return carry

        lax.fori_loop(1, n_tp, one, 0)

    targets = {
        "y": {"tp": tp_at(0, 1, 0)},
        "xp": {"tp": tp_at(1, 0, 0)},
        "xm": {"tp": tp_at(-1, 0, 0)},
        "c": {"tp": tp_at(0, 0, 1)},
    }
    moves = []

    def gather(which, side, place, span, consume):
        whole = (side * span, span)
        head = (side * span, span // 2)
        tail = (side * span + span // 2, span // 2)
        known = {}

        def copy_of(dx, dy, dc, part, number, to):
            ref = place(tp_at(dx, dy, dc), *part)
            return remote(
                ref, ref, g_send.at[which, side, number], g_recv.at[which, side, number], targets[to]
            )

        def go(dx, dy, to, part=whole):
            number = len(known)
            known[dx, dy, to] = (number, part)
            copy_of(dx, dy, 0, part, number, to).start()
            moves.append(lambda: copy_of(dx, dy, 0, part, number, to))

        def come(dx, dy, to):
            number, part = known[dx, dy, to]
            sx = dx + {"xp": -1, "xm": 1}.get(to, 0)
            sy = 1 - dy if to == "y" else dy
            copy_of(sx, sy, 1 if to == "c" else 0, part, number, to).wait_recv()

        def pair(dx, dy):
            come(dx, dy, "c")
            consume(tp_at(dx, dy, 0) // 2)

        def relay(dx, dy):
            go(dx, dy, "xp" if dx < 0 else "xm", head if dx < 0 else tail)

        def y_first():
            for to in ("y", "xp", "xm", "c"):
                go(0, 0, to)
            yield
            come(0, 0, "y")
            for to in ("xp", "xm", "c"):
                go(0, 1, to)
            pair(0, 0)
            yield
            for dx, to in ((-1, "xp"), (1, "xm")):
                come(0, 0, to)
                relay(dx, 0)
                go(dx, 0, "c")
            yield
            pair(0, 1)
            for dx, to in ((-1, "xp"), (1, "xm")):
                come(0, 1, to)
                relay(dx, 1)
                go(dx, 1, "c")
            yield
            pair(-1, 0)
            pair(1, 0)
            yield
            come(-1, 0, "xp")
            come(1, 0, "xm")
            go(2, 0, "c")
            pair(-1, 1)
            pair(1, 1)
            yield
            come(-1, 1, "xp")
            come(1, 1, "xm")
            go(2, 1, "c")
            pair(2, 0)
            yield
            pair(2, 1)
            yield

        def x_first():
            for to in ("xp", "xm", "y", "c"):
                go(0, 0, to)
            yield
            pair(0, 0)
            for dx, to in ((-1, "xp"), (1, "xm")):
                come(0, 0, to)
                relay(dx, 0)
                go(dx, 0, "y")
                go(dx, 0, "c")
            yield
            come(0, 0, "y")
            go(0, 1, "c")
            pair(-1, 0)
            pair(1, 0)
            yield
            come(-1, 0, "xp")
            come(1, 0, "xm")
            go(2, 0, "y")
            go(2, 0, "c")
            come(-1, 0, "y")
            go(-1, 1, "c")
            come(1, 0, "y")
            go(1, 1, "c")
            yield
            pair(0, 1)
            pair(2, 0)
            yield
            come(2, 0, "y")
            go(2, 1, "c")
            pair(-1, 1)
            pair(1, 1)
            yield
            pair(2, 1)
            yield

        return x_first() if side else y_first()

    ones = jnp.ones((16, half), BF16)
    tri = lax.broadcasted_iota(jnp.int32, (half, half), 0) <= lax.broadcasted_iota(
        jnp.int32, (half, half), 1
    )

    def unit(queries, acc, top_ref, side, blocks, masked=False):
        these = queries[side]
        scores = [jnp.dot(keys, these, preferred_element_type=F32) for keys, _ in blocks]
        if masked:
            scores = [jnp.where(tri, block, LOW) for block in scores]
        old = top_ref[side, 0:1, :]
        best = functools.reduce(jnp.maximum, scores)
        new = jnp.maximum(old, jnp.max(best, axis=0, keepdims=True))
        top_ref[side, 0:1, :] = new
        total = acc[side] * jnp.exp2((old - new) * scale)
        for block, (_, values) in zip(scores, blocks):
            weights = jnp.exp2((block - new) * scale).astype(BF16)
            total = total + jnp.dot(
                jnp.concatenate([values, ones], axis=0), weights, preferred_element_type=F32
            )
        acc[side] = total

    def own_block(side):
        return (k_ref[side * half : (side + 1) * half, :], vt_own[side])

    def block_at(slot, side):
        return (kbuf[slot, pl.ds(pl.multiple_of(side * half, half), half), :], vbuf[slot, side])

    def third_unit(slots):
        unit(qt_par, acc_par, max_par, y_hi, [block_at(slot, y_hi) for slot in slots])

    def last_unit(slot):
        side = jnp.where(slot <= z, 0, 1)
        unit(qt_own, acc_own, max_own, side, [block_at(slot, side)])

    def early(slots):
        blocks = [block_at(slot, 0) for slot in slots]
        unit(qt_par, acc_par, max_par, 1, blocks)
        unit(qt_own, acc_own, max_own, 1, blocks)

    def late(slots):
        third_unit(slots)
        for slot in slots:
            last_unit(slot)

    for load in loads[:2] + loads[3:5]:
        load.wait()

    def res_place(chunk, first, count):
        return res_all.at[chunk, pl.ds(first, count), :]

    def wo_place(chunk, first, count):
        return wo_all.at[head_rows(chunk, first, count), :]

    def att_place(chunk, first, count):
        return att_all.at[chunk, pl.ds(first, count), :]

    def nothing(chip):
        pass

    res_a = gather(1, 0, res_place, half, nothing)
    res_b = gather(1, 1, res_place, half, nothing)
    wo_a = gather(2, 0, wo_place, LANES // 2, nothing)
    wo_b = gather(2, 1, wo_place, LANES // 2, nothing)
    for stages in (res_a, res_b, wo_a, wo_b):
        next(stages)
    for load in loads[5:]:
        load.wait()
    str_acc[...] = jnp.zeros_like(str_acc)
    diagonal = lax.broadcasted_iota(jnp.int32, (LANES, LANES), 0) == lax.broadcasted_iota(
        jnp.int32, (LANES, LANES), 1
    )

    def to_column(line, count=LANES):
        return jnp.sum(jnp.where(diagonal[:count], line, 0.0), axis=1, keepdims=True)

    def to_line(column):
        picked = jnp.where(diagonal[: column.shape[0]], column, 0.0)
        return jnp.sum(picked, axis=0, keepdims=True)

    def scale_win():
        def block(head, carry):
            at = head_rows(head)
            column = to_column(gain_ref[pl.ds(head, 1), :])
            win[at, :] = (win[at, :].astype(F32) * column).astype(BF16)
            return carry

        lax.fori_loop(0, n_tp, block, 0)

    def chip_rows(chip):
        return pl.ds(pl.multiple_of(chip * 2 * LANES, 2 * LANES), 2 * LANES)

    def prepare(*offsets):
        for dx, dy in offsets:
            chip = tp_at(dx, dy, 0) // 2
            deep = chip_rows(chip)
            joint[deep, :] = jnp.dot(
                wo_all[deep, :], win[...], preferred_element_type=F32
            ).astype(BF16)
            left_side = jnp.concatenate([res_all[2 * chip], res_all[2 * chip + 1]], axis=1)
            str_acc[...] += jnp.dot(left_side, win[deep, :], preferred_element_type=F32)

    def steps(*names):
        for stages in names:
            next(stages)

    plan = {
        1: ((res_a, res_a, res_b), ()),
        2: ((wo_a, wo_a, wo_b, res_a, res_a, res_b), ()),
        3: ((res_a, res_b), ()),
        4: ((wo_b, wo_a, wo_a, res_a, res_b), ()),
        5: ((wo_a, wo_b, res_a, res_b), ()),
        6: ((wo_a, wo_b, res_b), ((0, 0), (0, 1))),
        7: ((wo_a, wo_b), ((-1, 0), (1, 0))),
    }

    def share_residual_rim():
        for copy in res_tails:
            copy.wait_recv()
        spread_each(0, res_all, lambda copy: copy.start())

    def extra(number):
        names, offsets = plan[number]
        steps(*names)
        prepare(*offsets)
        if number == 2:
            share_residual_rim()
        if number == 3:
            scale_win()
        if number == 5:
            spread_each(0, res_all, lambda copy: copy.wait_recv())
    for side in range(2):
        qt_own[side] = turned(q_ref, side)
    unit(qt_own, acc_own, max_own, 0, [own_block(0)], True)
    unit(qt_own, acc_own, max_own, 1, [own_block(1)], True)
    unit(qt_own, acc_own, max_own, 1, [own_block(0)])

    def key_wait(slot, side):
        key_copy(part_of(k_hbm, side), slot, side, right).wait_recv()

    def value_wait(slot, side):
        value_copy(vt_own.at[side], slot, side, right).wait_recv()

    def when(condition, act):
        if isinstance(condition, bool):
            if condition:
                act()
        else:
            pl.when(condition)(act)

    def pass_keys(step, side):
        back = ring - step
        key_wait(step, side)
        key_copy(part_of(kbuf.at[step], side), step + 1, side, right).start()
        key_wait(back, side)
        when(
            step < top - 1,
            lambda: key_copy(part_of(kbuf.at[back], side), back - 1, side, left).start(),
        )

    def pass_values(step, side):
        back = ring - step
        value_wait(step, side)
        when(
            step < top - 1,
            lambda: value_copy(vbuf.at[step, side], step + 1, side, right).start(),
        )
        value_wait(back, side)
        value_copy(vbuf.at[back, side], back - 1, side, left).start()

    def meet_partner():
        q_copy.wait_recv()
        for side in range(2):
            qt_par[side] = turned(qpar, side)
        unit(qt_par, acc_par, max_par, 1, [own_block(0)])
        pl.when(y_hi == 0)(lambda: unit(qt_par, acc_par, max_par, 0, [own_block(0)]))
        pl.when(y_hi == 1)(lambda: unit(qt_par, acc_par, max_par, 1, [own_block(1)]))

    def turn(step, carry):
        back = ring - step
        pass_keys(step, 0)
        pl.when(step > 1)(lambda: pass_keys(step - 1, 1))
        pl.when(step > 2)(lambda: late((step - 2, back + 2)))
        pl.when(step == 1)(meet_partner)
        pass_values(step, 0)
        pl.when(step > 1)(lambda: pass_values(step - 1, 1))
        early((step, back))
        for number in range(1, top):
            pl.when(step == number)(functools.partial(extra, number))
        return carry

    lax.fori_loop(1, top, turn, 0)
    for number in range(top, 8):
        extra(number)
    key_wait(top, 0)
    pass_keys(top - 1, 1)
    if top > 2:
        late((top - 2, top + 2))
    value_wait(top, 0)
    pass_values(top - 1, 1)
    far = (top - 1, top + 1, top)
    unit(qt_par, acc_par, max_par, 1, [block_at(top, 0)])
    pl.when(y_hi == 0)(lambda: third_unit(far))

    def settle(acc, top_ref, side):
        total = acc[side, width : width + 1, :]
        seen = total > 0.0
        held = jnp.where(seen, total, 1.0)
        level = jnp.where(seen, top_ref[side, 0:1, :] * scale + jnp.log2(held), LOW)
        return acc[side, :width, :] * (1.0 / held), level

    st_copies = [
        remote(st_send.at[n], st_recv.at[n], x_send.at[1 + n], x_recv.at[1 + n], across)
        for n in range(2)
    ]
    o_copies = [
        remote(o_send.at[n], o_recv.at[n], x_send.at[3 + n], x_recv.at[3 + n], across)
        for n in range(2)
    ]

    def send_partial(side):
        mean, level = settle(acc_par, max_par, side)
        o_send[side] = mean.astype(BF16)
        o_copies[side].start()
        st_send[side] = jnp.broadcast_to(level, (8, half))
        st_copies[side].start()

    send_partial(0)
    for slot in (top - 1, top + 1):
        last_unit(slot)
    prepare((-1, 1), (1, 1))
    key_wait(top, 1)
    value_wait(top, 1)
    pl.when(y_hi == 1)(lambda: third_unit(far))
    send_partial(1)
    unit(qt_own, acc_own, max_own, 1, [block_at(top, 0)])
    last_unit(top)
    steps(wo_b)
    prepare((2, 0), (2, 1))
    hid_acc[...] = res_all[tp].astype(F32)
    sides = (pl.ds(0, half), pl.ds(half, half))
    att_tails = tail_copies(att_all.at[tp], att_all, 7)

    def join(side):
        mean_own, level_own = settle(acc_own, max_own, side)
        st_copies[side].wait_recv()
        o_copies[side].wait_recv()
        level_other = st_recv[side, 0:1, :]
        most = jnp.maximum(level_own, level_other)
        w_own = jnp.exp2(level_own - most)
        w_other = jnp.exp2(level_other - most)
        share = 1.0 / (w_own + w_other)
        joined = mean_own * (w_own * share) + o_recv[side].astype(F32) * (w_other * share)
        att_all[tp, side * half : (side + 1) * half, :] = joined.T.astype(BF16)

    def project(at):

        def apply(chip):
            left_side = jnp.concatenate(
                [att_all[2 * chip, at, :], att_all[2 * chip + 1, at, :]], axis=1
            )
            deep = chip_rows(chip)
            weight = jnp.concatenate([wo_all[deep, own_cols], joint[deep, :]], axis=1)
            product = jnp.dot(left_side, weight, preferred_element_type=F32)
            hid_acc[at, :] += product[:, :LANES]
            str_acc[at, :] += product[:, LANES:]

        return apply

    def square_copy(side, step):
        peer = lax.rem(tp + step, n_tp)
        ref = sq_all.at[tp, side]
        return remote(ref, ref, w_send.at[side, step], w_recv.at[side, step], {"tp": peer})

    def square_each(side, act):
        def one(step, carry):
            act(square_copy(side, step))
            return carry

        lax.fori_loop(1, n_tp, one, 0)

    lines_used = half // LANES

    def finish_hidden(side):
        sq_all[tp, side] = jnp.zeros((8, LANES), F32)

        def squares(first, count, line):
            hidden = hid_acc[first : first + count, :].astype(BF16)
            if first < rows:
                hid_ref[first : first + count, :] = hidden
            wide = hidden.astype(F32)
            sq_all[tp, side, line : line + 1, :] = to_line(
                jnp.sum(wide * wide, axis=1, keepdims=True)
            )

        for g in range(lines_used):
            squares(side * half + g * LANES, LANES, g)
        if side:
            squares(rows, 2 * edge, lines_used)
        square_each(side, lambda copy: copy.start())

    def finish_streams(side):
        square_each(side, lambda copy: copy.wait_recv())
        lines = jnp.sum(sq_all[:, side], axis=0)

        def streams(first, count, line):
            mean_square = to_column(lines[line : line + 1, :], count) / (n_tp * LANES)
            scaled = str_acc[first : first + count, :] * lax.rsqrt(mean_square + 1e-6)
            return scaled.astype(BF16).astype(F32)

        for g in range(lines_used):
            at = slice(RIM + g * LANES, RIM + (g + 1) * LANES)
            ext[side, at, :] = streams(side * half + g * LANES, LANES, g)
        if side:
            outside = streams(rows, 2 * edge, lines_used)
            ext[0, :RIM, :] = jnp.where(dev == 0, 0.0, outside[RIM:edge])
            ext[1, :RIM, :] = jnp.where(
                dev == n_ctx - 1, ext[0, half : half + RIM, :], outside[edge + RIM :]
            )

    out_a = gather(0, 0, att_place, half, project(sides[0]))
    out_b = gather(0, 1, att_place, half, project(sides[1]))
    join(0)
    next(out_a)
    att_tails[0].start()
    join(1)
    next(out_b)
    att_tails[1].start()
    steps(out_a, out_a, out_b)
    for copy in att_tails:
        copy.wait_recv()
    spread_each(1, att_all, lambda copy: copy.start())
    steps(out_b, out_a, out_a, out_a, out_b, out_a, out_b, out_a)
    finish_hidden(0)
    spread_each(1, att_all, lambda copy: copy.wait_recv())
    project_rim = project(rim)
    for chip in range(n_tp // 2):
        project_rim(chip)
    steps(out_b, out_b)
    finish_hidden(1)

    lane_group = lax.broadcasted_iota(jnp.int32, (FILTER_TAPS, LANES), 1) // GROUP
    filt = jnp.zeros((FILTER_TAPS, LANES), F32)
    for g in range(LANES // GROUP):
        filt = jnp.where(lane_group == g, filt_ref[:, g : g + 1], filt)

    def convolve(side, low, high):
        count = high - low
        span = count + FILTER_TAPS - 1

        def featured(stream, first, number):
            cols = slice(stream * LANES, (stream + 1) * LANES)
            total = None
            for j in range(FEAT_TAPS):
                row = first + RIM - j
                term = taps_ref[j, stream : stream + 1, :] * ext[side, row : row + number, cols]
                total = term if total is None else total + term
            return total

        first = low - (FILTER_TAPS - 1)
        mix[0:span, :] = featured(0, first, span) * featured(2, first, span)
        response = None
        for j in range(FILTER_TAPS):
            row = FILTER_TAPS - 1 - j
            term = filt[j : j + 1, :] * mix[row : row + count, :]
            response = term if response is None else response + term
        out = featured(1, low, count) * response
        gated_ref[side * half + low : side * half + high, :] = out.astype(BF16)

    finish_streams(0)
    convolve(0, edge, half)
    finish_streams(1)
    convolve(0, 0, edge)
    convolve(1, 0, half)
    def drain(slot, carry):
        for side in range(2):
            key_copy(part_of(k_hbm, side), slot, side, right).wait_send()
            value_copy(part_of(v_hbm, side), slot, side, right).wait_send()
        return carry

    lax.fori_loop(1, ring, drain, 0)

    for side in range(2):
        square_each(side, lambda copy: copy.wait_send())
    spread_each(0, res_all, lambda copy: copy.wait_send())
    spread_each(1, att_all, lambda copy: copy.wait_send())
    for copy in [q_copy] + st_copies + o_copies + res_tails + att_tails:
        copy.wait_send()
    for move in moves:
        move().wait_send()


def local(queries, keys, values, residual, out_proj, norm_gain, in_proj, feat_taps, long_filter):
    rows, width = queries.shape
    half = rows // 2
    n_tp = lax.axis_size("tp")
    ring = lax.axis_size("ctx") // 2
    vmem = pl.BlockSpec(memory_space=pltpu.VMEM)
    hbm = pl.BlockSpec(memory_space=pltpu.HBM)
    dma = pltpu.SemaphoreType.DMA
    shape = jax.ShapeDtypeStruct((rows, width), BF16)
    return pl.pallas_call(
        functools.partial(kernel, ring),
        out_shape=(shape, shape),
        in_specs=[hbm] * 9,
        out_specs=(vmem, vmem),
        scratch_shapes=[
            pltpu.VMEM((rows, width), BF16),
            pltpu.VMEM((rows, width), BF16),
            pltpu.VMEM((rows, width), BF16),
            pltpu.VMEM((n_tp, LANES), F32),
            pltpu.VMEM((FEAT_TAPS, 3, LANES), F32),
            pltpu.VMEM((FILTER_TAPS, LANES // GROUP), F32),
            pltpu.VMEM((ring, rows, width), BF16),
            pltpu.VMEM((ring, 2, width, half), BF16),
            pltpu.VMEM((2, width, half), BF16),
            pltpu.VMEM((2, width, half), BF16),
            pltpu.VMEM((2, width, half), BF16),
            pltpu.VMEM((rows, width), BF16),
            pltpu.VMEM((2, width + 16, half), F32),
            pltpu.VMEM((2, width + 16, half), F32),
            pltpu.VMEM((2, 8, half), F32),
            pltpu.VMEM((2, 8, half), F32),
            pltpu.VMEM((2, width, half), BF16),
            pltpu.VMEM((2, width, half), BF16),
            pltpu.VMEM((2, 8, half), F32),
            pltpu.VMEM((2, 8, half), F32),
            pltpu.VMEM((n_tp * LANES, n_tp * LANES), BF16),
            pltpu.VMEM((n_tp * LANES, 3 * LANES), BF16),
            pltpu.VMEM((n_tp * LANES, 3 * LANES), BF16),
            pltpu.VMEM((n_tp, rows + 4 * RIM, width), BF16),
            pltpu.VMEM((n_tp, rows + 4 * RIM, width), BF16),
            pltpu.VMEM((rows + 4 * RIM, LANES), F32),
            pltpu.VMEM((rows + 4 * RIM, 3 * LANES), F32),
            pltpu.VMEM((n_tp, 2, 8, LANES), F32),
            pltpu.VMEM((2, RIM + half, 3 * LANES), F32),
            pltpu.VMEM((RIM + half, LANES), F32),
            dma((11,)),
            dma((ring, 2)),
            dma((ring, 2)),
            dma((ring, 2)),
            dma((ring, 2)),
            dma((9,)),
            dma((9,)),
            dma((2, n_tp)),
            dma((2, n_tp)),
            dma((2, n_tp)),
            dma((2, n_tp)),
            dma((3, 2, 17)),
            dma((3, 2, 17)),
        ],
        compiler_params=pltpu.CompilerParams(
            collective_id=0, has_side_effects=True, vmem_limit_bytes=40 * 1024 * 1024
        ),
        cost_estimate=pl.CostEstimate(
            flops=4 * 10**9, bytes_accessed=4 * 10**6, transcendentals=5 * 10**6
        ),
    )(
        *(
            pltpu.with_memory_space_constraint(operand, pltpu.HBM)
            for operand in (
                queries,
                keys,
                values,
                residual,
                out_proj,
                norm_gain.reshape(n_tp, LANES),
                jnp.transpose(in_proj, (1, 0, 2)),
                feat_taps,
                long_filter,
            )
        )
    )


def solution(mesh):
    return jax.shard_map(
        local,
        mesh=mesh,
        in_specs=(
            P("ctx", "tp"),
            P("ctx", "tp"),
            P("ctx", "tp"),
            P("ctx", "tp"),
            P("tp", None),
            P(),
            P(None, None, "tp"),
            P(None, None, "tp"),
            P(None, "tp"),
        ),
        out_specs=(P("ctx", "tp"), P("ctx", "tp")),
        check_vma=False,
    )
```

```python
import functools

import jax
import jax.numpy as jnp
from jax import lax
from jax.experimental import pallas as pl
from jax.experimental.pallas import tpu as pltpu
from jax.sharding import PartitionSpec as P

MESH = pl.DeviceIdType.MESH
LANES = 128
GROUP = 16
FEAT_TAPS = 3
FILTER_TAPS = 7
RIM = 8
LOW = -1e30
LOG2E = 1.4426950408889634
F32 = jnp.float32
BF16 = jnp.bfloat16


def kernel(
    ring,
    q_hbm,
    k_hbm,
    v_hbm,
    res_hbm,
    outp_hbm,
    gain_hbm,
    inp_hbm,
    taps_hbm,
    filt_hbm,
    hid_ref,
    gated_ref,
    q_ref,
    k_ref,
    v_ref,
    gain_ref,
    taps_ref,
    filt_ref,
    kbuf,
    vbuf,
    vt_own,
    qt_own,
    qt_par,
    qpar,
    acc_own,
    acc_par,
    max_own,
    max_par,
    o_send,
    o_recv,
    st_send,
    st_recv,
    wo_all,
    win,
    joint,
    att_all,
    res_all,
    hid_acc,
    str_acc,
    sq_all,
    ext,
    mix,
    in_sem,
    ks_sem,
    kr_sem,
    vs_sem,
    vr_sem,
    x_send,
    x_recv,
    w_send,
    w_recv,
    h_send,
    h_recv,
    g_send,
    g_recv,
):
    rows, width = q_ref.shape
    half = rows // 2
    edge = 2 * RIM
    rim = pl.ds(rows, 2 * edge)
    top = ring // 2
    n_ctx = 2 * ring
    n_tp = att_all.shape[0]
    n_x = n_tp // 4
    dev = lax.axis_index("ctx")
    y_hi = dev // ring
    z = lax.rem(dev, ring)
    tp = lax.axis_index("tp")
    x = tp // 4
    y_lo = lax.rem(tp, 4) // 2
    core = lax.rem(tp, 2)
    scale = LOG2E * width**-0.5

    def ctx_id(y_at, z_at):
        return {"ctx": y_at * ring + z_at}

    right = ctx_id(y_hi, lax.rem(z + 1, ring))
    left = ctx_id(y_hi, lax.rem(z + ring - 1, ring))
    across = ctx_id(1 - y_hi, z)
    beside = {"ctx": (1 - y_hi) * ring + z, "tp": tp + 2 - 4 * y_lo}
    after = {"ctx": lax.rem(dev + 1, n_ctx)}
    before = {"ctx": lax.rem(dev + n_ctx - 1, n_ctx)}

    def tp_at(dx, dy, dc):
        return (
            lax.rem(x + dx + n_x, n_x) * 4
            + (1 - y_lo if dy else y_lo) * 2
            + (1 - core if dc else core)
        )

    barrier = pltpu.get_barrier_semaphore()
    for other in (right, left, across, beside, after, before):
        pl.semaphore_signal(barrier, inc=1, device_id=other, device_id_type=MESH)

    def greet(step, carry):
        peer = lax.rem(tp + step, n_tp)
        pl.semaphore_signal(barrier, inc=1, device_id={"tp": peer}, device_id_type=MESH)
        return carry

    lax.fori_loop(1, n_tp, greet, 0)

    own_cols = pl.ds(pl.multiple_of(tp * LANES, LANES), LANES)

    def head_rows(head, first=0, count=LANES):
        return pl.ds(pl.multiple_of(head * LANES + first, count), count)

    loads = []
    for src, dst in [
        (q_hbm, q_ref),
        (k_hbm, k_ref),
        (v_hbm, v_ref),
        (res_hbm, res_all.at[tp, pl.ds(0, rows), :]),
        (outp_hbm, wo_all.at[head_rows(tp), :]),
        (gain_hbm, gain_ref),
        (taps_hbm, taps_ref),
        (filt_hbm, filt_ref),
    ] + [(inp_hbm.at[s], win.at[:, s * LANES : (s + 1) * LANES]) for s in range(3)]:
        load = pltpu.make_async_copy(src, dst, in_sem.at[len(loads)])
        load.start()
        loads.append(load)

    for acc, top_ref in ((acc_own, max_own), (acc_par, max_par)):
        acc[...] = jnp.zeros_like(acc)
        top_ref[...] = jnp.full(top_ref.shape, LOW, F32)
    pl.semaphore_wait(barrier, n_tp - 1 + 6)

    def remote(src, dst, send, recv, to):
        return pltpu.make_async_remote_copy(
            src_ref=src, dst_ref=dst, send_sem=send, recv_sem=recv, device_id=to, device_id_type=MESH
        )

    def part_of(ref, side):
        return ref.at[pl.ds(side * half, half), :]

    def key_copy(src, slot, side, to):
        dst = part_of(kbuf.at[slot], side)
        return remote(src, dst, ks_sem.at[slot, side], kr_sem.at[slot, side], to)

    def value_copy(src, slot, side, to):
        return remote(
            src, vbuf.at[slot, side], vs_sem.at[slot, side], vr_sem.at[slot, side], to
        )

    def turned(ref, side):
        return ref[side * half : (side + 1) * half, :].astype(F32).T.astype(BF16)

    q_copy = remote(q_hbm, qpar, x_send.at[0], x_recv.at[0], across)
    for side in range(2):
        for to, slot in ((right, 1), (left, ring - 1)):
            key_copy(part_of(k_hbm, side), slot, side, to).start()
        if side == 0:
            q_copy.start()
            loads[2].wait()
        vt_own[side] = turned(v_ref, side)
        for to, slot in ((right, 1), (left, ring - 1)):
            value_copy(vt_own.at[side], slot, side, to).start()

    def tail_copies(src, dst, first_sem):
        return [
            remote(
                src.at[pl.ds((side + 1) * half - edge, edge), :],
                dst.at[tp, pl.ds(rows + side * edge, edge), :],
                x_send.at[first_sem + side],
                x_recv.at[first_sem + side],
                to,
            )
            for side, to in enumerate((after, before))
        ]

    res_tails = tail_copies(res_hbm, res_all, 5)
    for copy in res_tails:
        copy.start()

    def spread_each(which, buf, act):
        def one(step, carry):
            ref = buf.at[tp, rim, :]
            peer = lax.rem(tp + step, n_tp)
            act(remote(ref, ref, h_send.at[which, step], h_recv.at[which, step], {"tp": peer}))
            return carry

        lax.fori_loop(1, n_tp, one, 0)

    targets = {
        "y": {"tp": tp_at(0, 1, 0)},
        "yy": beside,
        "xp": {"tp": tp_at(1, 0, 0)},
        "xm": {"tp": tp_at(-1, 0, 0)},
        "c": {"tp": tp_at(0, 0, 1)},
    }
    moves = []

    def gather(which, side, place, span, consume, twin=False):
        whole = (side * span, span)
        head = (side * span, span // 2)
        tail = (side * span + span // 2, span // 2)
        known = {}

        def copy_of(dx, dy, dc, part, number, to):
            ref = place(tp_at(dx, dy, dc), *part)
            return remote(
                ref, ref, g_send.at[which, side, number], g_recv.at[which, side, number], targets[to]
            )

        def go(dx, dy, to, part=whole):
            if twin and to == "y" and part == whole:
                go(dx, dy, "y", head)
                go(dx, dy, "yy", tail)
                return
            number = len(known)
            known[dx, dy, to] = (number, part)
            copy_of(dx, dy, 0, part, number, to).start()
            moves.append(lambda: copy_of(dx, dy, 0, part, number, to))

        def come(dx, dy, to):
            if twin and to == "y":
                come(dx, dy, "yy")
            number, part = known[dx, dy, to]
            sx = dx + {"xp": -1, "xm": 1}.get(to, 0)
            sy = 1 - dy if to in ("y", "yy") else dy
            copy_of(sx, sy, 1 if to == "c" else 0, part, number, to).wait_recv()

        def pair(dx, dy):
            come(dx, dy, "c")
            consume(tp_at(dx, dy, 0) // 2)

        def relay(dx, dy):
            go(dx, dy, "xp" if dx < 0 else "xm", head if dx < 0 else tail)

        def y_first():
            for to in ("y", "xp", "xm", "c"):
                go(0, 0, to)
            yield
            come(0, 0, "y")
            for to in ("xp", "xm", "c"):
                go(0, 1, to)
            pair(0, 0)
            yield
            for dx, to in ((-1, "xp"), (1, "xm")):
                come(0, 0, to)
                relay(dx, 0)
                go(dx, 0, "c")
            yield
            pair(0, 1)
            for dx, to in ((-1, "xp"), (1, "xm")):
                come(0, 1, to)
                relay(dx, 1)
                go(dx, 1, "c")
            yield
            pair(-1, 0)
            pair(1, 0)
            yield
            come(-1, 0, "xp")
            come(1, 0, "xm")
            go(2, 0, "c")
            pair(-1, 1)
            pair(1, 1)
            yield
            come(-1, 1, "xp")
            come(1, 1, "xm")
            go(2, 1, "c")
            pair(2, 0)
            yield
            pair(2, 1)
            yield

        def x_first():
            for to in ("xp", "xm", "y", "c"):
                go(0, 0, to)
            yield
            pair(0, 0)
            for dx, to in ((-1, "xp"), (1, "xm")):
                come(0, 0, to)
                relay(dx, 0)
                go(dx, 0, "y")
                go(dx, 0, "c")
            yield
            come(0, 0, "y")
            go(0, 1, "c")
            pair(-1, 0)
            pair(1, 0)
            yield
            come(-1, 0, "xp")
            come(1, 0, "xm")
            go(2, 0, "y")
            go(2, 0, "c")
            come(-1, 0, "y")
            go(-1, 1, "c")
            come(1, 0, "y")
            go(1, 1, "c")
            yield
            pair(0, 1)
            pair(2, 0)
            yield
            come(2, 0, "y")
            go(2, 1, "c")
            pair(-1, 1)
            pair(1, 1)
            yield
            pair(2, 1)
            yield

        return x_first() if side else y_first()

    ones = jnp.ones((16, half), BF16)
    tri = lax.broadcasted_iota(jnp.int32, (half, half), 0) <= lax.broadcasted_iota(
        jnp.int32, (half, half), 1
    )

    def unit(queries, acc, top_ref, side, blocks, masked=False):
        these = queries[side]
        scores = [jnp.dot(keys, these, preferred_element_type=F32) for keys, _ in blocks]
        if masked:
            scores = [jnp.where(tri, block, LOW) for block in scores]
        old = top_ref[side, 0:1, :]
        best = functools.reduce(jnp.maximum, scores)
        new = jnp.maximum(old, jnp.max(best, axis=0, keepdims=True))
        top_ref[side, 0:1, :] = new
        total = acc[side] * jnp.exp2((old - new) * scale)
        for block, (_, values) in zip(scores, blocks):
            weights = jnp.exp2((block - new) * scale).astype(BF16)
            total = total + jnp.dot(
                jnp.concatenate([values, ones], axis=0), weights, preferred_element_type=F32
            )
        acc[side] = total

    def own_block(side):
        return (k_ref[side * half : (side + 1) * half, :], vt_own[side])

    def block_at(slot, side):
        return (kbuf[slot, pl.ds(pl.multiple_of(side * half, half), half), :], vbuf[slot, side])

    def third_unit(slots):
        unit(qt_par, acc_par, max_par, y_hi, [block_at(slot, y_hi) for slot in slots])

    def last_unit(slot):
        side = jnp.where(slot <= z, 0, 1)
        unit(qt_own, acc_own, max_own, side, [block_at(slot, side)])

    def early(slots):
        blocks = [block_at(slot, 0) for slot in slots]
        unit(qt_par, acc_par, max_par, 1, blocks)
        unit(qt_own, acc_own, max_own, 1, blocks)

    def late(slots):
        third_unit(slots)
        for slot in slots:
            last_unit(slot)

    for load in loads[:2] + loads[3:5]:
        load.wait()

    def res_place(chunk, first, count):
        return res_all.at[chunk, pl.ds(first, count), :]

    def wo_place(chunk, first, count):
        return wo_all.at[head_rows(chunk, first, count), :]

    def att_place(chunk, first, count):
        return att_all.at[chunk, pl.ds(first, count), :]

    def nothing(chip):
        pass

    res_a = gather(1, 0, res_place, half, nothing)
    res_b = gather(1, 1, res_place, half, nothing)
    wo_a = gather(2, 0, wo_place, LANES // 2, nothing, True)
    wo_b = gather(2, 1, wo_place, LANES // 2, nothing, True)
    for stages in (res_a, res_b):
        next(stages)
    for load in loads[5:]:
        load.wait()
    str_acc[...] = jnp.zeros_like(str_acc)
    diagonal = lax.broadcasted_iota(jnp.int32, (LANES, LANES), 0) == lax.broadcasted_iota(
        jnp.int32, (LANES, LANES), 1
    )

    def to_column(line, count=LANES):
        return jnp.sum(jnp.where(diagonal[:count], line, 0.0), axis=1, keepdims=True)

    def to_line(column):
        picked = jnp.where(diagonal[: column.shape[0]], column, 0.0)
        return jnp.sum(picked, axis=0, keepdims=True)

    def scale_win():
        def block(head, carry):
            at = head_rows(head)
            column = to_column(gain_ref[pl.ds(head, 1), :])
            win[at, :] = (win[at, :].astype(F32) * column).astype(BF16)
            return carry

        lax.fori_loop(0, n_tp, block, 0)

    def chip_rows(chip):
        return pl.ds(pl.multiple_of(chip * 2 * LANES, 2 * LANES), 2 * LANES)

    def prepare(*offsets):
        for dx, dy in offsets:
            chip = tp_at(dx, dy, 0) // 2
            deep = chip_rows(chip)
            joint[deep, :] = jnp.dot(
                wo_all[deep, :], win[...], preferred_element_type=F32
            ).astype(BF16)
            left_side = jnp.concatenate([res_all[2 * chip], res_all[2 * chip + 1]], axis=1)
            str_acc[...] += jnp.dot(left_side, win[deep, :], preferred_element_type=F32)

    def steps(*names):
        for stages in names:
            next(stages)

    plan = {
        1: ((res_a, res_a, res_b, wo_a), ()),
        2: ((res_a, res_a, res_b, res_b, wo_b), ()),
        3: ((wo_a, wo_a, res_a, res_a, res_b), ()),
        4: ((wo_b, wo_b, res_a, res_b, res_b), ()),
        5: ((wo_a, wo_a), ((0, 0),)),
        6: ((wo_a, wo_b), ((-1, 0), (1, 0))),
        7: ((wo_a, wo_b, wo_b), ((0, 1), (-1, 1))),
    }

    def share_residual_rim():
        for copy in res_tails:
            copy.wait_recv()
        spread_each(0, res_all, lambda copy: copy.start())

    def extra(number):
        names, offsets = plan[number]
        steps(*names)
        prepare(*offsets)
        if number == 2:
            share_residual_rim()
        if number == 3:
            scale_win()
        if number == 4:
            spread_each(0, res_all, lambda copy: copy.wait_recv())
    for side in range(2):
        qt_own[side] = turned(q_ref, side)
    unit(qt_own, acc_own, max_own, 0, [own_block(0)], True)
    unit(qt_own, acc_own, max_own, 1, [own_block(1)], True)
    unit(qt_own, acc_own, max_own, 1, [own_block(0)])

    def key_wait(slot, side):
        key_copy(part_of(k_hbm, side), slot, side, right).wait_recv()

    def value_wait(slot, side):
        value_copy(vt_own.at[side], slot, side, right).wait_recv()

    def when(condition, act):
        if isinstance(condition, bool):
            if condition:
                act()
        else:
            pl.when(condition)(act)

    def pass_keys(step, side):
        back = ring - step
        key_wait(step, side)
        key_copy(part_of(kbuf.at[step], side), step + 1, side, right).start()
        key_wait(back, side)
        when(
            step < top - 1,
            lambda: key_copy(part_of(kbuf.at[back], side), back - 1, side, left).start(),
        )

    def pass_values(step, side):
        back = ring - step
        value_wait(step, side)
        when(
            step < top - 1,
            lambda: value_copy(vbuf.at[step, side], step + 1, side, right).start(),
        )
        value_wait(back, side)
        value_copy(vbuf.at[back, side], back - 1, side, left).start()

    def meet_partner():
        q_copy.wait_recv()
        for side in range(2):
            qt_par[side] = turned(qpar, side)
        unit(qt_par, acc_par, max_par, 1, [own_block(0)])
        pl.when(y_hi == 0)(lambda: unit(qt_par, acc_par, max_par, 0, [own_block(0)]))
        pl.when(y_hi == 1)(lambda: unit(qt_par, acc_par, max_par, 1, [own_block(1)]))

    def turn(step, carry):
        back = ring - step
        pass_keys(step, 0)
        pl.when(step > 1)(lambda: pass_keys(step - 1, 1))
        pl.when(step > 2)(lambda: late((step - 2, back + 2)))
        pl.when(step == 1)(meet_partner)
        pass_values(step, 0)
        pl.when(step > 1)(lambda: pass_values(step - 1, 1))
        early((step, back))
        for number in range(1, top):
            pl.when(step == number)(functools.partial(extra, number))
        return carry

    lax.fori_loop(1, top, turn, 0)
    for number in range(top, 8):
        extra(number)
    key_wait(top, 0)
    pass_keys(top - 1, 1)
    if top > 2:
        late((top - 2, top + 2))
    value_wait(top, 0)
    pass_values(top - 1, 1)
    far = (top - 1, top + 1, top)
    unit(qt_par, acc_par, max_par, 1, [block_at(top, 0)])
    pl.when(y_hi == 0)(lambda: third_unit(far))

    def settle(acc, top_ref, side):
        total = acc[side, width : width + 1, :]
        seen = total > 0.0
        held = jnp.where(seen, total, 1.0)
        level = jnp.where(seen, top_ref[side, 0:1, :] * scale + jnp.log2(held), LOW)
        return acc[side, :width, :] * (1.0 / held), level

    st_copies = [
        remote(st_send.at[n], st_recv.at[n], x_send.at[1 + n], x_recv.at[1 + n], across)
        for n in range(2)
    ]
    o_copies = [
        remote(o_send.at[n], o_recv.at[n], x_send.at[3 + n], x_recv.at[3 + n], across)
        for n in range(2)
    ]

    def send_partial(side):
        mean, level = settle(acc_par, max_par, side)
        o_send[side] = mean.astype(BF16)
        o_copies[side].start()
        st_send[side] = jnp.broadcast_to(level, (8, half))
        st_copies[side].start()

    send_partial(0)
    for slot in (top - 1, top + 1):
        last_unit(slot)
    steps(wo_a, wo_b)
    prepare((1, 1), (2, 0))
    key_wait(top, 1)
    value_wait(top, 1)
    pl.when(y_hi == 1)(lambda: third_unit(far))
    send_partial(1)
    unit(qt_own, acc_own, max_own, 1, [block_at(top, 0)])
    last_unit(top)
    prepare((2, 1),)
    hid_acc[...] = res_all[tp].astype(F32)
    sides = (pl.ds(0, half), pl.ds(half, half))
    att_tails = tail_copies(att_all.at[tp], att_all, 7)

    def join(side):
        mean_own, level_own = settle(acc_own, max_own, side)
        st_copies[side].wait_recv()
        o_copies[side].wait_recv()
        level_other = st_recv[side, 0:1, :]
        most = jnp.maximum(level_own, level_other)
        w_own = jnp.exp2(level_own - most)
        w_other = jnp.exp2(level_other - most)
        share = 1.0 / (w_own + w_other)
        joined = mean_own * (w_own * share) + o_recv[side].astype(F32) * (w_other * share)
        att_all[tp, side * half : (side + 1) * half, :] = joined.T.astype(BF16)

    def project(at):

        def apply(chip):
            left_side = jnp.concatenate(
                [att_all[2 * chip, at, :], att_all[2 * chip + 1, at, :]], axis=1
            )
            deep = chip_rows(chip)
            weight = jnp.concatenate([wo_all[deep, own_cols], joint[deep, :]], axis=1)
            product = jnp.dot(left_side, weight, preferred_element_type=F32)
            hid_acc[at, :] += product[:, :LANES]
            str_acc[at, :] += product[:, LANES:]

        return apply

    def square_copy(side, step):
        peer = lax.rem(tp + step, n_tp)
        ref = sq_all.at[tp, side]
        return remote(ref, ref, w_send.at[side, step], w_recv.at[side, step], {"tp": peer})

    def square_each(side, act):
        def one(step, carry):
            act(square_copy(side, step))
            return carry

        lax.fori_loop(1, n_tp, one, 0)

    lines_used = half // LANES

    def finish_hidden(side):
        sq_all[tp, side] = jnp.zeros((8, LANES), F32)

        def squares(first, count, line):
            hidden = hid_acc[first : first + count, :].astype(BF16)
            if first < rows:
                hid_ref[first : first + count, :] = hidden
            wide = hidden.astype(F32)
            sq_all[tp, side, line : line + 1, :] = to_line(
                jnp.sum(wide * wide, axis=1, keepdims=True)
            )

        for g in range(lines_used):
            squares(side * half + g * LANES, LANES, g)
        if side:
            squares(rows, 2 * edge, lines_used)
        square_each(side, lambda copy: copy.start())

    def finish_streams(side):
        square_each(side, lambda copy: copy.wait_recv())
        lines = jnp.sum(sq_all[:, side], axis=0)

        def streams(first, count, line):
            mean_square = to_column(lines[line : line + 1, :], count) / (n_tp * LANES)
            scaled = str_acc[first : first + count, :] * lax.rsqrt(mean_square + 1e-6)
            return scaled.astype(BF16).astype(F32)

        for g in range(lines_used):
            at = slice(RIM + g * LANES, RIM + (g + 1) * LANES)
            ext[side, at, :] = streams(side * half + g * LANES, LANES, g)
        if side:
            outside = streams(rows, 2 * edge, lines_used)
            ext[0, :RIM, :] = jnp.where(dev == 0, 0.0, outside[RIM:edge])
            ext[1, :RIM, :] = jnp.where(
                dev == n_ctx - 1, ext[0, half : half + RIM, :], outside[edge + RIM :]
            )

    out_a = gather(0, 0, att_place, half, project(sides[0]))
    out_b = gather(0, 1, att_place, half, project(sides[1]))
    join(0)
    next(out_a)
    att_tails[0].start()
    join(1)
    next(out_b)
    att_tails[1].start()
    steps(out_a, out_a, out_b)
    for copy in att_tails:
        copy.wait_recv()
    spread_each(1, att_all, lambda copy: copy.start())
    steps(out_b, out_a, out_a, out_a, out_b, out_a, out_b, out_a)
    finish_hidden(0)
    spread_each(1, att_all, lambda copy: copy.wait_recv())
    project_rim = project(rim)
    for chip in range(n_tp // 2):
        project_rim(chip)
    steps(out_b, out_b)
    finish_hidden(1)

    lane_group = lax.broadcasted_iota(jnp.int32, (FILTER_TAPS, LANES), 1) // GROUP
    filt = jnp.zeros((FILTER_TAPS, LANES), F32)
    for g in range(LANES // GROUP):
        filt = jnp.where(lane_group == g, filt_ref[:, g : g + 1], filt)

    def convolve(side, low, high):
        count = high - low
        span = count + FILTER_TAPS - 1

        def featured(stream, first, number):
            cols = slice(stream * LANES, (stream + 1) * LANES)
            total = None
            for j in range(FEAT_TAPS):
                row = first + RIM - j
                term = taps_ref[j, stream : stream + 1, :] * ext[side, row : row + number, cols]
                total = term if total is None else total + term
            return total

        first = low - (FILTER_TAPS - 1)
        mix[0:span, :] = featured(0, first, span) * featured(2, first, span)
        response = None
        for j in range(FILTER_TAPS):
            row = FILTER_TAPS - 1 - j
            term = filt[j : j + 1, :] * mix[row : row + count, :]
            response = term if response is None else response + term
        out = featured(1, low, count) * response
        gated_ref[side * half + low : side * half + high, :] = out.astype(BF16)

    finish_streams(0)
    convolve(0, edge, half)
    finish_streams(1)
    convolve(0, 0, edge)
    convolve(1, 0, half)
    def drain(slot, carry):
        for side in range(2):
            key_copy(part_of(k_hbm, side), slot, side, right).wait_send()
            value_copy(part_of(v_hbm, side), slot, side, right).wait_send()
        return carry

    lax.fori_loop(1, ring, drain, 0)

    for side in range(2):
        square_each(side, lambda copy: copy.wait_send())
    spread_each(0, res_all, lambda copy: copy.wait_send())
    spread_each(1, att_all, lambda copy: copy.wait_send())
    for copy in [q_copy] + st_copies + o_copies + res_tails + att_tails:
        copy.wait_send()
    for move in moves:
        move().wait_send()


def local(queries, keys, values, residual, out_proj, norm_gain, in_proj, feat_taps, long_filter):
    rows, width = queries.shape
    half = rows // 2
    n_tp = lax.axis_size("tp")
    ring = lax.axis_size("ctx") // 2
    vmem = pl.BlockSpec(memory_space=pltpu.VMEM)
    hbm = pl.BlockSpec(memory_space=pltpu.HBM)
    dma = pltpu.SemaphoreType.DMA
    shape = jax.ShapeDtypeStruct((rows, width), BF16)
    return pl.pallas_call(
        functools.partial(kernel, ring),
        out_shape=(shape, shape),
        in_specs=[hbm] * 9,
        out_specs=(vmem, vmem),
        scratch_shapes=[
            pltpu.VMEM((rows, width), BF16),
            pltpu.VMEM((rows, width), BF16),
            pltpu.VMEM((rows, width), BF16),
            pltpu.VMEM((n_tp, LANES), F32),
            pltpu.VMEM((FEAT_TAPS, 3, LANES), F32),
            pltpu.VMEM((FILTER_TAPS, LANES // GROUP), F32),
            pltpu.VMEM((ring, rows, width), BF16),
            pltpu.VMEM((ring, 2, width, half), BF16),
            pltpu.VMEM((2, width, half), BF16),
            pltpu.VMEM((2, width, half), BF16),
            pltpu.VMEM((2, width, half), BF16),
            pltpu.VMEM((rows, width), BF16),
            pltpu.VMEM((2, width + 16, half), F32),
            pltpu.VMEM((2, width + 16, half), F32),
            pltpu.VMEM((2, 8, half), F32),
            pltpu.VMEM((2, 8, half), F32),
            pltpu.VMEM((2, width, half), BF16),
            pltpu.VMEM((2, width, half), BF16),
            pltpu.VMEM((2, 8, half), F32),
            pltpu.VMEM((2, 8, half), F32),
            pltpu.VMEM((n_tp * LANES, n_tp * LANES), BF16),
            pltpu.VMEM((n_tp * LANES, 3 * LANES), BF16),
            pltpu.VMEM((n_tp * LANES, 3 * LANES), BF16),
            pltpu.VMEM((n_tp, rows + 4 * RIM, width), BF16),
            pltpu.VMEM((n_tp, rows + 4 * RIM, width), BF16),
            pltpu.VMEM((rows + 4 * RIM, LANES), F32),
            pltpu.VMEM((rows + 4 * RIM, 3 * LANES), F32),
            pltpu.VMEM((n_tp, 2, 8, LANES), F32),
            pltpu.VMEM((2, RIM + half, 3 * LANES), F32),
            pltpu.VMEM((RIM + half, LANES), F32),
            dma((11,)),
            dma((ring, 2)),
            dma((ring, 2)),
            dma((ring, 2)),
            dma((ring, 2)),
            dma((9,)),
            dma((9,)),
            dma((2, n_tp)),
            dma((2, n_tp)),
            dma((2, n_tp)),
            dma((2, n_tp)),
            dma((3, 2, 20)),
            dma((3, 2, 20)),
        ],
        compiler_params=pltpu.CompilerParams(
            collective_id=0, has_side_effects=True, vmem_limit_bytes=40 * 1024 * 1024
        ),
        cost_estimate=pl.CostEstimate(
            flops=4 * 10**9, bytes_accessed=4 * 10**6, transcendentals=5 * 10**6
        ),
    )(
        *(
            pltpu.with_memory_space_constraint(operand, pltpu.HBM)
            for operand in (
                queries,
                keys,
                values,
                residual,
                out_proj,
                norm_gain.reshape(n_tp, LANES),
                jnp.transpose(in_proj, (1, 0, 2)),
                feat_taps,
                long_filter,
            )
        )
    )


def solution(mesh):
    return jax.shard_map(
        local,
        mesh=mesh,
        in_specs=(
            P("ctx", "tp"),
            P("ctx", "tp"),
            P("ctx", "tp"),
            P("ctx", "tp"),
            P("tp", None),
            P(),
            P(None, None, "tp"),
            P(None, None, "tp"),
            P(None, "tp"),
        ),
        out_specs=(P("ctx", "tp"), P("ctx", "tp")),
        check_vma=False,
    )
```

```python
import functools

import jax
import jax.numpy as jnp
from jax import lax
from jax.experimental import pallas as pl
from jax.experimental.pallas import tpu as pltpu
from jax.sharding import PartitionSpec as P

MESH = pl.DeviceIdType.MESH
LANES = 128
GROUP = 16
FEAT_TAPS = 3
FILTER_TAPS = 7
RIM = 8
LOW = -1e30
LOG2E = 1.4426950408889634
F32 = jnp.float32
BF16 = jnp.bfloat16


def kernel(
    ring,
    q_hbm,
    k_hbm,
    v_hbm,
    res_hbm,
    outp_hbm,
    gain_hbm,
    inp_hbm,
    taps_hbm,
    filt_hbm,
    hid_ref,
    gated_ref,
    q_ref,
    k_ref,
    v_ref,
    gain_ref,
    taps_ref,
    filt_ref,
    kbuf,
    vbuf,
    vt_own,
    qt_own,
    qt_par,
    qpar,
    acc_own,
    acc_par,
    max_own,
    max_par,
    o_send,
    o_recv,
    st_send,
    st_recv,
    wo_all,
    win,
    joint,
    att_all,
    res_all,
    hid_acc,
    str_acc,
    sq_all,
    ext,
    mix,
    in_sem,
    ks_sem,
    kr_sem,
    vs_sem,
    vr_sem,
    x_send,
    x_recv,
    w_send,
    w_recv,
    h_send,
    h_recv,
    g_send,
    g_recv,
):
    rows, width = q_ref.shape
    half = rows // 2
    edge = 2 * RIM
    rim = pl.ds(rows, 2 * edge)
    top = ring // 2
    n_ctx = 2 * ring
    n_tp = att_all.shape[0]
    n_x = n_tp // 4
    dev = lax.axis_index("ctx")
    y_hi = dev // ring
    z = lax.rem(dev, ring)
    tp = lax.axis_index("tp")
    x = tp // 4
    y_lo = lax.rem(tp, 4) // 2
    core = lax.rem(tp, 2)
    scale = LOG2E * width**-0.5

    def ctx_id(y_at, z_at):
        return {"ctx": y_at * ring + z_at}

    right = ctx_id(y_hi, lax.rem(z + 1, ring))
    left = ctx_id(y_hi, lax.rem(z + ring - 1, ring))
    across = ctx_id(1 - y_hi, z)
    beside = {"ctx": (1 - y_hi) * ring + z, "tp": tp + 2 - 4 * y_lo}
    after = {"ctx": lax.rem(dev + 1, n_ctx)}
    before = {"ctx": lax.rem(dev + n_ctx - 1, n_ctx)}

    def tp_at(dx, dy, dc):
        return (
            lax.rem(x + dx + n_x, n_x) * 4
            + (1 - y_lo if dy else y_lo) * 2
            + (1 - core if dc else core)
        )

    barrier = pltpu.get_barrier_semaphore()
    for other in (right, left, across, beside, after, before):
        pl.semaphore_signal(barrier, inc=1, device_id=other, device_id_type=MESH)

    def greet(step, carry):
        peer = lax.rem(tp + step, n_tp)
        pl.semaphore_signal(barrier, inc=1, device_id={"tp": peer}, device_id_type=MESH)
        return carry

    lax.fori_loop(1, n_tp, greet, 0)

    own_cols = pl.ds(pl.multiple_of(tp * LANES, LANES), LANES)

    def head_rows(head, first=0, count=LANES):
        return pl.ds(pl.multiple_of(head * LANES + first, count), count)

    loads = []
    for src, dst in [
        (q_hbm, q_ref),
        (k_hbm, k_ref),
        (v_hbm, v_ref),
        (res_hbm, res_all.at[tp, pl.ds(0, rows), :]),
        (outp_hbm, wo_all.at[head_rows(tp), :]),
        (gain_hbm, gain_ref),
        (taps_hbm, taps_ref),
        (filt_hbm, filt_ref),
    ] + [(inp_hbm.at[s], win.at[:, s * LANES : (s + 1) * LANES]) for s in range(3)]:
        load = pltpu.make_async_copy(src, dst, in_sem.at[len(loads)])
        load.start()
        loads.append(load)

    for acc, top_ref in ((acc_own, max_own), (acc_par, max_par)):
        acc[...] = jnp.zeros_like(acc)
        top_ref[...] = jnp.full(top_ref.shape, LOW, F32)
    pl.semaphore_wait(barrier, n_tp - 1 + 6)

    def remote(src, dst, send, recv, to):
        return pltpu.make_async_remote_copy(
            src_ref=src, dst_ref=dst, send_sem=send, recv_sem=recv, device_id=to, device_id_type=MESH
        )

    def part_of(ref, side):
        return ref.at[pl.ds(side * half, half), :]

    def key_copy(src, slot, side, to):
        dst = part_of(kbuf.at[slot], side)
        return remote(src, dst, ks_sem.at[slot, side], kr_sem.at[slot, side], to)

    def value_copy(src, slot, side, to):
        return remote(
            src, vbuf.at[slot, side], vs_sem.at[slot, side], vr_sem.at[slot, side], to
        )

    def turned(ref, side):
        return ref[side * half : (side + 1) * half, :].astype(F32).T.astype(BF16)

    q_copy = remote(q_hbm, qpar, x_send.at[0], x_recv.at[0], across)
    for side in range(2):
        for to, slot in ((right, 1), (left, ring - 1)):
            key_copy(part_of(k_hbm, side), slot, side, to).start()
        if side == 0:
            q_copy.start()
            loads[2].wait()
        vt_own[side] = turned(v_ref, side)
        for to, slot in ((right, 1), (left, ring - 1)):
            value_copy(vt_own.at[side], slot, side, to).start()

    def tail_copies(src, dst, first_sem):
        return [
            remote(
                src.at[pl.ds((side + 1) * half - edge, edge), :],
                dst.at[tp, pl.ds(rows + side * edge, edge), :],
                x_send.at[first_sem + side],
                x_recv.at[first_sem + side],
                to,
            )
            for side, to in enumerate((after, before))
        ]

    res_tails = tail_copies(res_hbm, res_all, 5)
    for copy in res_tails:
        copy.start()

    def spread_each(which, buf, act):
        def one(step, carry):
            ref = buf.at[tp, rim, :]
            peer = lax.rem(tp + step, n_tp)
            act(remote(ref, ref, h_send.at[which, step], h_recv.at[which, step], {"tp": peer}))
            return carry

        lax.fori_loop(1, n_tp, one, 0)

    targets = {
        "y": {"tp": tp_at(0, 1, 0)},
        "yy": beside,
        "xp": {"tp": tp_at(1, 0, 0)},
        "xm": {"tp": tp_at(-1, 0, 0)},
        "c": {"tp": tp_at(0, 0, 1)},
    }
    moves = []

    def gather(which, side, place, span, consume, twin=False):
        whole = (side * span, span)
        head = (side * span, span // 2)
        tail = (side * span + span // 2, span // 2)
        known = {}

        def copy_of(dx, dy, dc, part, number, to):
            ref = place(tp_at(dx, dy, dc), *part)
            return remote(
                ref, ref, g_send.at[which, side, number], g_recv.at[which, side, number], targets[to]
            )

        def go(dx, dy, to, part=whole):
            if twin and to == "y" and part == whole:
                go(dx, dy, "y", head)
                go(dx, dy, "yy", tail)
                return
            number = len(known)
            known[dx, dy, to] = (number, part)
            copy_of(dx, dy, 0, part, number, to).start()
            moves.append(lambda: copy_of(dx, dy, 0, part, number, to))

        def come(dx, dy, to):
            if twin and to == "y":
                come(dx, dy, "yy")
            number, part = known[dx, dy, to]
            sx = dx + {"xp": -1, "xm": 1}.get(to, 0)
            sy = 1 - dy if to in ("y", "yy") else dy
            copy_of(sx, sy, 1 if to == "c" else 0, part, number, to).wait_recv()

        def pair(dx, dy):
            come(dx, dy, "c")
            consume(tp_at(dx, dy, 0) // 2)

        def relay(dx, dy):
            go(dx, dy, "xp" if dx < 0 else "xm", head if dx < 0 else tail)

        def y_first():
            for to in ("y", "xp", "xm", "c"):
                go(0, 0, to)
            yield
            come(0, 0, "y")
            for to in ("xp", "xm", "c"):
                go(0, 1, to)
            pair(0, 0)
            yield
            for dx, to in ((-1, "xp"), (1, "xm")):
                come(0, 0, to)
                relay(dx, 0)
                go(dx, 0, "c")
            yield
            pair(0, 1)
            for dx, to in ((-1, "xp"), (1, "xm")):
                come(0, 1, to)
                relay(dx, 1)
                go(dx, 1, "c")
            yield
            pair(-1, 0)
            pair(1, 0)
            yield
            come(-1, 0, "xp")
            come(1, 0, "xm")
            go(2, 0, "c")
            pair(-1, 1)
            pair(1, 1)
            yield
            come(-1, 1, "xp")
            come(1, 1, "xm")
            go(2, 1, "c")
            pair(2, 0)
            yield
            pair(2, 1)
            yield

        def x_first():
            for to in ("xp", "xm", "y", "c"):
                go(0, 0, to)
            yield
            pair(0, 0)
            for dx, to in ((-1, "xp"), (1, "xm")):
                come(0, 0, to)
                relay(dx, 0)
                go(dx, 0, "y")
                go(dx, 0, "c")
            yield
            come(0, 0, "y")
            go(0, 1, "c")
            pair(-1, 0)
            pair(1, 0)
            yield
            come(-1, 0, "xp")
            come(1, 0, "xm")
            go(2, 0, "y")
            go(2, 0, "c")
            come(-1, 0, "y")
            go(-1, 1, "c")
            come(1, 0, "y")
            go(1, 1, "c")
            pair(0, 1)
            yield
            pair(2, 0)
            yield
            come(2, 0, "y")
            go(2, 1, "c")
            pair(-1, 1)
            pair(1, 1)
            yield
            pair(2, 1)
            yield

        return x_first() if side % 2 else y_first()

    ones = jnp.ones((16, half), BF16)
    tri = lax.broadcasted_iota(jnp.int32, (half, half), 0) <= lax.broadcasted_iota(
        jnp.int32, (half, half), 1
    )

    def unit(queries, acc, top_ref, side, blocks, masked=False):
        these = queries[side]
        scores = [jnp.dot(keys, these, preferred_element_type=F32) for keys, _ in blocks]
        if masked:
            scores = [jnp.where(tri, block, LOW) for block in scores]
        old = top_ref[side, 0:1, :]
        best = functools.reduce(jnp.maximum, scores)
        new = jnp.maximum(old, jnp.max(best, axis=0, keepdims=True))
        top_ref[side, 0:1, :] = new
        total = acc[side] * jnp.exp2((old - new) * scale)
        for block, (_, values) in zip(scores, blocks):
            weights = jnp.exp2((block - new) * scale).astype(BF16)
            total = total + jnp.dot(
                jnp.concatenate([values, ones], axis=0), weights, preferred_element_type=F32
            )
        acc[side] = total

    def own_block(side):
        return (k_ref[side * half : (side + 1) * half, :], vt_own[side])

    def block_at(slot, side):
        return (kbuf[slot, pl.ds(pl.multiple_of(side * half, half), half), :], vbuf[slot, side])

    def third_unit(slots):
        unit(qt_par, acc_par, max_par, y_hi, [block_at(slot, y_hi) for slot in slots])

    def last_unit(slot):
        side = jnp.where(slot <= z, 0, 1)
        unit(qt_own, acc_own, max_own, side, [block_at(slot, side)])

    def early(slots):
        blocks = [block_at(slot, 0) for slot in slots]
        unit(qt_par, acc_par, max_par, 1, blocks)
        unit(qt_own, acc_own, max_own, 1, blocks)

    def late(slots):
        third_unit(slots)
        for slot in slots:
            last_unit(slot)

    for load in loads[:2] + loads[3:5]:
        load.wait()

    def res_place(chunk, first, count):
        return res_all.at[chunk, pl.ds(first, count), :]

    def wo_place(chunk, first, count):
        return wo_all.at[head_rows(chunk, first, count), :]

    def att_place(chunk, first, count):
        return att_all.at[chunk, pl.ds(first, count), :]

    def nothing(chip):
        pass

    res_a = gather(1, 0, res_place, half, nothing)
    res_b = gather(1, 1, res_place, half, nothing)
    wo_a = gather(2, 0, wo_place, LANES // 2, nothing, True)
    wo_b = gather(2, 1, wo_place, LANES // 2, nothing, True)
    for stages in (res_a, res_b, wo_a):
        next(stages)
    for load in loads[5:]:
        load.wait()
    str_acc[...] = jnp.zeros_like(str_acc)
    diagonal = lax.broadcasted_iota(jnp.int32, (LANES, LANES), 0) == lax.broadcasted_iota(
        jnp.int32, (LANES, LANES), 1
    )

    def to_column(line, count=LANES):
        return jnp.sum(jnp.where(diagonal[:count], line, 0.0), axis=1, keepdims=True)

    def to_line(column):
        picked = jnp.where(diagonal[: column.shape[0]], column, 0.0)
        return jnp.sum(picked, axis=0, keepdims=True)

    def scale_win():
        def block(head, carry):
            at = head_rows(head)
            column = to_column(gain_ref[pl.ds(head, 1), :])
            win[at, :] = (win[at, :].astype(F32) * column).astype(BF16)
            return carry

        lax.fori_loop(0, n_tp, block, 0)

    def chip_rows(chip):
        return pl.ds(pl.multiple_of(chip * 2 * LANES, 2 * LANES), 2 * LANES)

    def prepare(*offsets):
        for dx, dy in offsets:
            chip = tp_at(dx, dy, 0) // 2
            deep = chip_rows(chip)
            joint[deep, :] = jnp.dot(
                wo_all[deep, :], win[...], preferred_element_type=F32
            ).astype(BF16)
            left_side = jnp.concatenate([res_all[2 * chip], res_all[2 * chip + 1]], axis=1)
            str_acc[...] += jnp.dot(left_side, win[deep, :], preferred_element_type=F32)

    def steps(*names):
        for stages in names:
            next(stages)

    plan = {
        1: ((), ()),
        2: ((res_a, res_a, res_b, wo_b), ()),
        3: ((wo_a, wo_a, res_a, res_b), ()),
        4: ((wo_b, wo_b, res_a, res_b), ()),
        5: ((wo_a, wo_a, res_a, res_b), ((0, 0),)),
        6: ((wo_a, res_a, res_b), ((-1, 0),)),
        7: ((wo_a, wo_b, res_a, res_b), ((1, 0), (0, 1))),
    }

    def share_residual_rim():
        for copy in res_tails:
            copy.wait_recv()
        spread_each(0, res_all, lambda copy: copy.start())

    def extra(number):
        names, offsets = plan[number]
        steps(*names)
        prepare(*offsets)
        if number == 2:
            share_residual_rim()
        if number == 3:
            scale_win()
        if number == 4:
            spread_each(0, res_all, lambda copy: copy.wait_recv())
    for side in range(2):
        qt_own[side] = turned(q_ref, side)
    unit(qt_own, acc_own, max_own, 0, [own_block(0)], True)
    unit(qt_own, acc_own, max_own, 1, [own_block(1)], True)
    unit(qt_own, acc_own, max_own, 1, [own_block(0)])

    def key_wait(slot, side):
        key_copy(part_of(k_hbm, side), slot, side, right).wait_recv()

    def value_wait(slot, side):
        value_copy(vt_own.at[side], slot, side, right).wait_recv()

    def when(condition, act):
        if isinstance(condition, bool):
            if condition:
                act()
        else:
            pl.when(condition)(act)

    def pass_keys(step, side):
        back = ring - step
        key_wait(step, side)
        key_copy(part_of(kbuf.at[step], side), step + 1, side, right).start()
        key_wait(back, side)
        when(
            step < top - 1,
            lambda: key_copy(part_of(kbuf.at[back], side), back - 1, side, left).start(),
        )

    def pass_values(step, side):
        back = ring - step
        value_wait(step, side)
        when(
            step < top - 1,
            lambda: value_copy(vbuf.at[step, side], step + 1, side, right).start(),
        )
        value_wait(back, side)
        value_copy(vbuf.at[back, side], back - 1, side, left).start()

    def meet_partner():
        q_copy.wait_recv()
        for side in range(2):
            qt_par[side] = turned(qpar, side)
        unit(qt_par, acc_par, max_par, 1, [own_block(0)])
        pl.when(y_hi == 0)(lambda: unit(qt_par, acc_par, max_par, 0, [own_block(0)]))
        pl.when(y_hi == 1)(lambda: unit(qt_par, acc_par, max_par, 1, [own_block(1)]))

    def turn(step, carry):
        back = ring - step
        pass_keys(step, 0)
        pl.when(step > 1)(lambda: pass_keys(step - 1, 1))
        pl.when(step > 2)(lambda: late((step - 2, back + 2)))
        pl.when(step == 1)(meet_partner)
        pass_values(step, 0)
        pl.when(step > 1)(lambda: pass_values(step - 1, 1))
        early((step, back))
        for number in range(1, top):
            pl.when(step == number)(functools.partial(extra, number))
        return carry

    lax.fori_loop(1, top, turn, 0)
    for number in range(top, 8):
        extra(number)
    key_wait(top, 0)
    pass_keys(top - 1, 1)
    if top > 2:
        late((top - 2, top + 2))
    value_wait(top, 0)
    pass_values(top - 1, 1)
    far = (top - 1, top + 1, top)
    unit(qt_par, acc_par, max_par, 1, [block_at(top, 0)])
    pl.when(y_hi == 0)(lambda: third_unit(far))
    pl.when(y_hi == 1)(lambda: third_unit(far[:2]))

    def settle(acc, top_ref, side):
        total = acc[side, width : width + 1, :]
        seen = total > 0.0
        held = jnp.where(seen, total, 1.0)
        level = jnp.where(seen, top_ref[side, 0:1, :] * scale + jnp.log2(held), LOW)
        return acc[side, :width, :] * (1.0 / held), level

    st_copies = [
        remote(st_send.at[n], st_recv.at[n], x_send.at[1 + n], x_recv.at[1 + n], across)
        for n in range(2)
    ]
    o_copies = [
        remote(o_send.at[n], o_recv.at[n], x_send.at[3 + n], x_recv.at[3 + n], across)
        for n in range(2)
    ]

    def send_partial(side):
        mean, level = settle(acc_par, max_par, side)
        o_send[side] = mean.astype(BF16)
        o_copies[side].start()
        st_send[side] = jnp.broadcast_to(level, (8, half))
        st_copies[side].start()

    send_partial(0)
    for slot in (top - 1, top + 1):
        last_unit(slot)
    steps(wo_a, wo_b, wo_b)
    prepare((-1, 1), (1, 1))
    key_wait(top, 1)
    value_wait(top, 1)
    pl.when(y_hi == 1)(lambda: third_unit(far[2:]))
    send_partial(1)
    unit(qt_own, acc_own, max_own, 1, [block_at(top, 0)])
    last_unit(top)
    steps(wo_b)
    prepare((2, 0), (2, 1))
    hid_acc[...] = res_all[tp].astype(F32)
    sides = (pl.ds(0, half), pl.ds(half, half))
    att_tails = tail_copies(att_all.at[tp], att_all, 7)

    def join(side):
        mean_own, level_own = settle(acc_own, max_own, side)
        st_copies[side].wait_recv()
        o_copies[side].wait_recv()
        level_other = st_recv[side, 0:1, :]
        most = jnp.maximum(level_own, level_other)
        w_own = jnp.exp2(level_own - most)
        w_other = jnp.exp2(level_other - most)
        share = 1.0 / (w_own + w_other)
        joined = mean_own * (w_own * share) + o_recv[side].astype(F32) * (w_other * share)
        att_all[tp, side * half : (side + 1) * half, :] = joined.T.astype(BF16)

    def project(at):

        def apply(chip):
            left_side = jnp.concatenate(
                [att_all[2 * chip, at, :], att_all[2 * chip + 1, at, :]], axis=1
            )
            deep = chip_rows(chip)
            weight = jnp.concatenate([wo_all[deep, own_cols], joint[deep, :]], axis=1)
            product = jnp.dot(left_side, weight, preferred_element_type=F32)
            hid_acc[at, :] += product[:, :LANES]
            str_acc[at, :] += product[:, LANES:]

        return apply

    def square_copy(side, step):
        peer = lax.rem(tp + step, n_tp)
        ref = sq_all.at[tp, side]
        return remote(ref, ref, w_send.at[side, step], w_recv.at[side, step], {"tp": peer})

    def square_each(side, act):
        def one(step, carry):
            act(square_copy(side, step))
            return carry

        lax.fori_loop(1, n_tp, one, 0)

    lines_used = half // LANES

    def finish_hidden(side):
        sq_all[tp, side] = jnp.zeros((8, LANES), F32)

        def squares(first, count, line):
            hidden = hid_acc[first : first + count, :].astype(BF16)
            if first < rows:
                hid_ref[first : first + count, :] = hidden
            wide = hidden.astype(F32)
            sq_all[tp, side, line : line + 1, :] = to_line(
                jnp.sum(wide * wide, axis=1, keepdims=True)
            )

        for g in range(lines_used):
            squares(side * half + g * LANES, LANES, g)
        if side:
            squares(rows, 2 * edge, lines_used)
        square_each(side, lambda copy: copy.start())

    def finish_streams(side):
        square_each(side, lambda copy: copy.wait_recv())
        lines = jnp.sum(sq_all[:, side], axis=0)

        def streams(first, count, line):
            mean_square = to_column(lines[line : line + 1, :], count) / (n_tp * LANES)
            scaled = str_acc[first : first + count, :] * lax.rsqrt(mean_square + 1e-6)
            return scaled.astype(BF16).astype(F32)

        for g in range(lines_used):
            at = slice(RIM + g * LANES, RIM + (g + 1) * LANES)
            ext[side, at, :] = streams(side * half + g * LANES, LANES, g)
        if side:
            outside = streams(rows, 2 * edge, lines_used)
            ext[0, :RIM, :] = jnp.where(dev == 0, 0.0, outside[RIM:edge])
            ext[1, :RIM, :] = jnp.where(
                dev == n_ctx - 1, ext[0, half : half + RIM, :], outside[edge + RIM :]
            )

    outs = [
        gather(0, n, att_place, half // 2, project(pl.ds(n * half // 2, half // 2)))
        for n in range(4)
    ]

    def advance(first, *which):
        steps(*(outs[first + n] for n in which))

    join(0)
    advance(0, 0, 1)
    att_tails[0].start()
    join(1)
    advance(2, 0, 1)
    att_tails[1].start()
    advance(0, 0, 0, 1, 1)
    advance(2, 0, 0, 1, 1)
    for copy in att_tails:
        copy.wait_recv()
    spread_each(1, att_all, lambda copy: copy.start())
    advance(0, 0, 0, 0, 1)
    advance(2, 0, 0, 0, 1)
    advance(0, 0, 1, 0, 1, 1)
    finish_hidden(0)
    spread_each(1, att_all, lambda copy: copy.wait_recv())
    project_rim = project(rim)
    for chip in range(n_tp // 2):
        project_rim(chip)
    advance(2, 0, 1, 0, 1, 1)
    finish_hidden(1)

    lane_group = lax.broadcasted_iota(jnp.int32, (FILTER_TAPS, LANES), 1) // GROUP
    filt = jnp.zeros((FILTER_TAPS, LANES), F32)
    for g in range(LANES // GROUP):
        filt = jnp.where(lane_group == g, filt_ref[:, g : g + 1], filt)

    def convolve(side, low, high):
        count = high - low
        span = count + FILTER_TAPS - 1

        def featured(stream, first, number):
            cols = slice(stream * LANES, (stream + 1) * LANES)
            total = None
            for j in range(FEAT_TAPS):
                row = first + RIM - j
                term = taps_ref[j, stream : stream + 1, :] * ext[side, row : row + number, cols]
                total = term if total is None else total + term
            return total

        first = low - (FILTER_TAPS - 1)
        mix[0:span, :] = featured(0, first, span) * featured(2, first, span)
        response = None
        for j in range(FILTER_TAPS):
            row = FILTER_TAPS - 1 - j
            term = filt[j : j + 1, :] * mix[row : row + count, :]
            response = term if response is None else response + term
        out = featured(1, low, count) * response
        gated_ref[side * half + low : side * half + high, :] = out.astype(BF16)

    finish_streams(0)
    convolve(0, edge, half)
    finish_streams(1)
    convolve(0, 0, edge)
    convolve(1, 0, half)
    def drain(slot, carry):
        for side in range(2):
            key_copy(part_of(k_hbm, side), slot, side, right).wait_send()
            value_copy(part_of(v_hbm, side), slot, side, right).wait_send()
        return carry

    lax.fori_loop(1, ring, drain, 0)

    for side in range(2):
        square_each(side, lambda copy: copy.wait_send())
    spread_each(0, res_all, lambda copy: copy.wait_send())
    spread_each(1, att_all, lambda copy: copy.wait_send())
    for copy in [q_copy] + st_copies + o_copies + res_tails + att_tails:
        copy.wait_send()
    for move in moves:
        move().wait_send()


def local(queries, keys, values, residual, out_proj, norm_gain, in_proj, feat_taps, long_filter):
    rows, width = queries.shape
    half = rows // 2
    n_tp = lax.axis_size("tp")
    ring = lax.axis_size("ctx") // 2
    vmem = pl.BlockSpec(memory_space=pltpu.VMEM)
    hbm = pl.BlockSpec(memory_space=pltpu.HBM)
    dma = pltpu.SemaphoreType.DMA
    shape = jax.ShapeDtypeStruct((rows, width), BF16)
    return pl.pallas_call(
        functools.partial(kernel, ring),
        out_shape=(shape, shape),
        in_specs=[hbm] * 9,
        out_specs=(vmem, vmem),
        scratch_shapes=[
            pltpu.VMEM((rows, width), BF16),
            pltpu.VMEM((rows, width), BF16),
            pltpu.VMEM((rows, width), BF16),
            pltpu.VMEM((n_tp, LANES), F32),
            pltpu.VMEM((FEAT_TAPS, 3, LANES), F32),
            pltpu.VMEM((FILTER_TAPS, LANES // GROUP), F32),
            pltpu.VMEM((ring, rows, width), BF16),
            pltpu.VMEM((ring, 2, width, half), BF16),
            pltpu.VMEM((2, width, half), BF16),
            pltpu.VMEM((2, width, half), BF16),
            pltpu.VMEM((2, width, half), BF16),
            pltpu.VMEM((rows, width), BF16),
            pltpu.VMEM((2, width + 16, half), F32),
            pltpu.VMEM((2, width + 16, half), F32),
            pltpu.VMEM((2, 8, half), F32),
            pltpu.VMEM((2, 8, half), F32),
            pltpu.VMEM((2, width, half), BF16),
            pltpu.VMEM((2, width, half), BF16),
            pltpu.VMEM((2, 8, half), F32),
            pltpu.VMEM((2, 8, half), F32),
            pltpu.VMEM((n_tp * LANES, n_tp * LANES), BF16),
            pltpu.VMEM((n_tp * LANES, 3 * LANES), BF16),
            pltpu.VMEM((n_tp * LANES, 3 * LANES), BF16),
            pltpu.VMEM((n_tp, rows + 4 * RIM, width), BF16),
            pltpu.VMEM((n_tp, rows + 4 * RIM, width), BF16),
            pltpu.VMEM((rows + 4 * RIM, LANES), F32),
            pltpu.VMEM((rows + 4 * RIM, 3 * LANES), F32),
            pltpu.VMEM((n_tp, 2, 8, LANES), F32),
            pltpu.VMEM((2, RIM + half, 3 * LANES), F32),
            pltpu.VMEM((RIM + half, LANES), F32),
            dma((11,)),
            dma((ring, 2)),
            dma((ring, 2)),
            dma((ring, 2)),
            dma((ring, 2)),
            dma((9,)),
            dma((9,)),
            dma((2, n_tp)),
            dma((2, n_tp)),
            dma((2, n_tp)),
            dma((2, n_tp)),
            dma((3, 4, 20)),
            dma((3, 4, 20)),
        ],
        compiler_params=pltpu.CompilerParams(
            collective_id=0, has_side_effects=True, vmem_limit_bytes=40 * 1024 * 1024
        ),
        cost_estimate=pl.CostEstimate(
            flops=4 * 10**9, bytes_accessed=4 * 10**6, transcendentals=5 * 10**6
        ),
    )(
        *(
            pltpu.with_memory_space_constraint(operand, pltpu.HBM)
            for operand in (
                queries,
                keys,
                values,
                residual,
                out_proj,
                norm_gain.reshape(n_tp, LANES),
                jnp.transpose(in_proj, (1, 0, 2)),
                feat_taps,
                long_filter,
            )
        )
    )


def solution(mesh):
    return jax.shard_map(
        local,
        mesh=mesh,
        in_specs=(
            P("ctx", "tp"),
            P("ctx", "tp"),
            P("ctx", "tp"),
            P("ctx", "tp"),
            P("tp", None),
            P(),
            P(None, None, "tp"),
            P(None, None, "tp"),
            P(None, "tp"),
        ),
        out_specs=(P("ctx", "tp"), P("ctx", "tp")),
        check_vma=False,
    )
```

```python
import functools

import jax
import jax.numpy as jnp
from jax import lax
from jax.experimental import pallas as pl
from jax.experimental.pallas import tpu as pltpu
from jax.sharding import PartitionSpec as P

MESH = pl.DeviceIdType.MESH
LANES = 128
GROUP = 16
FEAT_TAPS = 3
FILTER_TAPS = 7
RIM = 8
LOW = -1e30
LOG2E = 1.4426950408889634
F32 = jnp.float32
BF16 = jnp.bfloat16


def kernel(
    ring,
    q_hbm,
    k_hbm,
    v_hbm,
    res_hbm,
    outp_hbm,
    gain_hbm,
    inp_hbm,
    taps_hbm,
    filt_hbm,
    hid_ref,
    gated_ref,
    q_ref,
    k_ref,
    v_ref,
    gain_ref,
    taps_ref,
    filt_ref,
    kbuf,
    vbuf,
    vt_own,
    qt_own,
    qt_par,
    qpar,
    acc_own,
    acc_par,
    max_own,
    max_par,
    o_send,
    o_recv,
    st_send,
    st_recv,
    wo_all,
    win,
    joint,
    att_all,
    res_all,
    hid_acc,
    str_acc,
    sq_all,
    ext,
    mix,
    in_sem,
    ks_sem,
    kr_sem,
    vs_sem,
    vr_sem,
    x_send,
    x_recv,
    w_send,
    w_recv,
    h_send,
    h_recv,
    g_send,
    g_recv,
):
    rows, width = q_ref.shape
    half = rows // 2
    edge = 2 * RIM
    rim = pl.ds(rows, 2 * edge)
    top = ring // 2
    n_ctx = 2 * ring
    n_tp = att_all.shape[0]
    n_x = n_tp // 4
    dev = lax.axis_index("ctx")
    y_hi = dev // ring
    z = lax.rem(dev, ring)
    tp = lax.axis_index("tp")
    x = tp // 4
    y_lo = lax.rem(tp, 4) // 2
    core = lax.rem(tp, 2)
    scale = LOG2E * width**-0.5

    def ctx_id(y_at, z_at):
        return {"ctx": y_at * ring + z_at}

    right = ctx_id(y_hi, lax.rem(z + 1, ring))
    left = ctx_id(y_hi, lax.rem(z + ring - 1, ring))
    across = ctx_id(1 - y_hi, z)
    beside = {"ctx": (1 - y_hi) * ring + z, "tp": tp + 2 - 4 * y_lo}
    after = {"ctx": lax.rem(dev + 1, n_ctx)}
    before = {"ctx": lax.rem(dev + n_ctx - 1, n_ctx)}

    def tp_at(dx, dy, dc):
        return (
            lax.rem(x + dx + n_x, n_x) * 4
            + (1 - y_lo if dy else y_lo) * 2
            + (1 - core if dc else core)
        )

    barrier = pltpu.get_barrier_semaphore()
    for other in (right, left, across, beside, after, before):
        pl.semaphore_signal(barrier, inc=1, device_id=other, device_id_type=MESH)

    def greet(step, carry):
        peer = lax.rem(tp + step, n_tp)
        pl.semaphore_signal(barrier, inc=1, device_id={"tp": peer}, device_id_type=MESH)
        return carry

    lax.fori_loop(1, n_tp, greet, 0)

    own_cols = pl.ds(pl.multiple_of(tp * LANES, LANES), LANES)

    def head_rows(head, first=0, count=LANES):
        return pl.ds(pl.multiple_of(head * LANES + first, count), count)

    loads = []
    for src, dst in [
        (q_hbm, q_ref),
        (k_hbm, k_ref),
        (v_hbm, v_ref),
        (res_hbm, res_all.at[tp, pl.ds(0, rows), :]),
        (outp_hbm, wo_all.at[head_rows(tp), :]),
        (gain_hbm, gain_ref),
        (taps_hbm, taps_ref),
        (filt_hbm, filt_ref),
    ] + [(inp_hbm.at[s], win.at[:, s * LANES : (s + 1) * LANES]) for s in range(3)]:
        load = pltpu.make_async_copy(src, dst, in_sem.at[len(loads)])
        load.start()
        loads.append(load)

    for acc, top_ref in ((acc_own, max_own), (acc_par, max_par)):
        acc[...] = jnp.zeros_like(acc)
        top_ref[...] = jnp.full(top_ref.shape, LOW, F32)
    pl.semaphore_wait(barrier, n_tp - 1 + 6)

    def remote(src, dst, send, recv, to):
        return pltpu.make_async_remote_copy(
            src_ref=src, dst_ref=dst, send_sem=send, recv_sem=recv, device_id=to, device_id_type=MESH
        )

    def key_copy(src, slot, to):
        return remote(src, kbuf.at[slot], ks_sem.at[slot], kr_sem.at[slot], to)

    def value_copy(src, slot, to):
        return remote(src, vbuf.at[slot], vs_sem.at[slot], vr_sem.at[slot], to)

    def turned(ref, side):
        return ref[side * half : (side + 1) * half, :].astype(F32).T.astype(BF16)

    q_copy = remote(q_hbm, qpar, x_send.at[0], x_recv.at[0], across)
    key_copy(k_hbm, 1, right).start()
    key_copy(k_hbm, ring - 1, left).start()
    q_copy.start()
    loads[2].wait()
    for side in range(2):
        vt_own[side] = turned(v_ref, side)
    value_copy(vt_own, 1, right).start()
    value_copy(vt_own, ring - 1, left).start()

    def tail_copies(src, dst, first_sem):
        return [
            remote(
                src.at[pl.ds((side + 1) * half - edge, edge), :],
                dst.at[tp, pl.ds(rows + side * edge, edge), :],
                x_send.at[first_sem + side],
                x_recv.at[first_sem + side],
                to,
            )
            for side, to in enumerate((after, before))
        ]

    res_tails = tail_copies(res_hbm, res_all, 5)
    for copy in res_tails:
        copy.start()

    def spread_each(which, buf, act):
        def one(step, carry):
            ref = buf.at[tp, rim, :]
            peer = lax.rem(tp + step, n_tp)
            act(remote(ref, ref, h_send.at[which, step], h_recv.at[which, step], {"tp": peer}))
            return carry

        lax.fori_loop(1, n_tp, one, 0)

    targets = {
        "y": {"tp": tp_at(0, 1, 0)},
        "yy": beside,
        "xp": {"tp": tp_at(1, 0, 0)},
        "xm": {"tp": tp_at(-1, 0, 0)},
        "c": {"tp": tp_at(0, 0, 1)},
    }
    moves = []

    def gather(which, side, place, span, consume, twin=False):
        whole = (side * span, span)
        head = (side * span, span // 2)
        tail = (side * span + span // 2, span // 2)
        known = {}

        def copy_of(dx, dy, dc, part, number, to):
            ref = place(tp_at(dx, dy, dc), *part)
            return remote(
                ref, ref, g_send.at[which, side, number], g_recv.at[which, side, number], targets[to]
            )

        def go(dx, dy, to, part=whole):
            if twin and to == "y" and part == whole:
                go(dx, dy, "y", head)
                go(dx, dy, "yy", tail)
                return
            number = len(known)
            known[dx, dy, to] = (number, part)
            copy_of(dx, dy, 0, part, number, to).start()
            moves.append(lambda: copy_of(dx, dy, 0, part, number, to))

        def come(dx, dy, to):
            if twin and to == "y":
                come(dx, dy, "yy")
            number, part = known[dx, dy, to]
            sx = dx + {"xp": -1, "xm": 1}.get(to, 0)
            sy = 1 - dy if to in ("y", "yy") else dy
            copy_of(sx, sy, 1 if to == "c" else 0, part, number, to).wait_recv()

        def pair(dx, dy):
            come(dx, dy, "c")
            consume(tp_at(dx, dy, 0) // 2)

        def relay(dx, dy):
            go(dx, dy, "xp" if dx < 0 else "xm", head if dx < 0 else tail)

        def y_first():
            for to in ("y", "xp", "xm", "c"):
                go(0, 0, to)
            yield
            come(0, 0, "y")
            for to in ("xp", "xm", "c"):
                go(0, 1, to)
            pair(0, 0)
            yield
            for dx, to in ((-1, "xp"), (1, "xm")):
                come(0, 0, to)
                relay(dx, 0)
                go(dx, 0, "c")
            yield
            pair(0, 1)
            for dx, to in ((-1, "xp"), (1, "xm")):
                come(0, 1, to)
                relay(dx, 1)
                go(dx, 1, "c")
            yield
            pair(-1, 0)
            pair(1, 0)
            yield
            come(-1, 0, "xp")
            come(1, 0, "xm")
            go(2, 0, "c")
            pair(-1, 1)
            pair(1, 1)
            yield
            come(-1, 1, "xp")
            come(1, 1, "xm")
            go(2, 1, "c")
            pair(2, 0)
            yield
            pair(2, 1)
            yield

        def x_first():
            for to in ("xp", "xm", "y", "c"):
                go(0, 0, to)
            yield
            pair(0, 0)
            for dx, to in ((-1, "xp"), (1, "xm")):
                come(0, 0, to)
                relay(dx, 0)
                go(dx, 0, "y")
                go(dx, 0, "c")
            yield
            come(0, 0, "y")
            go(0, 1, "c")
            pair(-1, 0)
            pair(1, 0)
            yield
            come(-1, 0, "xp")
            come(1, 0, "xm")
            go(2, 0, "y")
            go(2, 0, "c")
            come(-1, 0, "y")
            go(-1, 1, "c")
            come(1, 0, "y")
            go(1, 1, "c")
            yield
            pair(0, 1)
            pair(2, 0)
            yield
            come(2, 0, "y")
            go(2, 1, "c")
            pair(-1, 1)
            pair(1, 1)
            yield
            pair(2, 1)
            yield

        return x_first() if side else y_first()

    ones = jnp.ones((16, half), BF16)
    tri = lax.broadcasted_iota(jnp.int32, (half, half), 0) <= lax.broadcasted_iota(
        jnp.int32, (half, half), 1
    )

    def unit(queries, acc, top_ref, side, blocks, masked=False):
        these = queries[side]
        scores = [jnp.dot(keys, these, preferred_element_type=F32) for keys, _ in blocks]
        if masked:
            scores = [jnp.where(tri, block, LOW) for block in scores]
        old = top_ref[side, 0:1, :]
        best = functools.reduce(jnp.maximum, scores)
        new = jnp.maximum(old, jnp.max(best, axis=0, keepdims=True))
        top_ref[side, 0:1, :] = new
        total = acc[side] * jnp.exp2((old - new) * scale)
        for block, (_, values) in zip(scores, blocks):
            weights = jnp.exp2((block - new) * scale).astype(BF16)
            total = total + jnp.dot(
                jnp.concatenate([values, ones], axis=0), weights, preferred_element_type=F32
            )
        acc[side] = total

    def own_block(side):
        return (k_ref[side * half : (side + 1) * half, :], vt_own[side])

    def block_at(slot, side):
        return (kbuf[slot, pl.ds(pl.multiple_of(side * half, half), half), :], vbuf[slot, side])

    def third_unit(slots):
        unit(qt_par, acc_par, max_par, y_hi, [block_at(slot, y_hi) for slot in slots])

    def last_unit(slot):
        side = jnp.where(slot <= z, 0, 1)
        unit(qt_own, acc_own, max_own, side, [block_at(slot, side)])

    def early(slots):
        blocks = [block_at(slot, 0) for slot in slots]
        unit(qt_par, acc_par, max_par, 1, blocks)
        unit(qt_own, acc_own, max_own, 1, blocks)

    def late(slots):
        third_unit(slots)
        for slot in slots:
            last_unit(slot)

    for load in loads[:2] + loads[3:5]:
        load.wait()

    def res_place(chunk, first, count):
        return res_all.at[chunk, pl.ds(first, count), :]

    def wo_place(chunk, first, count):
        return wo_all.at[head_rows(chunk, first, count), :]

    def att_place(chunk, first, count):
        return att_all.at[chunk, pl.ds(first, count), :]

    def nothing(chip):
        pass

    res_a = gather(1, 0, res_place, half, nothing)
    res_b = gather(1, 1, res_place, half, nothing)
    wo_a = gather(2, 0, wo_place, LANES // 2, nothing, True)
    wo_b = gather(2, 1, wo_place, LANES // 2, nothing, True)
    for stages in (res_a, res_b):
        next(stages)
    for load in loads[5:]:
        load.wait()
    str_acc[...] = jnp.zeros_like(str_acc)
    diagonal = lax.broadcasted_iota(jnp.int32, (LANES, LANES), 0) == lax.broadcasted_iota(
        jnp.int32, (LANES, LANES), 1
    )

    def to_column(line, count=LANES):
        return jnp.sum(jnp.where(diagonal[:count], line, 0.0), axis=1, keepdims=True)

    def to_line(column):
        picked = jnp.where(diagonal[: column.shape[0]], column, 0.0)
        return jnp.sum(picked, axis=0, keepdims=True)

    def scale_win():
        def block(head, carry):
            at = head_rows(head)
            column = to_column(gain_ref[pl.ds(head, 1), :])
            win[at, :] = (win[at, :].astype(F32) * column).astype(BF16)
            return carry

        lax.fori_loop(0, n_tp, block, 0)

    def chip_rows(chip):
        return pl.ds(pl.multiple_of(chip * 2 * LANES, 2 * LANES), 2 * LANES)

    def prepare(*offsets):
        for dx, dy in offsets:
            chip = tp_at(dx, dy, 0) // 2
            deep = chip_rows(chip)
            joint[deep, :] = jnp.dot(
                wo_all[deep, :], win[...], preferred_element_type=F32
            ).astype(BF16)
            left_side = jnp.concatenate([res_all[2 * chip], res_all[2 * chip + 1]], axis=1)
            str_acc[...] += jnp.dot(left_side, win[deep, :], preferred_element_type=F32)

    def steps(*names):
        for stages in names:
            next(stages)

    plan = {
        1: ((res_a, res_a, res_b, wo_a), ()),
        2: ((res_a, res_a, res_b, res_b, wo_b), ()),
        3: ((wo_a, wo_a, res_a, res_a, res_b), ()),
        4: ((wo_b, wo_b, res_a, res_b, res_b), ()),
        5: ((wo_a, wo_a), ((0, 0),)),
        6: ((wo_a, wo_b), ((-1, 0), (1, 0))),
        7: ((wo_a, wo_b, wo_b), ((0, 1), (-1, 1))),
    }

    def share_residual_rim():
        for copy in res_tails:
            copy.wait_recv()
        spread_each(0, res_all, lambda copy: copy.start())

    def extra(number):
        names, offsets = plan[number]
        steps(*names)
        prepare(*offsets)
        if number == 2:
            share_residual_rim()
        if number == 3:
            scale_win()
        if number == 4:
            spread_each(0, res_all, lambda copy: copy.wait_recv())
    for side in range(2):
        qt_own[side] = turned(q_ref, side)
    unit(qt_own, acc_own, max_own, 0, [own_block(0)], True)
    unit(qt_own, acc_own, max_own, 1, [own_block(1)], True)
    unit(qt_own, acc_own, max_own, 1, [own_block(0)])

    def key_wait(slot):
        key_copy(k_hbm, slot, right).wait_recv()

    def value_wait(slot):
        value_copy(vt_own, slot, right).wait_recv()

    def pass_keys(step):
        back = ring - step
        key_wait(step)
        key_copy(kbuf.at[step], step + 1, right).start()
        key_wait(back)

        @pl.when(step < top - 1)
        def _():
            key_copy(kbuf.at[back], back - 1, left).start()

    def pass_values(step):
        back = ring - step
        value_wait(step)

        @pl.when(step < top - 1)
        def _():
            value_copy(vbuf.at[step], step + 1, right).start()

        value_wait(back)
        value_copy(vbuf.at[back], back - 1, left).start()

    def meet_partner():
        q_copy.wait_recv()
        for side in range(2):
            qt_par[side] = turned(qpar, side)
        unit(qt_par, acc_par, max_par, 1, [own_block(0)])
        pl.when(y_hi == 0)(lambda: unit(qt_par, acc_par, max_par, 0, [own_block(0)]))
        pl.when(y_hi == 1)(lambda: unit(qt_par, acc_par, max_par, 1, [own_block(1)]))

    def turn(step, carry):
        back = ring - step
        pass_keys(step)
        pl.when(step > 1)(lambda: late((step - 1, back + 1)))
        pl.when(step == 1)(meet_partner)
        pass_values(step)
        early((step, back))
        for number in range(1, top):
            pl.when(step == number)(functools.partial(extra, number))
        return carry

    lax.fori_loop(1, top, turn, 0)
    for number in range(top, 8):
        extra(number)
    late((top - 1, top + 1))
    prepare((1, 1), (2, 0))
    key_wait(top)
    value_wait(top)
    unit(qt_par, acc_par, max_par, 1, [block_at(top, 0)])
    third_unit((top,))

    def settle(acc, top_ref, side):
        total = acc[side, width : width + 1, :]
        seen = total > 0.0
        held = jnp.where(seen, total, 1.0)
        level = jnp.where(seen, top_ref[side, 0:1, :] * scale + jnp.log2(held), LOW)
        return acc[side, :width, :] * (1.0 / held), level

    st_copies = [
        remote(st_send.at[n], st_recv.at[n], x_send.at[1 + n], x_recv.at[1 + n], across)
        for n in range(2)
    ]
    o_copies = [
        remote(o_send.at[n], o_recv.at[n], x_send.at[3 + n], x_recv.at[3 + n], across)
        for n in range(2)
    ]

    def send_partial(side):
        mean, level = settle(acc_par, max_par, side)
        o_send[side] = mean.astype(BF16)
        o_copies[side].start()
        st_send[side] = jnp.broadcast_to(level, (8, half))
        st_copies[side].start()

    send_partial(0)
    send_partial(1)
    unit(qt_own, acc_own, max_own, 1, [block_at(top, 0)])
    last_unit(top)
    steps(wo_a, wo_b)
    prepare((2, 1))
    hid_acc[...] = res_all[tp].astype(F32)
    sides = (pl.ds(0, half), pl.ds(half, half))
    att_tails = tail_copies(att_all.at[tp], att_all, 7)

    def join(side):
        mean_own, level_own = settle(acc_own, max_own, side)
        st_copies[side].wait_recv()
        o_copies[side].wait_recv()
        level_other = st_recv[side, 0:1, :]
        most = jnp.maximum(level_own, level_other)
        w_own = jnp.exp2(level_own - most)
        w_other = jnp.exp2(level_other - most)
        share = 1.0 / (w_own + w_other)
        joined = mean_own * (w_own * share) + o_recv[side].astype(F32) * (w_other * share)
        att_all[tp, side * half : (side + 1) * half, :] = joined.T.astype(BF16)

    def project(at):

        def apply(chip):
            left_side = jnp.concatenate(
                [att_all[2 * chip, at, :], att_all[2 * chip + 1, at, :]], axis=1
            )
            deep = chip_rows(chip)
            weight = jnp.concatenate([wo_all[deep, own_cols], joint[deep, :]], axis=1)
            product = jnp.dot(left_side, weight, preferred_element_type=F32)
            hid_acc[at, :] += product[:, :LANES]
            str_acc[at, :] += product[:, LANES:]

        return apply

    def square_copy(side, step):
        peer = lax.rem(tp + step, n_tp)
        ref = sq_all.at[tp, side]
        return remote(ref, ref, w_send.at[side, step], w_recv.at[side, step], {"tp": peer})

    def square_each(side, act):
        def one(step, carry):
            act(square_copy(side, step))
            return carry

        lax.fori_loop(1, n_tp, one, 0)

    lines_used = half // LANES

    def finish_hidden(side):
        sq_all[tp, side] = jnp.zeros((8, LANES), F32)

        def squares(first, count, line):
            hidden = hid_acc[first : first + count, :].astype(BF16)
            if first < rows:
                hid_ref[first : first + count, :] = hidden
            wide = hidden.astype(F32)
            sq_all[tp, side, line : line + 1, :] = to_line(
                jnp.sum(wide * wide, axis=1, keepdims=True)
            )

        for g in range(lines_used):
            squares(side * half + g * LANES, LANES, g)
        if side:
            squares(rows, 2 * edge, lines_used)
        square_each(side, lambda copy: copy.start())

    def finish_streams(side):
        square_each(side, lambda copy: copy.wait_recv())
        lines = jnp.sum(sq_all[:, side], axis=0)

        def streams(first, count, line):
            mean_square = to_column(lines[line : line + 1, :], count) / (n_tp * LANES)
            scaled = str_acc[first : first + count, :] * lax.rsqrt(mean_square + 1e-6)
            return scaled.astype(BF16).astype(F32)

        for g in range(lines_used):
            at = slice(RIM + g * LANES, RIM + (g + 1) * LANES)
            ext[side, at, :] = streams(side * half + g * LANES, LANES, g)
        if side:
            outside = streams(rows, 2 * edge, lines_used)
            ext[0, :RIM, :] = jnp.where(dev == 0, 0.0, outside[RIM:edge])
            ext[1, :RIM, :] = jnp.where(
                dev == n_ctx - 1, ext[0, half : half + RIM, :], outside[edge + RIM :]
            )

    out_a = gather(0, 0, att_place, half, project(sides[0]))
    out_b = gather(0, 1, att_place, half, project(sides[1]))
    join(0)
    next(out_a)
    att_tails[0].start()
    join(1)
    next(out_b)
    att_tails[1].start()
    steps(out_a, out_a, out_b)
    for copy in att_tails:
        copy.wait_recv()
    spread_each(1, att_all, lambda copy: copy.start())
    steps(out_b, out_a, out_a, out_a, out_b, out_a, out_b, out_a)
    finish_hidden(0)
    spread_each(1, att_all, lambda copy: copy.wait_recv())
    project_rim = project(rim)
    for chip in range(n_tp // 2):
        project_rim(chip)
    steps(out_b, out_b)
    finish_hidden(1)

    lane_group = lax.broadcasted_iota(jnp.int32, (FILTER_TAPS, LANES), 1) // GROUP
    filt = jnp.zeros((FILTER_TAPS, LANES), F32)
    for g in range(LANES // GROUP):
        filt = jnp.where(lane_group == g, filt_ref[:, g : g + 1], filt)

    def convolve(side, low, high):
        count = high - low
        span = count + FILTER_TAPS - 1

        def featured(stream, first, number):
            cols = slice(stream * LANES, (stream + 1) * LANES)
            total = None
            for j in range(FEAT_TAPS):
                row = first + RIM - j
                term = taps_ref[j, stream : stream + 1, :] * ext[side, row : row + number, cols]
                total = term if total is None else total + term
            return total

        first = low - (FILTER_TAPS - 1)
        mix[0:span, :] = featured(0, first, span) * featured(2, first, span)
        response = None
        for j in range(FILTER_TAPS):
            row = FILTER_TAPS - 1 - j
            term = filt[j : j + 1, :] * mix[row : row + count, :]
            response = term if response is None else response + term
        out = featured(1, low, count) * response
        gated_ref[side * half + low : side * half + high, :] = out.astype(BF16)

    finish_streams(0)
    convolve(0, edge, half)
    finish_streams(1)
    convolve(0, 0, edge)
    convolve(1, 0, half)
    def drain(slot, carry):
        key_copy(k_hbm, slot, right).wait_send()
        value_copy(vt_own, slot, right).wait_send()
        return carry

    lax.fori_loop(1, ring, drain, 0)

    for side in range(2):
        square_each(side, lambda copy: copy.wait_send())
    spread_each(0, res_all, lambda copy: copy.wait_send())
    spread_each(1, att_all, lambda copy: copy.wait_send())
    for copy in [q_copy] + st_copies + o_copies + res_tails + att_tails:
        copy.wait_send()
    for move in moves:
        move().wait_send()


def local(queries, keys, values, residual, out_proj, norm_gain, in_proj, feat_taps, long_filter):
    rows, width = queries.shape
    half = rows // 2
    n_tp = lax.axis_size("tp")
    ring = lax.axis_size("ctx") // 2
    vmem = pl.BlockSpec(memory_space=pltpu.VMEM)
    hbm = pl.BlockSpec(memory_space=pltpu.HBM)
    dma = pltpu.SemaphoreType.DMA
    shape = jax.ShapeDtypeStruct((rows, width), BF16)
    return pl.pallas_call(
        functools.partial(kernel, ring),
        out_shape=(shape, shape),
        in_specs=[hbm] * 9,
        out_specs=(vmem, vmem),
        scratch_shapes=[
            pltpu.VMEM((rows, width), BF16),
            pltpu.VMEM((rows, width), BF16),
            pltpu.VMEM((rows, width), BF16),
            pltpu.VMEM((n_tp, LANES), F32),
            pltpu.VMEM((FEAT_TAPS, 3, LANES), F32),
            pltpu.VMEM((FILTER_TAPS, LANES // GROUP), F32),
            pltpu.VMEM((ring, rows, width), BF16),
            pltpu.VMEM((ring, 2, width, half), BF16),
            pltpu.VMEM((2, width, half), BF16),
            pltpu.VMEM((2, width, half), BF16),
            pltpu.VMEM((2, width, half), BF16),
            pltpu.VMEM((rows, width), BF16),
            pltpu.VMEM((2, width + 16, half), F32),
            pltpu.VMEM((2, width + 16, half), F32),
            pltpu.VMEM((2, 8, half), F32),
            pltpu.VMEM((2, 8, half), F32),
            pltpu.VMEM((2, width, half), BF16),
            pltpu.VMEM((2, width, half), BF16),
            pltpu.VMEM((2, 8, half), F32),
            pltpu.VMEM((2, 8, half), F32),
            pltpu.VMEM((n_tp * LANES, n_tp * LANES), BF16),
            pltpu.VMEM((n_tp * LANES, 3 * LANES), BF16),
            pltpu.VMEM((n_tp * LANES, 3 * LANES), BF16),
            pltpu.VMEM((n_tp, rows + 4 * RIM, width), BF16),
            pltpu.VMEM((n_tp, rows + 4 * RIM, width), BF16),
            pltpu.VMEM((rows + 4 * RIM, LANES), F32),
            pltpu.VMEM((rows + 4 * RIM, 3 * LANES), F32),
            pltpu.VMEM((n_tp, 2, 8, LANES), F32),
            pltpu.VMEM((2, RIM + half, 3 * LANES), F32),
            pltpu.VMEM((RIM + half, LANES), F32),
            dma((11,)),
            dma((ring,)),
            dma((ring,)),
            dma((ring,)),
            dma((ring,)),
            dma((9,)),
            dma((9,)),
            dma((2, n_tp)),
            dma((2, n_tp)),
            dma((2, n_tp)),
            dma((2, n_tp)),
            dma((3, 2, 20)),
            dma((3, 2, 20)),
        ],
        compiler_params=pltpu.CompilerParams(
            collective_id=0, has_side_effects=True, vmem_limit_bytes=40 * 1024 * 1024
        ),
        cost_estimate=pl.CostEstimate(
            flops=4 * 10**9, bytes_accessed=4 * 10**6, transcendentals=5 * 10**6
        ),
    )(
        *(
            pltpu.with_memory_space_constraint(operand, pltpu.HBM)
            for operand in (
                queries,
                keys,
                values,
                residual,
                out_proj,
                norm_gain.reshape(n_tp, LANES),
                jnp.transpose(in_proj, (1, 0, 2)),
                feat_taps,
                long_filter,
            )
        )
    )


def solution(mesh):
    return jax.shard_map(
        local,
        mesh=mesh,
        in_specs=(
            P("ctx", "tp"),
            P("ctx", "tp"),
            P("ctx", "tp"),
            P("ctx", "tp"),
            P("tp", None),
            P(),
            P(None, None, "tp"),
            P(None, None, "tp"),
            P(None, "tp"),
        ),
        out_specs=(P("ctx", "tp"), P("ctx", "tp")),
        check_vma=False,
    )
```

```python
import functools

import jax
import jax.numpy as jnp
from jax import lax
from jax.experimental import pallas as pl
from jax.experimental.pallas import tpu as pltpu
from jax.sharding import PartitionSpec as P

MESH = pl.DeviceIdType.MESH
LANES = 128
GROUP = 16
FEAT_TAPS = 3
FILTER_TAPS = 7
RIM = 8
LOW = -1e30
LOG2E = 1.4426950408889634
F32 = jnp.float32
BF16 = jnp.bfloat16


def kernel(
    ring,
    q_hbm,
    k_hbm,
    v_hbm,
    res_hbm,
    outp_hbm,
    gain_hbm,
    inp_hbm,
    taps_hbm,
    filt_hbm,
    hid_ref,
    gated_ref,
    q_ref,
    k_ref,
    v_ref,
    gain_ref,
    taps_ref,
    filt_ref,
    kbuf,
    vbuf,
    vt_own,
    qt_own,
    qt_par,
    qpar,
    acc_own,
    acc_par,
    max_own,
    max_par,
    o_send,
    o_recv,
    st_send,
    st_recv,
    wo_all,
    win,
    joint,
    att_all,
    res_all,
    hid_acc,
    str_acc,
    sq_all,
    ext,
    mix,
    in_sem,
    ks_sem,
    kr_sem,
    vs_sem,
    vr_sem,
    x_send,
    x_recv,
    w_send,
    w_recv,
    h_send,
    h_recv,
    g_send,
    g_recv,
):
    rows, width = q_ref.shape
    half = rows // 2
    edge = 2 * RIM
    rim = pl.ds(rows, 2 * edge)
    top = ring // 2
    n_ctx = 2 * ring
    n_tp = att_all.shape[0]
    n_x = n_tp // 4
    dev = lax.axis_index("ctx")
    y_hi = dev // ring
    z = lax.rem(dev, ring)
    tp = lax.axis_index("tp")
    x = tp // 4
    y_lo = lax.rem(tp, 4) // 2
    core = lax.rem(tp, 2)
    scale = LOG2E * width**-0.5

    def ctx_id(y_at, z_at):
        return {"ctx": y_at * ring + z_at}

    right = ctx_id(y_hi, lax.rem(z + 1, ring))
    left = ctx_id(y_hi, lax.rem(z + ring - 1, ring))
    across = ctx_id(1 - y_hi, z)
    beside = {"ctx": (1 - y_hi) * ring + z, "tp": tp + 2 - 4 * y_lo}
    after = {"ctx": lax.rem(dev + 1, n_ctx)}
    before = {"ctx": lax.rem(dev + n_ctx - 1, n_ctx)}

    def tp_at(dx, dy, dc):
        return (
            lax.rem(x + dx + n_x, n_x) * 4
            + (1 - y_lo if dy else y_lo) * 2
            + (1 - core if dc else core)
        )

    barrier = pltpu.get_barrier_semaphore()
    for other in (right, left, across, beside, after, before):
        pl.semaphore_signal(barrier, inc=1, device_id=other, device_id_type=MESH)

    def greet(step, carry):
        peer = lax.rem(tp + step, n_tp)
        pl.semaphore_signal(barrier, inc=1, device_id={"tp": peer}, device_id_type=MESH)
        return carry

    lax.fori_loop(1, n_tp, greet, 0)

    own_cols = pl.ds(pl.multiple_of(tp * LANES, LANES), LANES)

    def head_rows(head, first=0, count=LANES):
        return pl.ds(pl.multiple_of(head * LANES + first, count), count)

    loads = []
    for src, dst in [
        (q_hbm, q_ref),
        (k_hbm, k_ref),
        (v_hbm, v_ref),
        (res_hbm, res_all.at[tp, pl.ds(0, rows), :]),
        (outp_hbm, wo_all.at[head_rows(tp), :]),
        (gain_hbm, gain_ref),
        (taps_hbm, taps_ref),
        (filt_hbm, filt_ref),
    ] + [(inp_hbm.at[s], win.at[:, s * LANES : (s + 1) * LANES]) for s in range(3)]:
        load = pltpu.make_async_copy(src, dst, in_sem.at[len(loads)])
        load.start()
        loads.append(load)

    for acc, top_ref in ((acc_own, max_own), (acc_par, max_par)):
        acc[...] = jnp.zeros_like(acc)
        top_ref[...] = jnp.full(top_ref.shape, LOW, F32)
    pl.semaphore_wait(barrier, n_tp - 1 + 6)

    def remote(src, dst, send, recv, to):
        return pltpu.make_async_remote_copy(
            src_ref=src, dst_ref=dst, send_sem=send, recv_sem=recv, device_id=to, device_id_type=MESH
        )

    def key_copy(src, slot, to):
        return remote(src, kbuf.at[slot], ks_sem.at[slot], kr_sem.at[slot], to)

    def value_copy(src, slot, to):
        return remote(src, vbuf.at[slot], vs_sem.at[slot], vr_sem.at[slot], to)

    def turned(ref, side):
        return ref[side * half : (side + 1) * half, :].astype(F32).T.astype(BF16)

    q_copy = remote(q_hbm, qpar, x_send.at[0], x_recv.at[0], across)
    key_copy(k_hbm, 1, right).start()
    key_copy(k_hbm, ring - 1, left).start()
    q_copy.start()
    loads[2].wait()
    for side in range(2):
        vt_own[side] = turned(v_ref, side)
    value_copy(vt_own, 1, right).start()
    value_copy(vt_own, ring - 1, left).start()

    def tail_copies(src, dst, first_sem):
        return [
            remote(
                src.at[pl.ds((side + 1) * half - edge, edge), :],
                dst.at[tp, pl.ds(rows + side * edge, edge), :],
                x_send.at[first_sem + side],
                x_recv.at[first_sem + side],
                to,
            )
            for side, to in enumerate((after, before))
        ]

    res_tails = tail_copies(res_hbm, res_all, 5)
    for copy in res_tails:
        copy.start()

    def spread_each(which, buf, act):
        def one(step, carry):
            ref = buf.at[tp, rim, :]
            peer = lax.rem(tp + step, n_tp)
            act(remote(ref, ref, h_send.at[which, step], h_recv.at[which, step], {"tp": peer}))
            return carry

        lax.fori_loop(1, n_tp, one, 0)

    targets = {
        "y": {"tp": tp_at(0, 1, 0)},
        "yy": beside,
        "xp": {"tp": tp_at(1, 0, 0)},
        "xm": {"tp": tp_at(-1, 0, 0)},
        "c": {"tp": tp_at(0, 0, 1)},
    }
    moves = []

    def gather(which, side, place, span, consume, twin=False):
        whole = (side * span, span)
        head = (side * span, span // 2)
        tail = (side * span + span // 2, span // 2)
        known = {}

        def copy_of(dx, dy, dc, part, number, to):
            ref = place(tp_at(dx, dy, dc), *part)
            return remote(
                ref, ref, g_send.at[which, side, number], g_recv.at[which, side, number], targets[to]
            )

        def go(dx, dy, to, part=whole):
            if twin and to == "y" and part == whole:
                go(dx, dy, "y", head)
                go(dx, dy, "yy", tail)
                return
            number = len(known)
            known[dx, dy, to] = (number, part)
            copy_of(dx, dy, 0, part, number, to).start()
            moves.append(lambda: copy_of(dx, dy, 0, part, number, to))

        def come(dx, dy, to):
            if twin and to == "y":
                come(dx, dy, "yy")
            number, part = known[dx, dy, to]
            sx = dx + {"xp": -1, "xm": 1}.get(to, 0)
            sy = 1 - dy if to in ("y", "yy") else dy
            copy_of(sx, sy, 1 if to == "c" else 0, part, number, to).wait_recv()

        def pair(dx, dy):
            come(dx, dy, "c")
            consume(tp_at(dx, dy, 0) // 2)

        def relay(dx, dy):
            go(dx, dy, "xp" if dx < 0 else "xm", head if dx < 0 else tail)

        def y_first():
            for to in ("y", "xp", "xm", "c"):
                go(0, 0, to)
            yield
            come(0, 0, "y")
            for to in ("xp", "xm", "c"):
                go(0, 1, to)
            pair(0, 0)
            yield
            for dx, to in ((-1, "xp"), (1, "xm")):
                come(0, 0, to)
                relay(dx, 0)
                go(dx, 0, "c")
            yield
            pair(0, 1)
            for dx, to in ((-1, "xp"), (1, "xm")):
                come(0, 1, to)
                relay(dx, 1)
                go(dx, 1, "c")
            yield
            pair(-1, 0)
            pair(1, 0)
            yield
            come(-1, 0, "xp")
            come(1, 0, "xm")
            go(2, 0, "c")
            pair(-1, 1)
            pair(1, 1)
            yield
            come(-1, 1, "xp")
            come(1, 1, "xm")
            go(2, 1, "c")
            pair(2, 0)
            yield
            pair(2, 1)
            yield

        def x_first():
            for to in ("xp", "xm", "y", "c"):
                go(0, 0, to)
            yield
            pair(0, 0)
            for dx, to in ((-1, "xp"), (1, "xm")):
                come(0, 0, to)
                relay(dx, 0)
                go(dx, 0, "y")
                go(dx, 0, "c")
            yield
            come(0, 0, "y")
            go(0, 1, "c")
            pair(-1, 0)
            pair(1, 0)
            yield
            come(-1, 0, "xp")
            come(1, 0, "xm")
            go(2, 0, "y")
            go(2, 0, "c")
            come(-1, 0, "y")
            go(-1, 1, "c")
            come(1, 0, "y")
            go(1, 1, "c")
            yield
            pair(0, 1)
            pair(2, 0)
            yield
            come(2, 0, "y")
            go(2, 1, "c")
            pair(-1, 1)
            pair(1, 1)
            yield
            pair(2, 1)
            yield

        return x_first() if side else y_first()

    ones = jnp.ones((16, half), BF16)
    tri = lax.broadcasted_iota(jnp.int32, (half, half), 0) <= lax.broadcasted_iota(
        jnp.int32, (half, half), 1
    )

    def unit(queries, acc, top_ref, side, blocks, masked=False):
        these = queries[side]
        scores = [jnp.dot(keys, these, preferred_element_type=F32) for keys, _ in blocks]
        if masked:
            scores = [jnp.where(tri, block, LOW) for block in scores]
        old = top_ref[side, 0:1, :]
        best = functools.reduce(jnp.maximum, scores)
        new = jnp.maximum(old, jnp.max(best, axis=0, keepdims=True))
        top_ref[side, 0:1, :] = new
        total = acc[side] * jnp.exp2((old - new) * scale)
        for block, (_, values) in zip(scores, blocks):
            weights = jnp.exp2((block - new) * scale).astype(BF16)
            total = total + jnp.dot(
                jnp.concatenate([values, ones], axis=0), weights, preferred_element_type=F32
            )
        acc[side] = total

    def own_block(side):
        return (k_ref[side * half : (side + 1) * half, :], vt_own[side])

    def block_at(slot, side):
        return (kbuf[slot, pl.ds(pl.multiple_of(side * half, half), half), :], vbuf[slot, side])

    def third_unit(slots):
        unit(qt_par, acc_par, max_par, y_hi, [block_at(slot, y_hi) for slot in slots])

    def last_unit(slot):
        side = jnp.where(slot <= z, 0, 1)
        unit(qt_own, acc_own, max_own, side, [block_at(slot, side)])

    def early(slots):
        blocks = [block_at(slot, 0) for slot in slots]
        unit(qt_par, acc_par, max_par, 1, blocks)
        unit(qt_own, acc_own, max_own, 1, blocks)

    def late(slots):
        third_unit(slots)
        for slot in slots:
            last_unit(slot)

    for load in loads[:2] + loads[3:5]:
        load.wait()

    def res_place(chunk, first, count):
        return res_all.at[chunk, pl.ds(first, count), :]

    def wo_place(chunk, first, count):
        return wo_all.at[head_rows(chunk, first, count), :]

    def att_place(chunk, first, count):
        return att_all.at[chunk, pl.ds(first, count), :]

    def nothing(chip):
        pass

    res_a = gather(1, 0, res_place, half, nothing)
    res_b = gather(1, 1, res_place, half, nothing)
    wo_a = gather(2, 0, wo_place, LANES // 2, nothing, True)
    wo_b = gather(2, 1, wo_place, LANES // 2, nothing, True)
    for stages in (res_a, res_b):
        next(stages)
    for load in loads[5:]:
        load.wait()
    str_acc[...] = jnp.zeros_like(str_acc)
    diagonal = lax.broadcasted_iota(jnp.int32, (LANES, LANES), 0) == lax.broadcasted_iota(
        jnp.int32, (LANES, LANES), 1
    )

    def to_column(line, count=LANES):
        return jnp.sum(jnp.where(diagonal[:count], line, 0.0), axis=1, keepdims=True)

    def to_line(column):
        picked = jnp.where(diagonal[: column.shape[0]], column, 0.0)
        return jnp.sum(picked, axis=0, keepdims=True)

    def scale_win():
        def block(head, carry):
            at = head_rows(head)
            column = to_column(gain_ref[pl.ds(head, 1), :])
            win[at, :] = (win[at, :].astype(F32) * column).astype(BF16)
            return carry

        lax.fori_loop(0, n_tp, block, 0)

    def chip_rows(chip):
        return pl.ds(pl.multiple_of(chip * 2 * LANES, 2 * LANES), 2 * LANES)

    def prepare(*offsets):
        for dx, dy in offsets:
            chip = tp_at(dx, dy, 0) // 2
            deep = chip_rows(chip)
            joint[deep, :] = jnp.dot(
                wo_all[deep, :], win[...], preferred_element_type=F32
            ).astype(BF16)
            left_side = jnp.concatenate([res_all[2 * chip], res_all[2 * chip + 1]], axis=1)
            str_acc[...] += jnp.dot(left_side, win[deep, :], preferred_element_type=F32)

    def steps(*names):
        for stages in names:
            next(stages)

    plan = {
        1: ((res_a, res_a, res_b, wo_a), ()),
        2: ((res_a, res_a, res_b, res_b, wo_b), ()),
        3: ((wo_a, wo_a, res_a, res_a, res_b), ()),
        4: ((wo_b, wo_b, res_a, res_b, res_b), ()),
        5: ((wo_a, wo_a), ((0, 0),)),
        6: ((wo_a, wo_b), ((-1, 0), (1, 0))),
        7: ((wo_a, wo_b, wo_b), ((0, 1), (-1, 1))),
    }

    def share_residual_rim():
        for copy in res_tails:
            copy.wait_recv()
        spread_each(0, res_all, lambda copy: copy.start())

    def extra(number):
        names, offsets = plan[number]
        steps(*names)
        prepare(*offsets)
        if number == 2:
            share_residual_rim()
        if number == 3:
            scale_win()
        if number == 4:
            spread_each(0, res_all, lambda copy: copy.wait_recv())
    for side in range(2):
        qt_own[side] = turned(q_ref, side)
    unit(qt_own, acc_own, max_own, 0, [own_block(0)], True)
    unit(qt_own, acc_own, max_own, 1, [own_block(1)], True)
    unit(qt_own, acc_own, max_own, 1, [own_block(0)])

    def key_wait(slot):
        key_copy(k_hbm, slot, right).wait_recv()

    def value_wait(slot):
        value_copy(vt_own, slot, right).wait_recv()

    def pass_keys(step):
        back = ring - step
        key_wait(step)
        key_copy(kbuf.at[step], step + 1, right).start()
        key_wait(back)

        @pl.when(step < top - 1)
        def _():
            key_copy(kbuf.at[back], back - 1, left).start()

    def pass_values(step):
        back = ring - step
        value_wait(step)

        @pl.when(step < top - 1)
        def _():
            value_copy(vbuf.at[step], step + 1, right).start()

        value_wait(back)
        value_copy(vbuf.at[back], back - 1, left).start()

    def meet_partner():
        q_copy.wait_recv()
        for side in range(2):
            qt_par[side] = turned(qpar, side)
        unit(qt_par, acc_par, max_par, 1, [own_block(0)])
        pl.when(y_hi == 0)(lambda: unit(qt_par, acc_par, max_par, 0, [own_block(0)]))
        pl.when(y_hi == 1)(lambda: unit(qt_par, acc_par, max_par, 1, [own_block(1)]))

    def turn(step, carry):
        back = ring - step
        pass_keys(step)
        pl.when(step > 1)(lambda: late((step - 1, back + 1)))
        pl.when(step == 1)(meet_partner)
        pass_values(step)
        early((step, back))
        for number in range(1, top):
            pl.when(step == number)(functools.partial(extra, number))
        return carry

    lax.fori_loop(1, top, turn, 0)
    for number in range(top, 8):
        extra(number)
    late((top - 1, top + 1))
    prepare((1, 1), (2, 0))
    key_wait(top)
    value_wait(top)
    unit(qt_par, acc_par, max_par, 1, [block_at(top, 0)])
    third_unit((top,))

    def settle(acc, top_ref, side):
        total = acc[side, width : width + 1, :]
        seen = total > 0.0
        held = jnp.where(seen, total, 1.0)
        level = jnp.where(seen, top_ref[side, 0:1, :] * scale + jnp.log2(held), LOW)
        return acc[side, :width, :] * (1.0 / held), level

    st_copies = [
        remote(st_send.at[n], st_recv.at[n], x_send.at[1 + n], x_recv.at[1 + n], across)
        for n in range(2)
    ]
    o_copies = [
        remote(o_send.at[n], o_recv.at[n], x_send.at[3 + n], x_recv.at[3 + n], across)
        for n in range(2)
    ]

    def send_partial(side):
        mean, level = settle(acc_par, max_par, side)
        o_send[side] = mean.astype(BF16)
        o_copies[side].start()
        st_send[side] = jnp.broadcast_to(level, (8, half))
        st_copies[side].start()

    send_partial(0)
    send_partial(1)
    unit(qt_own, acc_own, max_own, 1, [block_at(top, 0)])
    last_unit(top)
    steps(wo_a, wo_b)
    prepare((2, 1))
    hid_acc[...] = res_all[tp].astype(F32)
    sides = (pl.ds(0, half), pl.ds(half, half))
    att_tails = tail_copies(att_all.at[tp], att_all, 7)

    def join(side):
        mean_own, level_own = settle(acc_own, max_own, side)
        st_copies[side].wait_recv()
        o_copies[side].wait_recv()
        level_other = st_recv[side, 0:1, :]
        most = jnp.maximum(level_own, level_other)
        w_own = jnp.exp2(level_own - most)
        w_other = jnp.exp2(level_other - most)
        share = 1.0 / (w_own + w_other)
        joined = mean_own * (w_own * share) + o_recv[side].astype(F32) * (w_other * share)
        att_all[tp, side * half : (side + 1) * half, :] = joined.T.astype(BF16)

    def project(at):

        def apply(chip):
            left_side = jnp.concatenate(
                [att_all[2 * chip, at, :], att_all[2 * chip + 1, at, :]], axis=1
            )
            deep = chip_rows(chip)
            weight = jnp.concatenate([wo_all[deep, own_cols], joint[deep, :]], axis=1)
            product = jnp.dot(left_side, weight, preferred_element_type=F32)
            hid_acc[at, :] += product[:, :LANES]
            str_acc[at, :] += product[:, LANES:]

        return apply

    def square_copy(step):
        peer = lax.rem(tp + step, n_tp)
        ref = sq_all.at[tp]
        return remote(ref, ref, w_send.at[step], w_recv.at[step], {"tp": peer})

    def square_each(act):
        def one(step, carry):
            act(square_copy(step))
            return carry

        lax.fori_loop(1, n_tp, one, 0)

    lines_used = half // LANES

    def finish_hidden(side):
        sq_all[tp, side] = jnp.zeros((8, LANES), F32)

        def squares(first, count, line):
            hidden = hid_acc[first : first + count, :].astype(BF16)
            if first < rows:
                hid_ref[first : first + count, :] = hidden
            wide = hidden.astype(F32)
            sq_all[tp, side, line : line + 1, :] = to_line(
                jnp.sum(wide * wide, axis=1, keepdims=True)
            )

        for g in range(lines_used):
            squares(side * half + g * LANES, LANES, g)
        if side:
            squares(rows, 2 * edge, lines_used)
            square_each(lambda copy: copy.start())

    def finish_streams(side):
        lines = jnp.sum(sq_all[:, side], axis=0)

        def streams(first, count, line):
            mean_square = to_column(lines[line : line + 1, :], count) / (n_tp * LANES)
            scaled = str_acc[first : first + count, :] * lax.rsqrt(mean_square + 1e-6)
            return scaled.astype(BF16).astype(F32)

        for g in range(lines_used):
            at = slice(RIM + g * LANES, RIM + (g + 1) * LANES)
            ext[side, at, :] = streams(side * half + g * LANES, LANES, g)
        if side:
            outside = streams(rows, 2 * edge, lines_used)
            ext[0, :RIM, :] = jnp.where(dev == 0, 0.0, outside[RIM:edge])
            ext[1, :RIM, :] = jnp.where(
                dev == n_ctx - 1, ext[0, half : half + RIM, :], outside[edge + RIM :]
            )

    out_a = gather(0, 0, att_place, half, project(sides[0]))
    out_b = gather(0, 1, att_place, half, project(sides[1]))
    join(0)
    next(out_a)
    att_tails[0].start()
    join(1)
    next(out_b)
    att_tails[1].start()
    steps(out_a, out_a, out_b)
    for copy in att_tails:
        copy.wait_recv()
    spread_each(1, att_all, lambda copy: copy.start())
    steps(out_b, out_a, out_a, out_a, out_b, out_a, out_b, out_a)
    finish_hidden(0)
    spread_each(1, att_all, lambda copy: copy.wait_recv())
    project_rim = project(rim)
    for chip in range(n_tp // 2):
        project_rim(chip)
    steps(out_b, out_b)
    finish_hidden(1)

    lane_group = lax.broadcasted_iota(jnp.int32, (FILTER_TAPS, LANES), 1) // GROUP
    filt = jnp.zeros((FILTER_TAPS, LANES), F32)
    for g in range(LANES // GROUP):
        filt = jnp.where(lane_group == g, filt_ref[:, g : g + 1], filt)

    def convolve(side, low, high):
        count = high - low
        span = count + FILTER_TAPS - 1

        def featured(stream, first, number):
            cols = slice(stream * LANES, (stream + 1) * LANES)
            total = None
            for j in range(FEAT_TAPS):
                row = first + RIM - j
                term = taps_ref[j, stream : stream + 1, :] * ext[side, row : row + number, cols]
                total = term if total is None else total + term
            return total

        first = low - (FILTER_TAPS - 1)
        mix[0:span, :] = featured(0, first, span) * featured(2, first, span)
        response = None
        for j in range(FILTER_TAPS):
            row = FILTER_TAPS - 1 - j
            term = filt[j : j + 1, :] * mix[row : row + count, :]
            response = term if response is None else response + term
        out = featured(1, low, count) * response
        gated_ref[side * half + low : side * half + high, :] = out.astype(BF16)

    square_each(lambda copy: copy.wait_recv())
    finish_streams(0)
    convolve(0, edge, half)
    finish_streams(1)
    convolve(0, 0, edge)
    convolve(1, 0, half)
    def drain(slot, carry):
        key_copy(k_hbm, slot, right).wait_send()
        value_copy(vt_own, slot, right).wait_send()
        return carry

    lax.fori_loop(1, ring, drain, 0)

    square_each(lambda copy: copy.wait_send())
    spread_each(0, res_all, lambda copy: copy.wait_send())
    spread_each(1, att_all, lambda copy: copy.wait_send())
    for copy in [q_copy] + st_copies + o_copies + res_tails + att_tails:
        copy.wait_send()
    for move in moves:
        move().wait_send()


def local(queries, keys, values, residual, out_proj, norm_gain, in_proj, feat_taps, long_filter):
    rows, width = queries.shape
    half = rows // 2
    n_tp = lax.axis_size("tp")
    ring = lax.axis_size("ctx") // 2
    vmem = pl.BlockSpec(memory_space=pltpu.VMEM)
    hbm = pl.BlockSpec(memory_space=pltpu.HBM)
    dma = pltpu.SemaphoreType.DMA
    shape = jax.ShapeDtypeStruct((rows, width), BF16)
    return pl.pallas_call(
        functools.partial(kernel, ring),
        out_shape=(shape, shape),
        in_specs=[hbm] * 9,
        out_specs=(vmem, vmem),
        scratch_shapes=[
            pltpu.VMEM((rows, width), BF16),
            pltpu.VMEM((rows, width), BF16),
            pltpu.VMEM((rows, width), BF16),
            pltpu.VMEM((n_tp, LANES), F32),
            pltpu.VMEM((FEAT_TAPS, 3, LANES), F32),
            pltpu.VMEM((FILTER_TAPS, LANES // GROUP), F32),
            pltpu.VMEM((ring, rows, width), BF16),
            pltpu.VMEM((ring, 2, width, half), BF16),
            pltpu.VMEM((2, width, half), BF16),
            pltpu.VMEM((2, width, half), BF16),
            pltpu.VMEM((2, width, half), BF16),
            pltpu.VMEM((rows, width), BF16),
            pltpu.VMEM((2, width + 16, half), F32),
            pltpu.VMEM((2, width + 16, half), F32),
            pltpu.VMEM((2, 8, half), F32),
            pltpu.VMEM((2, 8, half), F32),
            pltpu.VMEM((2, width, half), BF16),
            pltpu.VMEM((2, width, half), BF16),
            pltpu.VMEM((2, 8, half), F32),
            pltpu.VMEM((2, 8, half), F32),
            pltpu.VMEM((n_tp * LANES, n_tp * LANES), BF16),
            pltpu.VMEM((n_tp * LANES, 3 * LANES), BF16),
            pltpu.VMEM((n_tp * LANES, 3 * LANES), BF16),
            pltpu.VMEM((n_tp, rows + 4 * RIM, width), BF16),
            pltpu.VMEM((n_tp, rows + 4 * RIM, width), BF16),
            pltpu.VMEM((rows + 4 * RIM, LANES), F32),
            pltpu.VMEM((rows + 4 * RIM, 3 * LANES), F32),
            pltpu.VMEM((n_tp, 2, 8, LANES), F32),
            pltpu.VMEM((2, RIM + half, 3 * LANES), F32),
            pltpu.VMEM((RIM + half, LANES), F32),
            dma((11,)),
            dma((ring,)),
            dma((ring,)),
            dma((ring,)),
            dma((ring,)),
            dma((9,)),
            dma((9,)),
            dma((n_tp,)),
            dma((n_tp,)),
            dma((2, n_tp)),
            dma((2, n_tp)),
            dma((3, 2, 20)),
            dma((3, 2, 20)),
        ],
        compiler_params=pltpu.CompilerParams(
            collective_id=0, has_side_effects=True, vmem_limit_bytes=40 * 1024 * 1024
        ),
        cost_estimate=pl.CostEstimate(
            flops=4 * 10**9, bytes_accessed=4 * 10**6, transcendentals=5 * 10**6
        ),
    )(
        *(
            pltpu.with_memory_space_constraint(operand, pltpu.HBM)
            for operand in (
                queries,
                keys,
                values,
                residual,
                out_proj,
                norm_gain.reshape(n_tp, LANES),
                jnp.transpose(in_proj, (1, 0, 2)),
                feat_taps,
                long_filter,
            )
        )
    )


def solution(mesh):
    return jax.shard_map(
        local,
        mesh=mesh,
        in_specs=(
            P("ctx", "tp"),
            P("ctx", "tp"),
            P("ctx", "tp"),
            P("ctx", "tp"),
            P("tp", None),
            P(),
            P(None, None, "tp"),
            P(None, None, "tp"),
            P(None, "tp"),
        ),
        out_specs=(P("ctx", "tp"), P("ctx", "tp")),
        check_vma=False,
    )
```
